32 devices in a mesh: dp: 16 (over z, y, core), fsdp: 2 (over x).
Axes of the slice: x: 2, y: 2, z: 4, core: 2. Of those that a mesh axis runs over, the one named last changes fastest.
Arguments:
- tokens: bfloat16 [16384, 768], P(('dp', 'fsdp')), may hold values from -6 to 6
- lengths: int32 [32], P(('dp', 'fsdp')), may hold values from 128 to 512, as said below
- buckets: int32 [32, 3, 512, 512], P(('dp', 'fsdp')), may hold values from 0 to 31
- qkv_weight: bfloat16 [768, 2304], P('fsdp'), may hold values from -0.21875 to 0.21875
- q_bias: bfloat16 [768], P('fsdp'), may hold values from -3 to 3
- v_bias: bfloat16 [768], P('fsdp'), may hold values from -0.3125 to 0.3125
- out_weight: bfloat16 [768, 768], P('fsdp'), may hold values from -1.75 to 1.75
- out_bias: bfloat16 [768], P('fsdp'), may hold values from -1.75 to 1.75
- bias_table: bfloat16 [96, 12], P('fsdp'), may hold values from -3 to 3
- norm1_gain: bfloat16 [768], P('fsdp'), may hold values from 0.5 to 1.5
- norm1_bias: bfloat16 [768], P('fsdp'), may hold values from -1.75 to 1.75
- up_weight: bfloat16 [768, 3072], P('fsdp'), may hold values from -0.21875 to 0.21875
- up_bias: bfloat16 [3072], P('fsdp'), may hold values from -1.75 to 1.75
- down_weight: bfloat16 [3072, 768], P('fsdp'), may hold values from -0.109375 to 0.109375
- down_bias: bfloat16 [768], P('fsdp'), may hold values from -1.75 to 1.75
- norm2_gain: bfloat16 [768], P('fsdp'), may hold values from 0.5 to 1.5
- norm2_bias: bfloat16 [768], P('fsdp'), may hold values from -1.75 to 1.75
- cotangent: bfloat16 [16384, 768], P(('dp', 'fsdp')), may hold values from -6 to 6
Outputs:
- output: bfloat16 [16384, 768], P(('dp', 'fsdp'))
- tokens_grad: bfloat16 [16384, 768], P(('dp', 'fsdp'))
- qkv_weight_grad: float32 [768, 2304], P('fsdp')
- q_bias_grad: float32 [768], P('fsdp')
- v_bias_grad: float32 [768], P('fsdp')
- out_weight_grad: float32 [768, 768], P('fsdp')
- out_bias_grad: float32 [768], P('fsdp')
- bias_table_grad: float32 [96, 12], P('fsdp')
- norm1_gain_grad: float32 [768], P('fsdp')
- norm1_bias_grad: float32 [768], P('fsdp')
- up_weight_grad: float32 [768, 3072], P('fsdp')
- up_bias_grad: float32 [3072], P('fsdp')
- down_weight_grad: float32 [3072, 768], P('fsdp')
- down_bias_grad: float32 [768], P('fsdp')
- norm2_gain_grad: float32 [768], P('fsdp')
- norm2_bias_grad: float32 [768], P('fsdp')
The draws below stay inside these ranges and needn't reach their ends.
Inputs may be any that keep to these rules, and one draw needn't show every extreme that they name: `lengths`: each window has at least a quarter of its rows real, and some window has exactly 512.
All inputs are finite; a program needn't handle non-finite values.
Results may differ from the reference program's by a relative error of at most 0.02.
Values may be sent and summed in bfloat16 or wider, within the bound.
No kernel may reach another device: no remote copies, remote signals or barrier semaphores. Data moves between devices by JAX's collectives and lax.ppermute only.
A program may use at most 192 MiB of HBM per device.

```python
import jax
import jax.numpy as jnp
from jax import lax

D = 768
HEADS = 12
HEAD = 64
FF = 3072
BUCKETS = 32
L = 512
WINDOWS = 32
TOKENS = 16384


def draw_lengths(key, part):
    first_key, second_key = jax.random.split(jax.random.fold_in(key, 17))
    drawn = jax.random.randint(first_key, (WINDOWS,), L // 4, L + 1, dtype=jnp.int32)
    chosen = jax.random.randint(second_key, (), 0, WINDOWS, dtype=jnp.int32)
    return jnp.where(jnp.arange(WINDOWS, dtype=jnp.int32) == chosen, L, drawn).astype(jnp.int32)


def plant(array, stream_key, smallest, largest):
    dims = array.shape
    spot = [jax.random.randint(jax.random.fold_in(stream_key, axis), (), 0, dims[axis]) for axis in range(len(dims))]
    array = array.at[tuple(spot)].set(smallest)
    longest = dims.index(max(dims))
    spot[longest] = (spot[longest] + 1) % dims[longest]
    return array.at[tuple(spot)].set(largest)


def block_scale(rng, extent, shards, least, high):
    def one(dim, parts):
        draws = jax.random.uniform(jax.random.fold_in(jax.random.fold_in(rng, 6), dim), (parts,), jnp.float32, least / len(shards), high / len(shards))
        return jnp.repeat(jnp.exp(draws), extent[dim] // parts).reshape((-1,) + (1,) * (len(extent) - dim - 1))

    loudness = one(*shards[0])
    for cut in shards[1:]:
        loudness = loudness * one(*cut)
    return loudness


def centred(rng, dims, scale, reach, cuts=(), kind=jnp.bfloat16):
    level = block_scale(rng, dims, cuts, -0.22, 0.18) if cuts else 1.0
    result = jax.random.normal(rng, dims, jnp.float32) * scale * level
    return jnp.minimum(jnp.maximum(result, -reach), reach).astype(kind)


def setup_inputs(seed: int = 0) -> dict:
    key_list = jax.random.split(jax.random.key(seed), 19)
    tokens = centred(key_list[0], (TOKENS, D), 1.0, 6.0, ((0, 32),))
    lengths = draw_lengths(jax.random.fold_in(key_list[18], 71), 0)
    buckets = plant(jax.random.randint(key_list[2], (WINDOWS, 3, L, L), 0, BUCKETS), jax.random.fold_in(key_list[2], 1), 0, BUCKETS - 1).astype(jnp.int32)
    qkv_weight = centred(key_list[3], (D, 3 * D), D ** -0.5, 0.21875, ((0, 2),))
    q_bias = centred(key_list[4], (D,), 0.5, 3.0, ((0, 2),))
    v_bias = centred(key_list[5], (D,), 0.05, 0.3125, ((0, 2),))
    out_weight = centred(key_list[6], (D, D), (max(D // 64, 1)) ** -0.5, 1.75, ((0, 2),))
    out_bias = centred(key_list[7], (D,), 0.3, 1.75, ((0, 2),))
    bias_table = centred(key_list[8], (3 * BUCKETS, HEADS), 0.5, 3.0, ((0, 2),))
    norm1_gain = jnp.clip(1.0 + 0.1 * jax.random.normal(key_list[9], (D,), jnp.float32), 0.5, 1.5).astype(jnp.bfloat16)
    norm1_bias = centred(key_list[10], (D,), 0.3, 1.75, ((0, 2),))
    up_weight = centred(key_list[11], (D, FF), D ** -0.5, 0.21875, ((0, 2),))
    up_bias = centred(key_list[12], (FF,), 0.3, 1.75, ((0, 2),))
    down_weight = centred(key_list[13], (FF, D), FF ** -0.5, 0.109375, ((0, 2),))
    down_bias = centred(key_list[14], (D,), 0.3, 1.75, ((0, 2),))
    norm2_gain = jnp.clip(1.0 + 0.1 * jax.random.normal(key_list[15], (D,), jnp.float32), 0.5, 1.5).astype(jnp.bfloat16)
    norm2_bias = centred(key_list[16], (D,), 0.3, 1.75, ((0, 2),))
    cotangent = centred(key_list[17], (TOKENS, D), 1.0, 6.0, ((0, 32),))
    return dict(tokens=tokens, lengths=lengths, buckets=buckets, qkv_weight=qkv_weight, q_bias=q_bias, v_bias=v_bias, out_weight=out_weight, out_bias=out_bias, bias_table=bias_table, norm1_gain=norm1_gain, norm1_bias=norm1_bias, up_weight=up_weight, up_bias=up_bias, down_weight=down_weight, down_bias=down_bias, norm2_gain=norm2_gain, norm2_bias=norm2_bias, cotangent=cotangent)


@jax.custom_vjp
def low(v):
    return lax.optimization_barrier(v.astype(jnp.bfloat16)).astype(jnp.float32)

@jax.custom_vjp
def low_back(v):
    return v

def low_keep(v):
    return (low(v), None)

def low_pass(kept, grad):
    return (grad,)

def back_keep(v):
    return (v, None)

def back_low(kept, grad):
    return (low(grad),)
low.defvjp(low_keep, low_pass)
low_back.defvjp(back_keep, back_low)

def layer_norm(inputs, gain_vec, shift_vec):
    center = inputs - lax.optimization_barrier(jnp.mean(inputs, axis=-1, keepdims=True))
    inverse = lax.rsqrt(lax.optimization_barrier(jnp.mean(center * center, axis=-1, keepdims=True)) + 1e-05)
    return center * inverse * gain_vec + shift_vec

def window_forward(inputs, length, bucket, weight_set):
    qkv_w, q_b, v_b, out_w, out_b, table, gain_one, shift_one, up_w, up_b, down_w, down_b, gain_two, shift_two = weight_set
    highest = lax.Precision.HIGHEST
    packed = jnp.dot(inputs, qkv_w, precision=highest)
    queries = low_back(low((packed[:, :D] + q_b) * HEAD ** (-0.5)))
    keys_low = low_back(low(packed[:, D:2 * D]))
    values_low = low_back(low(packed[:, 2 * D:] + v_b))
    q_heads = queries.reshape(L, HEADS, HEAD)
    k_heads = keys_low.reshape(L, HEADS, HEAD)
    v_heads = values_low.reshape(L, HEADS, HEAD)
    scores = jnp.einsum('qhd,khd->hqk', q_heads, k_heads, precision=highest)
    offsets = jnp.arange(3, dtype=jnp.int32)[:, None, None] * BUCKETS
    picked = table[(bucket + offsets).astype(jnp.int32)]
    pair_bias = jnp.transpose(lax.optimization_barrier(jnp.sum(picked, axis=0)), (2, 0, 1))
    scores = low_back(scores + pair_bias)
    key_keep = jnp.arange(L, dtype=jnp.int32) < length
    scores = jnp.where(key_keep[None, None, :], scores, -1000000000.0)
    row_max = lax.optimization_barrier(jnp.max(scores, axis=-1, keepdims=True))
    shifted_exp = jnp.exp(scores - row_max)
    attn_probs = low(shifted_exp / lax.optimization_barrier(jnp.sum(shifted_exp, axis=-1, keepdims=True)))
    mixed_heads = jnp.einsum('hqk,khd->qhd', attn_probs, v_heads, precision=highest).reshape(L, D)
    mixed_heads = low_back(low(mixed_heads))
    attn_out = low_back(jnp.dot(mixed_heads, out_w, precision=highest) + out_b)
    first_norm = layer_norm(inputs + attn_out, gain_one, shift_one)
    hidden_in = low_back(jnp.dot(low(first_norm), up_w, precision=highest) + up_b)
    hidden = low(jax.nn.gelu(hidden_in, approximate=False))
    branch = low_back(jnp.dot(hidden, down_w, precision=highest) + down_b)
    second_norm = layer_norm(first_norm + branch, gain_two, shift_two)
    row_valid = (jnp.arange(L, dtype=jnp.int32) < length).astype(inputs.dtype)
    return second_norm * row_valid[:, None]

def reference(tokens, lengths, buckets, qkv_weight, q_bias, v_bias, out_weight, out_bias, bias_table, norm1_gain, norm1_bias, up_weight, up_bias, down_weight, down_bias, norm2_gain, norm2_bias, cotangent):
    weight_set = tuple((item.astype(jnp.float32) for item in (qkv_weight, q_bias, v_bias, out_weight, out_bias, bias_table, norm1_gain, norm1_bias, up_weight, up_bias, down_weight, down_bias, norm2_gain, norm2_bias)))
    windows_in = tokens.astype(jnp.float32).reshape(WINDOWS, L, D)
    cotangents = cotangent.astype(jnp.float32).reshape(WINDOWS, L, D)

    def window_step(grad_acc, window_item):
        inputs, length, bucket, window_ct = window_item

        def forward_fn(inputs_in, weights_in):
            return window_forward(inputs_in, length, bucket, weights_in)
        window_out, pullback = jax.vjp(forward_fn, inputs, weight_set)
        grad_tokens, grad_weights = pullback(window_ct)
        grad_acc = jax.tree.map(lambda first_a, second_a: first_a + second_a, grad_acc, grad_weights)
        return (grad_acc, (window_out.astype(jnp.bfloat16), grad_tokens.astype(jnp.bfloat16)))
    initial = jax.tree.map(jnp.zeros_like, weight_set)
    summed, (outputs, grads_in) = lax.scan(window_step, initial, (windows_in, lengths, buckets, cotangents))
    return (outputs.reshape(TOKENS, D), grads_in.reshape(TOKENS, D), summed[0], summed[1], summed[2], summed[3], summed[4], summed[5], summed[6], summed[7], summed[8], summed[9], summed[10], summed[11], summed[12], summed[13])
```

```python
import functools

import jax
import jax.numpy as jnp
from jax import lax
from jax.experimental import pallas as pl
from jax.experimental.pallas import tpu as pltpu
from jax.sharding import PartitionSpec as P

EPSILON = 1e-05
MASKED = -1000000000.0
BF = jnp.bfloat16
F32 = jnp.float32
NN = (((1,), (0,)), ((), ()))
NT = (((1,), (1,)), ((), ()))
TN = (((0,), (0,)), ((), ()))
VMEM_LIMIT = 56 * 2**20
WIDE = 128


def dg(left, right, dims):
    return lax.dot_general(left, right, dims, preferred_element_type=F32)


def onehot_rows(ids_ref, group, oh_ref, bucket_count, length):
    sub = lax.broadcasted_iota(jnp.int32, (16, length), 0)
    one = jnp.ones((16, length), BF)
    zero = jnp.zeros((16, length), BF)
    half = bucket_count // 2
    for kind in range(3):
        ids = ids_ref[kind, group]
        for pair in range(half):
            level = jnp.where(sub < 8, 2 * pair, 2 * pair + 1).astype(F32).astype(BF)
            oh_ref[pl.ds((kind * half + pair) * 16, 16), :] = jnp.where(ids == level, one, zero)


def bias_kernel(len_ref, ids_ref, table_ref, out_ref, oh_ref, *, bucket_count):
    block = pl.program_id(0)
    heads, rows, length = out_ref.shape
    valid = len_ref[0]

    def body(step, carry):
        parts = []
        for u in range(2):
            onehot_rows(ids_ref, step * 2 + u, oh_ref.at[u], bucket_count, length)
            part = dg(table_ref[...], oh_ref[u], NN)
            parts.append(part.reshape(heads, 8, length))
        bias = jnp.concatenate(parts, axis=1)
        key = lax.broadcasted_iota(jnp.int32, (1, 16, length), 1) + (block * rows + step * 16)
        out_ref[:, pl.ds(pl.multiple_of(step * 16, 16), 16), :] = jnp.where(
            key < valid, bias, MASKED
        ).astype(BF)
        return carry

    lax.fori_loop(0, rows // 16, body, 0, unroll=True)


def table_kernel(ids_ref, grad_ref, out_ref, oh_ref, *, bucket_count):
    heads, rows, length = grad_ref.shape

    @pl.when(pl.program_id(0) == 0)
    def _():
        out_ref[...] = jnp.zeros_like(out_ref)

    def body(step, carry):
        grads = grad_ref[:, pl.ds(pl.multiple_of(step * 16, 16), 16), :].astype(F32)
        total = None
        for u in range(2):
            onehot_rows(ids_ref, step * 2 + u, oh_ref.at[u], bucket_count, length)
            part = dg(
                oh_ref[u],
                grads[:, u * 8 : (u + 1) * 8, :].reshape(heads * 8, length).astype(BF),
                NT,
            )
            total = part if total is None else total + part
        out_ref[...] += total
        return carry

    lax.fori_loop(0, rows // 16, body, 0, unroll=True)


def attend_kernel(q_ref, k_ref, v_ref, bias_ref, p_ref, o_ref, *, size):
    width = q_ref.shape[1]
    lane = lax.broadcasted_iota(jnp.int32, (1, width), 1)
    q = q_ref[...]
    k = k_ref[...]
    vt = v_ref[...].T
    mixed = []
    for g in range(width // size):
        mine = (lane >= g * size) & (lane < (g + 1) * size)
        scores = dg(jnp.where(mine, k, jnp.zeros_like(k)), q, NT) + bias_ref[g].astype(F32)
        top = jnp.max(scores, axis=0, keepdims=True)
        shifted = jnp.exp(scores - top)
        norm = jnp.sum(shifted, axis=0, keepdims=True)
        probs = (shifted * (1.0 / norm)).astype(BF)
        p_ref[g] = probs
        mixed.append(dg(vt[g * size : (g + 1) * size], probs, NN))
    o_ref[...] = jnp.concatenate(mixed, axis=0).T.astype(BF)


def attend_back_kernel(
    q_ref, k_ref, v_ref, p_ref, o_ref, g_ref, out_ref, ds_ref, *, size, factor
):
    pair = pl.program_id(0)
    width = q_ref.shape[1]
    model = out_ref.shape[1] // 3
    count = width // size
    lane = lax.broadcasted_iota(jnp.int32, (1, width), 1)
    q = q_ref[...]
    v = v_ref[...]
    ob = g_ref[...]
    kt = k_ref[...].T
    product = o_ref[...].astype(F32) * ob.astype(F32)
    qs, ks, vs = [], [], []
    for g in range(count):
        mine = (lane >= g * size) & (lane < (g + 1) * size)
        spare = ((g + 1) % count) * size
        inner = jnp.sum(jnp.where(mine, product, 0.0), axis=1, keepdims=True)
        high = inner.astype(BF).astype(F32)
        extra = jnp.where(lane == spare, high, jnp.where(lane == spare + 1, inner - high, 0.0))
        minus = jnp.where((lane == spare) | (lane == spare + 1), -1.0, 0.0)
        left = jnp.where(mine, v, minus.astype(BF))
        right = jnp.where(mine, ob, extra.astype(BF))
        probs = p_ref[g]
        ds = (probs.astype(F32) * dg(left, right, NT)).astype(BF)
        ds_ref[g] = ds
        vs.append(dg(probs, ob, NN))
        ks.append(dg(ds, q, NN))
        qs.append(dg(kt[g * size : (g + 1) * size], ds, NN))

    def pick(items):
        chosen = items[0]
        for g in range(1, count):
            chosen = jnp.where(lane >= g * size, items[g], chosen)
        return chosen

    def place(start):
        return pl.ds(pl.multiple_of(start + pair * width, width), width)

    q_grad = jnp.concatenate(qs, axis=0).T.astype(BF).astype(F32) * factor
    out_ref[:, place(0)] = q_grad.astype(BF)
    out_ref[:, place(model)] = pick(ks).astype(BF)
    out_ref[:, place(2 * model)] = pick(vs).astype(BF)


def params():
    return pltpu.CompilerParams(vmem_limit_bytes=VMEM_LIMIT)


def twice(buckets):
    length = buckets.shape[-1]
    turned = jnp.swapaxes(buckets[0].astype(BF), 1, 2).reshape(3, length // 8, 1, 8, length)
    return jnp.broadcast_to(turned, (3, length // 8, 2, 8, length)).reshape(
        3, length // 8, 16, length
    )


def bias_scores(ids, valid, table, block=8):
    length = ids.shape[-1]
    bucket_count = table.shape[0] // 3
    heads = table.shape[1]
    spread = (table.T[:, None, :, None] * jnp.eye(8, dtype=BF)[None, :, None, :]).reshape(
        heads * 8, 3 * bucket_count * 8
    )
    return pl.pallas_call(
        functools.partial(bias_kernel, bucket_count=bucket_count),
        grid=(length // 8 // block,),
        in_specs=[
            pl.BlockSpec(memory_space=pltpu.SMEM),
            pl.BlockSpec((3, block, 16, length), lambda i: (0, i, 0, 0)),
            pl.BlockSpec(spread.shape, lambda i: (0, 0)),
        ],
        out_specs=pl.BlockSpec((heads, block * 8, length), lambda i: (0, i, 0)),
        out_shape=jax.ShapeDtypeStruct((heads, length, length), BF),
        scratch_shapes=[pltpu.VMEM((2, 3 * bucket_count * 8, length), BF)],
        compiler_params=params(),
        name="bias_scores",
    )(valid, ids, spread)


def table_grad(ids, grads, bucket_count, block=8):
    heads, length, _ = grads.shape
    wide = pl.pallas_call(
        functools.partial(table_kernel, bucket_count=bucket_count),
        grid=(length // 8 // block,),
        in_specs=[
            pl.BlockSpec((3, block, 16, length), lambda i: (0, i, 0, 0)),
            pl.BlockSpec((heads, block * 8, length), lambda i: (0, i, 0)),
        ],
        out_specs=pl.BlockSpec((3 * bucket_count * 8, heads * 8), lambda i: (0, 0)),
        out_shape=jax.ShapeDtypeStruct((3 * bucket_count * 8, heads * 8), F32),
        scratch_shapes=[pltpu.VMEM((2, 3 * bucket_count * 8, length), BF)],
        compiler_params=params(),
        name="table_grad",
    )(ids, grads)
    row = jnp.arange(3 * bucket_count * 8, dtype=jnp.int32) % 8
    col = jnp.arange(heads * 8, dtype=jnp.int32) % 8
    kept = jnp.where(row[:, None] == col[None, :], wide, 0.0)
    return kept.reshape(3 * bucket_count, 8, heads, 8).sum((1, 3))


def attend(qkv, bias, size):
    length = qkv.shape[0]
    model = qkv.shape[1] // 3
    blocks = model // WIDE
    group = WIDE // size
    return pl.pallas_call(
        functools.partial(attend_kernel, size=size),
        grid=(blocks,),
        in_specs=[
            pl.BlockSpec((length, WIDE), lambda i: (0, i)),
            pl.BlockSpec((length, WIDE), lambda i: (0, blocks + i)),
            pl.BlockSpec((length, WIDE), lambda i: (0, 2 * blocks + i)),
            pl.BlockSpec((group, length, length), lambda i: (i, 0, 0)),
        ],
        out_specs=[
            pl.BlockSpec((group, length, length), lambda i: (i, 0, 0)),
            pl.BlockSpec((length, WIDE), lambda i: (0, i)),
        ],
        out_shape=[
            jax.ShapeDtypeStruct((model // size, length, length), BF),
            jax.ShapeDtypeStruct((length, model), BF),
        ],
        compiler_params=params(),
        name="attend",
    )(qkv, qkv, qkv, bias)


def attend_back(qkv, probs, mixed, grad_mixed, size):
    length = qkv.shape[0]
    model = qkv.shape[1] // 3
    blocks = model // WIDE
    group = WIDE // size
    return pl.pallas_call(
        functools.partial(attend_back_kernel, size=size, factor=size**-0.5),
        grid=(blocks,),
        in_specs=[
            pl.BlockSpec((length, WIDE), lambda i: (0, i)),
            pl.BlockSpec((length, WIDE), lambda i: (0, blocks + i)),
            pl.BlockSpec((length, WIDE), lambda i: (0, 2 * blocks + i)),
            pl.BlockSpec((group, length, length), lambda i: (i, 0, 0)),
            pl.BlockSpec((length, WIDE), lambda i: (0, i)),
            pl.BlockSpec((length, WIDE), lambda i: (0, i)),
        ],
        out_specs=[
            pl.BlockSpec((length, 3 * model), lambda i: (0, 0)),
            pl.BlockSpec((group, length, length), lambda i: (i, 0, 0)),
        ],
        out_shape=[
            jax.ShapeDtypeStruct((length, 3 * model), BF),
            jax.ShapeDtypeStruct((model // size, length, length), BF),
        ],
        compiler_params=params(),
        name="attend_back",
    )(qkv, qkv, qkv, probs, mixed, grad_mixed)


class Axis:
    def __init__(self, name, total, stride, size):
        self.name = name
        self.total = total
        self.stride = stride
        self.size = size
        self.at = (lax.axis_index(name) // stride) % size

    def send(self, value, step):
        pairs = []
        for index in range(self.total):
            place = (index // self.stride) % self.size
            pairs.append((index, index + ((place + step) % self.size - place) * self.stride))
        return lax.ppermute(value, self.name, pairs)

    def peer(self, step):
        return (self.at + step) % self.size


def take(stack, index):
    return lax.dynamic_index_in_dim(stack, index, axis=0, keepdims=False)


def gather(axis, block):
    stack = jnp.zeros((axis.size,) + block.shape, block.dtype)
    stack = lax.dynamic_update_index_in_dim(stack, block, axis.at, 0)
    for step in range(1, axis.size):
        stack = lax.dynamic_update_index_in_dim(
            stack, axis.send(block, step), axis.peer(-step), 0
        )
    return stack


class Links:
    def __init__(self, dp, fsdp):
        core = 2 if dp % 2 == 0 else 1
        rest = dp // core
        near = 2 if rest % 2 == 0 else 1
        self.core = Axis("dp", dp, 1, core)
        self.near = Axis("dp", dp, core, near)
        self.far = Axis("dp", dp, core * near, rest // near)
        self.shard = Axis("fsdp", fsdp, 1, fsdp)

    def weight(self, block, after=None):
        core, near, shard = self.core, self.near, self.shard
        rows, columns = block.shape
        parts = block.reshape(core.size * near.size, rows // (core.size * near.size), columns)
        mine = take(parts, core.at * near.size + near.at)
        if after is not None:
            mine, _ = lax.optimization_barrier((mine, after))
        others = jnp.stack([shard.send(mine, step) for step in range(1, shard.size)])
        token = others
        shared = gather(core, gather(near, others))
        whole = jnp.zeros((shard.size, rows, columns), block.dtype)
        whole = lax.dynamic_update_index_in_dim(whole, block, shard.at, 0)
        for step in range(1, shard.size):
            piece = shared[:, :, step - 1].reshape(rows, columns)
            whole = lax.dynamic_update_index_in_dim(whole, piece, shard.peer(-step), 0)
        return whole.reshape(shard.size * rows, columns), token

    def vector(self, block):
        return gather(self.shard, block)

    def reduce(self, left, right):
        core, near, far, shard = self.core, self.near, self.far, self.shard
        rows = left.shape[1] // shard.size
        columns = right.shape[1] // core.size
        piece = rows // (near.size * far.size)
        shape = (shard.size, near.size, far.size, piece, columns)

        def product(index):
            return dg(left, lax.dynamic_slice_in_dim(right, index * columns, columns, 1), TN)

        total = product(core.at).reshape(shape)
        for step in range(1, core.size):
            total = total + core.send(product(core.peer(step)).astype(BF), step).reshape(shape).astype(F32)
        for axis in (shard, near, far):
            kept = take(total, axis.at)
            for step in range(1, axis.size):
                kept = kept + axis.send(take(total, axis.peer(step)).astype(BF), step).astype(F32)
            total = kept
        done = total.astype(BF)
        for axis in (far, near, core):
            done = gather(axis, done)
        done = done.reshape(core.size, rows, columns).astype(F32)
        return jnp.swapaxes(done, 0, 1).reshape(rows, core.size * columns)

    def reduce_vector(self, stack):
        shard = self.shard
        total = take(stack, shard.at)
        for step in range(1, shard.size):
            total = total + shard.send(take(stack, shard.peer(step)), step)
        for axis in (self.core, self.near, self.far):
            part = total
            for step in range(1, axis.size):
                total = total + axis.send(part, step)
        return total


def pack(items, shards):
    return jnp.concatenate([item.reshape(shards, -1) for item in items], axis=1)


def gelu_pair(inputs):
    hidden, back = jax.vjp(lambda u: jax.nn.gelu(u, approximate=False), inputs)
    return hidden, back(jnp.ones_like(inputs))[0]


def norm_forward(inputs, gain_vec, shift_vec):
    center = inputs - jnp.mean(inputs, axis=-1, keepdims=True)
    inverse = lax.rsqrt(jnp.mean(center * center, axis=-1, keepdims=True) + EPSILON)
    scaled = center * inverse
    return (scaled * gain_vec + shift_vec, scaled, inverse)


def norm_backward(grad_in, scaled, inverse, gain_vec):
    gain_grad = jnp.sum(grad_in * scaled, axis=0)
    shift_grad = jnp.sum(grad_in, axis=0)
    inner_term = grad_in * gain_vec
    centered = inner_term - jnp.mean(inner_term, axis=-1, keepdims=True)
    grad_out = inverse * (centered - scaled * jnp.mean(inner_term * scaled, axis=-1, keepdims=True))
    return (gain_grad, shift_grad, grad_out)


def column_sum(grad_low):
    return jnp.sum(grad_low.astype(F32), axis=0)


def per_device(
    dp,
    fsdp,
    tokens,
    lengths,
    buckets,
    qkv_weight,
    q_bias,
    v_bias,
    out_weight,
    out_bias,
    bias_table,
    norm1_gain,
    norm1_bias,
    up_weight,
    up_bias,
    down_weight,
    down_bias,
    norm2_gain,
    norm2_bias,
    cotangent,
):
    links = Links(dp, fsdp)
    length = buckets.shape[2]
    model = tokens.shape[1]
    heads = bias_table.shape[1]
    size = model // heads
    factor = size ** (-0.5)
    vectors = (
        bias_table,
        q_bias,
        v_bias,
        out_bias,
        norm1_gain,
        norm1_bias,
        up_bias,
        down_bias,
        norm2_gain,
        norm2_bias,
    )
    packed = links.vector(jnp.concatenate([item.reshape(-1) for item in vectors]))
    full = []
    start = 0
    for item in vectors:
        full.append(packed[:, start : start + item.size].reshape(-1))
        start += item.size
    table = full[0].reshape(-1, heads)
    b_query, b_value, b_out, gain_one, shift_one, b_up, b_down, gain_two, shift_two = [
        item.astype(F32) for item in full[1:]
    ]
    w_qkv, token = links.weight(qkv_weight)
    w_out, token = links.weight(out_weight, token)
    w_up, token = links.weight(up_weight, token)
    w_down, token = links.weight(down_weight, token)

    ids = twice(buckets)
    bias = bias_scores(ids, lengths, table)
    row_valid = (
        (jnp.arange(length, dtype=jnp.int32) < lengths[0]).astype(F32).reshape(length, 1)
    )
    shift_row = jnp.concatenate([b_query, jnp.zeros_like(b_query), b_value])
    scale_row = jnp.concatenate([jnp.full((model,), factor, F32), jnp.ones((2 * model,), F32)])
    qkv = ((dg(tokens, w_qkv, NN) + shift_row) * scale_row).astype(BF)
    probs, mixed = attend(qkv, bias, size)
    first_norm, scaled_one, inverse_one = norm_forward(
        tokens.astype(F32) + (dg(mixed, w_out, NN) + b_out), gain_one, shift_one
    )
    first_low = first_norm.astype(BF)
    hidden, slope = gelu_pair(dg(first_low, w_up, NN) + b_up)
    hidden_low = hidden.astype(BF)
    slope = slope.astype(BF)
    second_norm, scaled_two, inverse_two = norm_forward(
        first_norm + (dg(hidden_low, w_down, NN) + b_down), gain_two, shift_two
    )
    output = (second_norm * row_valid).astype(BF)

    grad_second = cotangent.astype(F32) * row_valid
    g_gain_two, g_shift_two, grad_sum_two = norm_backward(
        grad_second, scaled_two, inverse_two, gain_two
    )
    grad_branch = grad_sum_two.astype(BF)
    g_down = links.reduce(hidden_low, grad_branch)
    grad_hidden_in = (dg(grad_branch, w_down, NT) * slope.astype(F32)).astype(BF)
    g_up = links.reduce(first_low, grad_hidden_in)
    grad_first = grad_sum_two + dg(grad_hidden_in, w_up, NT)
    g_gain_one, g_shift_one, grad_sum_one = norm_backward(
        grad_first, scaled_one, inverse_one, gain_one
    )
    grad_attn = grad_sum_one.astype(BF)
    g_out = links.reduce(mixed, grad_attn)
    early = links.reduce_vector(
        pack(
            (
                column_sum(grad_attn),
                g_gain_one,
                g_shift_one,
                column_sum(grad_hidden_in),
                column_sum(grad_branch),
                g_gain_two,
                g_shift_two,
            ),
            fsdp,
        )
    )
    grad_mixed = dg(grad_attn, w_out, NT).astype(BF)
    grad_packed, grad_scores = attend_back(qkv, probs, mixed, grad_mixed, size)
    g_qkv = links.reduce(tokens, grad_packed)
    tokens_grad = (grad_sum_one + dg(grad_packed, w_qkv, NT)).astype(BF)
    g_table = table_grad(ids, grad_scores, table.shape[0] // 3)
    sums = column_sum(grad_packed)
    late = links.reduce_vector(pack((g_table, sums[:model], sums[2 * model :]), fsdp))

    def split(vector, sizes):
        pieces = []
        begin = 0
        for count in sizes:
            pieces.append(vector[begin : begin + count])
            begin += count
        return pieces

    narrow = out_bias.size
    g_out_bias, g_gain_one, g_shift_one, g_up_bias, g_down_bias, g_gain_two, g_shift_two = split(
        early, (narrow, narrow, narrow, up_bias.size, narrow, narrow, narrow)
    )
    g_table, g_query_bias, g_value_bias = split(late, (bias_table.size, narrow, narrow))
    return (
        output,
        tokens_grad,
        g_qkv,
        g_query_bias,
        g_value_bias,
        g_out,
        g_out_bias,
        g_table.reshape(bias_table.shape),
        g_gain_one,
        g_shift_one,
        g_up,
        g_up_bias,
        g_down,
        g_down_bias,
        g_gain_two,
        g_shift_two,
    )


def solution(mesh):
    rows = P(("dp", "fsdp"), None)
    mat = P("fsdp", None)
    vec = P("fsdp")
    return jax.shard_map(
        functools.partial(per_device, mesh.shape["dp"], mesh.shape["fsdp"]),
        mesh=mesh,
        in_specs=(
            rows,
            P(("dp", "fsdp")),
            P(("dp", "fsdp"), None, None, None),
            mat,
            vec,
            vec,
            mat,
            vec,
            mat,
            vec,
            vec,
            mat,
            vec,
            mat,
            vec,
            vec,
            vec,
            rows,
        ),
        out_specs=(
            rows,
            rows,
            mat,
            vec,
            vec,
            mat,
            vec,
            mat,
            vec,
            vec,
            mat,
            vec,
            mat,
            vec,
            vec,
            vec,
        ),
        check_vma=False,
    )
```

```python
import functools

import jax
import jax.numpy as jnp
from jax import lax
from jax.experimental import pallas as pl
from jax.experimental.pallas import tpu as pltpu
from jax.sharding import PartitionSpec as P

EPSILON = 1e-05
MASKED = -1000000000.0
BF = jnp.bfloat16
F32 = jnp.float32
NN = (((1,), (0,)), ((), ()))
NT = (((1,), (1,)), ((), ()))
TN = (((0,), (0,)), ((), ()))
VMEM_LIMIT = 56 * 2**20
WIDE = 128
ANY = pl.BlockSpec(memory_space=pl.ANY)
SMEM = pl.BlockSpec(memory_space=pltpu.SMEM)
VMEM = pl.BlockSpec(memory_space=pltpu.VMEM)


def dg(left, right, dims):
    return lax.dot_general(left, right, dims, preferred_element_type=F32)


def params():
    return pltpu.CompilerParams(vmem_limit_bytes=VMEM_LIMIT)


def shaped(shape, dtype):
    return jax.ShapeDtypeStruct(shape, dtype)


def onehot_rows(ids, oh_ref, bucket_count):
    length = ids[0].shape[1]
    sub = lax.broadcasted_iota(jnp.int32, (16, length), 0)
    one = jnp.ones((16, length), BF)
    zero = jnp.zeros((16, length), BF)
    half = bucket_count // 2
    for kind in range(3):
        both = jnp.concatenate([ids[kind], ids[kind]], axis=0).astype(BF)
        for pair in range(half):
            level = jnp.where(sub < 8, 2 * pair, 2 * pair + 1).astype(F32).astype(BF)
            oh_ref[pl.ds((kind * half + pair) * 16, 16), :] = jnp.where(both == level, one, zero)


def iota2(shape, dim):
    return lax.broadcasted_iota(jnp.int32, shape, dim)


def bias_kernel(len_ref, ids_ref, table_ref, out_ref, turned_ref, spread_ref, held_ref, oh_ref):
    block = pl.program_id(0)
    heads, rows, length = out_ref.shape
    entries = table_ref.shape[0]
    valid = len_ref[0]

    @pl.when(block == 0)
    def _():
        pick_head = (iota2((heads * 8, heads), 0) >> 3) == iota2((heads * 8, heads), 1)
        rows_of = dg(pick_head.astype(F32).astype(BF), table_ref[...], NT).astype(BF)
        shape = (entries, entries * 8)
        pick_entry = iota2(shape, 0) == (iota2(shape, 1) >> 3)
        wide = dg(rows_of, pick_entry.astype(F32).astype(BF), NN)
        shape = (heads * 8, entries * 8)
        same = (iota2(shape, 0) & 7) == (iota2(shape, 1) & 7)
        spread_ref[...] = jnp.where(same, wide, 0.0).astype(BF)

    for kind in range(3):
        turned = ids_ref[0, kind].astype(F32).T
        held_ref[kind] = turned
        turned_ref[kind] = turned.astype(BF)

    def body(step, carry):
        parts = []
        for u in range(2):
            group = pl.ds(pl.multiple_of(step * 16 + u * 8, 8), 8)
            onehot_rows([held_ref[kind, group, :] for kind in range(3)], oh_ref.at[u], entries // 3)
            parts.append(dg(spread_ref[...], oh_ref[u], NN).reshape(heads, 8, length))
        bias = jnp.concatenate(parts, axis=1)
        key = iota2((1, 16, length), 1) + (block * rows + step * 16)
        out_ref[:, pl.ds(pl.multiple_of(step * 16, 16), 16), :] = jnp.where(
            key < valid, bias, MASKED
        ).astype(BF)
        return carry

    lax.fori_loop(0, rows // 16, body, 0, unroll=4)


def bias_scores(buckets, valid, table, rows=128):
    length = buckets.shape[-1]
    entries, heads = table.shape
    return pl.pallas_call(
        bias_kernel,
        grid=(length // rows,),
        in_specs=[
            SMEM,
            pl.BlockSpec((1, 3, length, rows), lambda i: (0, 0, 0, i)),
            pl.BlockSpec((entries, heads), lambda i: (0, 0)),
        ],
        out_specs=[
            pl.BlockSpec((heads, rows, length), lambda i: (0, i, 0)),
            pl.BlockSpec((3, rows, length), lambda i: (0, i, 0)),
        ],
        out_shape=[shaped((heads, length, length), BF), shaped((3, length, length), BF)],
        scratch_shapes=[
            pltpu.VMEM((heads * 8, entries * 8), BF),
            pltpu.VMEM((3, rows, length), F32),
            pltpu.VMEM((2, entries * 8, length), BF),
        ],
        compiler_params=params(),
        name="bias_scores",
    )(valid, buckets, table)


def table_kernel(ids_ref, grad_ref, out_ref, acc_ref, oh_ref):
    heads, rows, length = grad_ref.shape
    entries = out_ref.shape[0]

    @pl.when(pl.program_id(0) == 0)
    def _():
        acc_ref[...] = jnp.zeros_like(acc_ref)

    def body(step, carry):
        tile = pl.ds(pl.multiple_of(step * 16, 16), 16)
        grads = grad_ref[:, tile, :].astype(F32)
        ids = [ids_ref[kind, tile, :].astype(F32) for kind in range(3)]
        total = None
        for u in range(2):
            part = slice(u * 8, (u + 1) * 8)
            onehot_rows([item[part] for item in ids], oh_ref.at[u], entries // 3)
            part = dg(oh_ref[u], grads[:, part, :].reshape(heads * 8, length).astype(BF), NT)
            total = part if total is None else total + part
        acc_ref[...] += total
        return carry

    lax.fori_loop(0, rows // 16, body, 0, unroll=4)

    @pl.when(pl.program_id(0) == pl.num_programs(0) - 1)
    def _():
        shape = acc_ref.shape
        same = (iota2(shape, 0) & 7) == (iota2(shape, 1) & 7)
        kept = jnp.where(same, acc_ref[...], 0.0)
        rows_in = kept.reshape(entries, 8, heads * 8).sum(axis=1)
        fold = ((iota2((heads * 8, heads), 0) >> 3) == iota2((heads * 8, heads), 1)).astype(F32)
        out_ref[...] = lax.dot_general(
            rows_in, fold, NN, precision=lax.Precision.HIGHEST, preferred_element_type=F32
        )


def table_grad(ids, grads, entries, rows=64):
    heads, length, _ = grads.shape
    return pl.pallas_call(
        table_kernel,
        grid=(length // rows,),
        in_specs=[
            pl.BlockSpec((3, rows, length), lambda i: (0, i, 0)),
            pl.BlockSpec((heads, rows, length), lambda i: (0, i, 0)),
        ],
        out_specs=pl.BlockSpec((entries, heads), lambda i: (0, 0)),
        out_shape=shaped((entries, heads), F32),
        scratch_shapes=[
            pltpu.VMEM((entries * 8, heads * 8), F32),
            pltpu.VMEM((2, entries * 8, length), BF),
        ],
        compiler_params=params(),
        name="table_grad",
    )(ids, grads)


class Weight:
    def __init__(self, pieces, unit, shape):
        self.pieces = pieces
        self.unit = unit
        self.shape = shape


def start_fetch(refs, units_ref, unit, whole_ref, sem_ref, first):
    copies = []
    for index, ref in enumerate(refs):
        begin = pl.multiple_of(units_ref[index] * unit, unit)
        copy = pltpu.make_async_copy(
            ref, whole_ref.at[pl.ds(begin, ref.shape[0])], sem_ref.at[first + index]
        )
        copy.start()
        copies.append(copy)
    return copies


def finish(copies):
    for copy in copies:
        copy.wait()


def attend_kernel(*refs, size, count, unit, factor):
    units_ref, x_ref, shift_ref, bias_ref = refs[:4]
    pieces = refs[4 : 4 + count]
    qkv_ref, p_ref, o_ref, w_ref, sem_ref = refs[4 + count :]
    pair = pl.program_id(0)
    model = x_ref.shape[1]
    width = o_ref.shape[1]

    @pl.when(pair == 0)
    def _():
        finish(start_fetch(pieces, units_ref, unit, w_ref, sem_ref, 0))
        for part in range(3):
            cols = slice(part * model, (part + 1) * model)
            value = dg(x_ref[...], w_ref[:, cols], NN) + shift_ref[:, cols]
            if part == 0:
                value = value * factor
            qkv_ref[:, cols] = value.astype(BF)

    def block(part):
        return qkv_ref[:, pl.ds(pl.multiple_of(part * model + pair * width, width), width)]

    lane = iota2((1, width), 1)
    q = block(0)
    k = block(1)
    vt = block(2).T
    mixed = []
    for g in range(width // size):
        mine = (lane >= g * size) & (lane < (g + 1) * size)
        scores = dg(jnp.where(mine, k, jnp.zeros_like(k)), q, NT) + bias_ref[g].astype(F32)
        top = jnp.max(scores, axis=0, keepdims=True)
        shifted = jnp.exp(scores - top)
        norm = jnp.sum(shifted, axis=0, keepdims=True)
        probs = (shifted * (1.0 / norm)).astype(BF)
        p_ref[g] = probs
        mixed.append(dg(vt[g * size : (g + 1) * size], probs, NN))
    o_ref[...] = jnp.concatenate(mixed, axis=0).T.astype(BF)


def attend(units, tokens, shift_row, weight, bias, size):
    length, model = tokens.shape
    group = WIDE // size
    count = len(weight.pieces)
    return pl.pallas_call(
        functools.partial(
            attend_kernel, size=size, count=count, unit=weight.unit, factor=size**-0.5
        ),
        grid=(model // WIDE,),
        in_specs=[
            SMEM,
            pl.BlockSpec((length, model), lambda i: (0, 0)),
            pl.BlockSpec((1, 3 * model), lambda i: (0, 0)),
            pl.BlockSpec((group, length, length), lambda i: (i, 0, 0)),
        ]
        + [ANY] * count,
        out_specs=[
            pl.BlockSpec((length, 3 * model), lambda i: (0, 0)),
            pl.BlockSpec((group, length, length), lambda i: (i, 0, 0)),
            pl.BlockSpec((length, WIDE), lambda i: (0, i)),
        ],
        out_shape=[
            shaped((length, 3 * model), BF),
            shaped((model // size, length, length), BF),
            shaped((length, model), BF),
        ],
        scratch_shapes=[
            pltpu.VMEM(weight.shape, BF),
            pltpu.SemaphoreType.DMA((count,)),
        ],
        compiler_params=params(),
        name="attend",
    )(units, tokens, shift_row, bias, *weight.pieces)


def attend_back_kernel(
    q_ref, k_ref, v_ref, p_ref, o_ref, g_ref, out_ref, ds_ref, *, size, factor
):
    pair = pl.program_id(0)
    width = q_ref.shape[1]
    model = out_ref.shape[1] // 3
    count = width // size
    lane = iota2((1, width), 1)
    q = q_ref[...]
    v = v_ref[...]
    ob = g_ref[...]
    kt = k_ref[...].T
    product = o_ref[...].astype(F32) * ob.astype(F32)
    qs, ks, vs = [], [], []
    for g in range(count):
        mine = (lane >= g * size) & (lane < (g + 1) * size)
        spare = ((g + 1) % count) * size
        inner = jnp.sum(jnp.where(mine, product, 0.0), axis=1, keepdims=True)
        high = inner.astype(BF).astype(F32)
        extra = jnp.where(lane == spare, high, jnp.where(lane == spare + 1, inner - high, 0.0))
        minus = jnp.where((lane == spare) | (lane == spare + 1), -1.0, 0.0)
        left = jnp.where(mine, v, minus.astype(BF))
        right = jnp.where(mine, ob, extra.astype(BF))
        probs = p_ref[g]
        ds = (probs.astype(F32) * dg(left, right, NT)).astype(BF)
        ds_ref[g] = ds
        vs.append(dg(probs, ob, NN))
        ks.append(dg(ds, q, NN))
        qs.append(dg(kt[g * size : (g + 1) * size], ds, NN))

    def pick(items):
        chosen = items[0]
        for g in range(1, count):
            chosen = jnp.where(lane >= g * size, items[g], chosen)
        return chosen

    def place(start):
        return pl.ds(pl.multiple_of(start + pair * width, width), width)

    q_grad = jnp.concatenate(qs, axis=0).T.astype(BF).astype(F32) * factor
    out_ref[:, place(0)] = q_grad.astype(BF)
    out_ref[:, place(model)] = pick(ks).astype(BF)
    out_ref[:, place(2 * model)] = pick(vs).astype(BF)


def attend_back(qkv, probs, mixed, grad_mixed, size):
    length = qkv.shape[0]
    model = qkv.shape[1] // 3
    blocks = model // WIDE
    group = WIDE // size
    return pl.pallas_call(
        functools.partial(attend_back_kernel, size=size, factor=size**-0.5),
        grid=(blocks,),
        in_specs=[
            pl.BlockSpec((length, WIDE), lambda i: (0, i)),
            pl.BlockSpec((length, WIDE), lambda i: (0, blocks + i)),
            pl.BlockSpec((length, WIDE), lambda i: (0, 2 * blocks + i)),
            pl.BlockSpec((group, length, length), lambda i: (i, 0, 0)),
            pl.BlockSpec((length, WIDE), lambda i: (0, i)),
            pl.BlockSpec((length, WIDE), lambda i: (0, i)),
        ],
        out_specs=[
            pl.BlockSpec((length, 3 * model), lambda i: (0, 0)),
            pl.BlockSpec((group, length, length), lambda i: (i, 0, 0)),
        ],
        out_shape=[
            shaped((length, 3 * model), BF),
            shaped((model // size, length, length), BF),
        ],
        compiler_params=params(),
        name="attend_back",
    )(qkv, qkv, qkv, probs, mixed, grad_mixed)


def norm_forward(inputs, gain_vec, shift_vec):
    center = inputs - jnp.mean(inputs, axis=-1, keepdims=True)
    inverse = lax.rsqrt(jnp.mean(center * center, axis=-1, keepdims=True) + EPSILON)
    scaled = center * inverse
    return (scaled * gain_vec + shift_vec, scaled, inverse)


def norm_backward(grad_in, scaled, inverse, gain_vec):
    inner_term = grad_in * gain_vec
    centered = inner_term - jnp.mean(inner_term, axis=-1, keepdims=True)
    return inverse * (centered - scaled * jnp.mean(inner_term * scaled, axis=-1, keepdims=True))


def gelu_pair(u):
    square = jnp.exp(u * u * -0.5)
    t = 1.0 / (1.0 + jnp.abs(u) * (0.3275911 * 0.7071067811865476))
    poly = t * (
        0.254829592
        + t * (-0.284496736 + t * (1.421413741 + t * (-1.453152027 + t * 1.061405429)))
    )
    tail = 0.5 * poly * square
    below = jnp.where(u >= 0.0, 1.0 - tail, tail)
    return u * below, below + u * (square * 0.3989422804014327)


def column_sum(values):
    return jnp.sum(values, axis=0, keepdims=True)


OUT_B, GAIN1, SHIFT1, DOWN_B, GAIN2, SHIFT2 = range(2, 8)


def forward_kernel(*refs, count, unit_out, unit_up, unit_down, chunk):
    units_ref, len_ref, mixed_ref, x_ref, cot_ref, vec_ref, upb_ref = refs[:7]
    out_pieces = refs[7 : 7 + count]
    up_pieces = refs[7 + count : 7 + 2 * count]
    down_pieces = refs[7 + 2 * count : 7 + 3 * count]
    (
        y_ref,
        n1_ref,
        z1_ref,
        r1_ref,
        hidden_out,
        slope_out,
        fb_ref,
        r2_ref,
        sums_ref,
        w_out,
        w_up,
        w_down,
        hidden,
        slope,
        sem_ref,
        out_sem,
    ) = refs[7 + 3 * count :]
    first = start_fetch(out_pieces, units_ref, unit_out, w_out, sem_ref, 0)
    second = start_fetch(up_pieces, units_ref, unit_up, w_up, sem_ref, count)
    third = start_fetch(down_pieces, units_ref, unit_down, w_down, sem_ref, 2 * count)

    def vec(row):
        return vec_ref[row : row + 1, :]

    finish(first)
    summed = x_ref[...].astype(F32) + (dg(mixed_ref[...], w_out[...], NN) + vec(OUT_B))
    n1, z1, r1 = norm_forward(summed, vec(GAIN1), vec(SHIFT1))
    low = n1.astype(BF)
    n1_ref[...] = low
    z1_ref[...] = z1
    r1_ref[...] = r1
    finish(second)
    total = hidden.shape[1]
    for begin in range(0, total, chunk):
        cols = slice(begin, begin + chunk)
        h, s = gelu_pair(dg(low, w_up[:, cols], NN) + upb_ref[:, cols])
        hidden[:, cols] = h.astype(BF)
        slope[:, cols] = s.astype(BF)
    saves = [
        pltpu.make_async_copy(hidden, hidden_out, out_sem.at[0]),
        pltpu.make_async_copy(slope, slope_out, out_sem.at[1]),
    ]
    for save in saves:
        save.start()
    finish(third)
    n2, z2, r2 = norm_forward(
        n1 + (dg(hidden[...], w_down[...], NN) + vec(DOWN_B)), vec(GAIN2), vec(SHIFT2)
    )
    rows = x_ref.shape[0]
    valid = (iota2((rows, 1), 0) < len_ref[0]).astype(F32)
    y_ref[...] = (n2 * valid).astype(BF)
    g2 = cot_ref[...].astype(F32) * valid
    back = norm_backward(g2, z2, r2, vec(GAIN2))
    r2_ref[...] = back
    fb = back.astype(BF)
    fb_ref[...] = fb
    sums_ref[...] = jnp.concatenate(
        [column_sum(fb.astype(F32)), column_sum(g2 * z2), column_sum(g2)]
        + [jnp.zeros((5, x_ref.shape[1]), F32)],
        axis=0,
    )
    finish(saves)


def forward(units, lengths, mixed, tokens, cotangent, vecs, up_bias, w_out, w_up, w_down):
    length, model = tokens.shape
    wide = up_bias.shape[1]
    count = len(w_out.pieces)
    return pl.pallas_call(
        functools.partial(
            forward_kernel,
            count=count,
            unit_out=w_out.unit,
            unit_up=w_up.unit,
            unit_down=w_down.unit,
            chunk=512,
        ),
        in_specs=[SMEM, SMEM] + [VMEM] * 5 + [ANY] * (3 * count),
        out_specs=[VMEM] * 4 + [ANY] * 2 + [VMEM] * 3,
        out_shape=[
            shaped((length, model), BF),
            shaped((length, model), BF),
            shaped((length, model), F32),
            shaped((length, 1), F32),
            shaped((length, wide), BF),
            shaped((length, wide), BF),
            shaped((length, model), BF),
            shaped((length, model), F32),
            shaped((8, model), F32),
        ],
        scratch_shapes=[
            pltpu.VMEM(w_out.shape, BF),
            pltpu.VMEM(w_up.shape, BF),
            pltpu.VMEM(w_down.shape, BF),
            pltpu.VMEM((length, wide), BF),
            pltpu.VMEM((length, wide), BF),
            pltpu.SemaphoreType.DMA((3 * count,)),
            pltpu.SemaphoreType.DMA((2,)),
        ],
        compiler_params=params(),
        name="forward",
    )(
        units,
        lengths,
        mixed,
        tokens,
        cotangent,
        vecs,
        up_bias,
        *w_out.pieces,
        *w_up.pieces,
        *w_down.pieces,
    )


def backward_kernel(*refs, count, unit_out, unit_up, unit_down, chunk):
    units_ref, fb_ref, r2_ref, z1_ref, r1_ref, vec_ref, slope_in = refs[:7]
    out_pieces = refs[7 : 7 + count]
    up_pieces = refs[7 + count : 7 + 2 * count]
    down_pieces = refs[7 + 2 * count : 7 + 3 * count]
    (
        ub_out,
        back_ref,
        ab_ref,
        ob_ref,
        sums_ref,
        upsum_ref,
        w_out,
        w_up,
        w_down,
        slope,
        sem_ref,
        own_sem,
    ) = refs[7 + 3 * count :]
    load = pltpu.make_async_copy(slope_in, slope, own_sem.at[0])
    third = start_fetch(down_pieces, units_ref, unit_down, w_down, sem_ref, 0)
    load.start()
    second = start_fetch(up_pieces, units_ref, unit_up, w_up, sem_ref, count)
    first = start_fetch(out_pieces, units_ref, unit_out, w_out, sem_ref, 2 * count)
    fb = fb_ref[...]
    finish(third)
    load.wait()
    for begin in range(0, slope.shape[1], chunk):
        cols = slice(begin, begin + chunk)
        ub = (slope[:, cols].astype(F32) * dg(fb, w_down[cols, :], NT)).astype(BF)
        slope[:, cols] = ub
        upsum_ref[:, cols] = column_sum(ub.astype(F32))
    save = pltpu.make_async_copy(slope, ub_out, own_sem.at[1])
    save.start()
    finish(second)
    n1b = r2_ref[...] + dg(slope[...], w_up[...], NT)
    z1 = z1_ref[...]
    back = norm_backward(n1b, z1, r1_ref[...], vec_ref[GAIN1 : GAIN1 + 1, :])
    back_ref[...] = back
    ab = back.astype(BF)
    ab_ref[...] = ab
    sums_ref[...] = jnp.concatenate(
        [column_sum(ab.astype(F32)), column_sum(n1b * z1), column_sum(n1b)]
        + [jnp.zeros((5, z1.shape[1]), F32)],
        axis=0,
    )
    finish(first)
    ob_ref[...] = dg(ab, w_out[...], NT).astype(BF)
    save.wait()


def backward(units, fb, r2, z1, r1, vecs, slope, w_out, w_up, w_down):
    length, model = fb.shape
    wide = slope.shape[1]
    count = len(w_out.pieces)
    return pl.pallas_call(
        functools.partial(
            backward_kernel,
            count=count,
            unit_out=w_out.unit,
            unit_up=w_up.unit,
            unit_down=w_down.unit,
            chunk=512,
        ),
        in_specs=[SMEM] + [VMEM] * 5 + [ANY] * (1 + 3 * count),
        out_specs=[ANY] + [VMEM] * 5,
        out_shape=[
            shaped((length, wide), BF),
            shaped((length, model), F32),
            shaped((length, model), BF),
            shaped((length, model), BF),
            shaped((8, model), F32),
            shaped((1, wide), F32),
        ],
        scratch_shapes=[
            pltpu.VMEM(w_out.shape, BF),
            pltpu.VMEM(w_up.shape, BF),
            pltpu.VMEM(w_down.shape, BF),
            pltpu.VMEM((length, wide), BF),
            pltpu.SemaphoreType.DMA((3 * count,)),
            pltpu.SemaphoreType.DMA((2,)),
        ],
        compiler_params=params(),
        name="backward",
    )(
        units,
        fb,
        r2,
        z1,
        r1,
        vecs,
        slope,
        *w_out.pieces,
        *w_up.pieces,
        *w_down.pieces,
    )


def inputs_kernel(*refs, count, unit):
    units_ref, pb_ref, back_ref = refs[:3]
    pieces = refs[3 : 3 + count]
    out_ref, sums_ref, w_ref, sem_ref = refs[3 + count :]
    copies = start_fetch(pieces, units_ref, unit, w_ref, sem_ref, 0)
    pb = pb_ref[...]
    sums_ref[...] = column_sum(pb.astype(F32))
    finish(copies)
    out_ref[...] = (back_ref[...] + dg(pb, w_ref[...], NT)).astype(BF)


def inputs_grad(units, grad_packed, back, weight):
    length, model = back.shape
    count = len(weight.pieces)
    return pl.pallas_call(
        functools.partial(inputs_kernel, count=count, unit=weight.unit),
        in_specs=[SMEM] + [VMEM] * 2 + [ANY] * count,
        out_specs=[VMEM] * 2,
        out_shape=[shaped((length, model), BF), shaped((1, 3 * model), F32)],
        scratch_shapes=[
            pltpu.VMEM(weight.shape, BF),
            pltpu.SemaphoreType.DMA((count,)),
        ],
        compiler_params=params(),
        name="inputs_grad",
    )(units, grad_packed, back, *weight.pieces)


def product_kernel(at_ref, left_ref, right_ref, *rest):
    value = dg(left_ref[...], right_ref[...], TN)
    if len(rest) == 2:
        value = value + rest[0][...].astype(F32)
    rest[-1][...] = value.astype(BF)


def product(left, right, half, halves, extra=None):
    length, rows = left.shape
    columns = right.shape[1] // halves
    if rows % WIDE or columns % WIDE:
        value = dg(left, lax.dynamic_slice_in_dim(right, half * columns, columns, 1), TN)
        return (value if extra is None else value + extra.astype(F32)).astype(BF)
    step = WIDE
    while step < 512 and rows % (2 * step) == 0:
        step *= 2
    spec = pl.BlockSpec((step, columns), lambda i, at: (i, 0))
    return pl.pallas_call(
        product_kernel,
        grid_spec=pltpu.PrefetchScalarGridSpec(
            num_scalar_prefetch=1,
            grid=(rows // step,),
            in_specs=[
                pl.BlockSpec((length, step), lambda i, at: (0, i)),
                pl.BlockSpec((length, columns), lambda i, at: (0, at[0])),
            ]
            + ([] if extra is None else [spec]),
            out_specs=spec,
        ),
        out_shape=shaped((rows, columns), BF),
        compiler_params=params(),
        name="product",
    )(half.reshape(1), left, right, *(() if extra is None else (extra,)))


def finish_kernel(at_ref, mine_ref, theirs_ref, out_ref):
    columns = mine_ref.shape[1]
    first = at_ref[0] == 0
    mine = mine_ref[...]
    theirs = theirs_ref[...]
    out_ref[:, :columns] = jnp.where(first, mine, theirs).astype(F32)
    out_ref[:, columns:] = jnp.where(first, theirs, mine).astype(F32)


def finish_pair(core, mine, theirs):
    rows, columns = mine.shape
    step = rows // 4 if (rows // 4) % 16 == 0 else rows
    spec = pl.BlockSpec((step, columns), lambda i: (i, 0))
    return pl.pallas_call(
        finish_kernel,
        grid=(rows // step,),
        in_specs=[SMEM, spec, spec],
        out_specs=pl.BlockSpec((step, 2 * columns), lambda i: (i, 0)),
        out_shape=shaped((rows, 2 * columns), F32),
        compiler_params=params(),
        name="finish_pair",
    )(core.reshape(1), mine, theirs)


class Axis:
    def __init__(self, name, total, stride, size):
        self.name = name
        self.total = total
        self.stride = stride
        self.size = size
        self.at = (lax.axis_index(name) // stride) % size

    def send(self, value, step):
        pairs = []
        for index in range(self.total):
            place = (index // self.stride) % self.size
            pairs.append((index, index + ((place + step) % self.size - place) * self.stride))
        return lax.ppermute(value, self.name, pairs)

    def peer(self, step):
        return (self.at + step) % self.size


def tie(value, *others):
    return lax.optimization_barrier((value,) + others)[0]


def take(stack, index, dim=0):
    return lax.dynamic_index_in_dim(stack, index, axis=dim, keepdims=False)


def gather(axis, block, dim=0):
    if axis.size == 1:
        return jnp.expand_dims(block, dim)
    shape = [1] * (block.ndim + 1)
    shape[dim] = axis.size
    place = jnp.arange(axis.size, dtype=jnp.int32).reshape(shape)
    stack = jnp.expand_dims(block, dim)
    for step in range(1, axis.size):
        got = jnp.expand_dims(axis.send(block, step), dim)
        stack = jnp.where(place == axis.peer(-step), got, stack)
    return stack


class Links:
    def __init__(self, dp, fsdp):
        core = 2 if dp % 2 == 0 else 1
        rest = dp // core
        near = 2 if rest % 2 == 0 else 1
        self.core = Axis("dp", dp, 1, core)
        self.near = Axis("dp", dp, core, near)
        self.far = Axis("dp", dp, core * near, rest // near)
        self.shard = Axis("fsdp", fsdp, 1, fsdp)

    def plan(self, least_rows):
        core, near, shard = self.core, self.near, self.shard
        self.sharing = (core, near)
        if least_rows % (core.size * near.size * 16):
            self.sharing = (core,)
        parts = 1
        for axis in self.sharing:
            parts *= axis.size
        self.parts = parts
        units = [shard.at * parts]
        for step in range(1, shard.size):
            base = shard.peer(-step) * parts
            if len(self.sharing) == 1:
                spots = [core.peer(-s) for s in range(core.size)]
            else:
                spots = [
                    core.peer(-s) * near.size + near.peer(-t)
                    for s in range(core.size)
                    for t in range(near.size)
                ]
            units += [base + spot for spot in spots]
        return jnp.stack(units).astype(jnp.int32)

    def fetch(self, block, *after):
        core, near, shard = self.core, self.near, self.shard
        rows, columns = block.shape
        unit = rows // self.parts
        stack = block.reshape(self.parts, unit, columns)
        spot = core.at if len(self.sharing) == 1 else core.at * near.size + near.at
        mine = take(stack, spot)
        if after:
            mine = tie(mine, *after)
        pieces = [block]
        hops = []
        for step in range(1, shard.size):
            group = [shard.send(mine, step)]
            hops.append(group[0])
            if len(self.sharing) > 1:
                group += [near.send(group[0], t) for t in range(1, near.size)]
            pieces += group
            for s in range(1, core.size):
                pieces += [core.send(item, s) for item in group]
        return Weight(pieces, unit, (rows * shard.size, columns)), hops

    def halves(self, left, right, *after):
        core = self.core
        if core.size == 1:
            return product(left, right, core.at, 1)
        sent = product(left, right, core.peer(1), core.size)
        got = core.send(sent, 1)
        return sent, lambda: product(left, right, core.at, core.size, got)

    def spread(self, half):
        rows, columns = half.shape
        sizes = (self.shard.size, self.near.size, self.far.size)
        return half.reshape(sizes + (rows // (sizes[0] * sizes[1] * sizes[2]), columns))

    def hop(self, terms, axis, dim, *after):
        if axis.size == 1:
            return [take(term, axis.at, dim) for term in terms], []

        def part(index):
            total = None
            for term in terms:
                piece = take(term, index, dim).astype(F32)
                total = piece if total is None else total + piece
            return total.astype(BF)

        kept = [take(term, axis.at, dim) for term in terms]
        sent = []
        for step in range(1, axis.size):
            value = part(axis.peer(step))
            sent.append(tie(value, *after) if after else value)
        return kept + [axis.send(value, step + 1) for step, value in enumerate(sent)], sent

    def settle(self, terms):
        total = terms[0].astype(F32)
        for term in terms[1:]:
            total = total + term.astype(F32)
        return total.astype(BF)

    def spread_out(self, block):
        whole = gather(self.near, gather(self.far, block))
        whole = whole.reshape(-1, block.shape[-1])
        if self.core.size == 1:
            return whole.astype(F32)
        return finish_pair(self.core.at, whole, self.core.send(whole, 1))

    def reduce_vector(self, stack):
        shard = self.shard
        total = take(stack, shard.at)
        for step in range(1, shard.size):
            total = total + shard.send(take(stack, shard.peer(step)), step)
        for axis in (self.core, self.near, self.far):
            part = total
            for step in range(1, axis.size):
                total = total + axis.send(part, step)
        return total


def pack(items, shards):
    return jnp.concatenate([item.reshape(shards, -1) for item in items], axis=1)


def split(vector, sizes):
    pieces = []
    begin = 0
    for count in sizes:
        pieces.append(vector[begin : begin + count])
        begin += count
    return pieces


def per_device(
    dp,
    fsdp,
    tokens,
    lengths,
    buckets,
    qkv_weight,
    q_bias,
    v_bias,
    out_weight,
    out_bias,
    bias_table,
    norm1_gain,
    norm1_bias,
    up_weight,
    up_bias,
    down_weight,
    down_bias,
    norm2_gain,
    norm2_bias,
    cotangent,
):
    links = Links(dp, fsdp)
    model = tokens.shape[1]
    heads = bias_table.shape[1]
    size = model // heads
    units = links.plan(min(out_weight.shape[0], down_weight.shape[0]))

    w_qkv, hop_qkv = links.fetch(qkv_weight)
    table = gather(links.shard, bias_table).reshape(-1, heads)
    narrow = (q_bias, v_bias, out_bias, norm1_gain, norm1_bias, down_bias, norm2_gain, norm2_bias)
    row = jnp.arange(8, dtype=jnp.int32)[:, None]
    rows = jnp.broadcast_to(narrow[0][None], (8, narrow[0].size))
    for index in range(1, 8):
        rows = jnp.where(row == index, narrow[index][None], rows)
    vecs = jnp.swapaxes(gather(links.shard, rows), 0, 1).reshape(8, model).astype(F32)
    up_vec = gather(links.shard, up_bias).reshape(1, -1).astype(F32)
    w_out, hop_out = links.fetch(out_weight, *hop_qkv)
    w_up, hop_up = links.fetch(up_weight, *hop_qkv)
    w_down, _ = links.fetch(down_weight, *hop_up)

    bias, ids = bias_scores(buckets, lengths, table)
    shift_row = jnp.concatenate([vecs[0:1], jnp.zeros((1, model), F32), vecs[1:2]], axis=1)
    qkv, probs, mixed = attend(units, tokens, shift_row, w_qkv, bias, size)
    output, n1, z1, r1, hidden, slope, fb, r2, sums_two = forward(
        units, lengths, mixed, tokens, cotangent, vecs, up_vec, w_out, w_up, w_down
    )

    sent_down, half_down = links.halves(hidden, fb)
    fb = tie(fb, sent_down)
    ub, back, ab, ob, sums_one, up_sum = backward(
        units, fb, r2, z1, r1, vecs, slope, w_out, w_up, w_down
    )
    down = links.spread(half_down())
    down, sent = links.hop([down], links.shard, 0)
    ub = tie(ub, *sent)
    sent_up, half_up = links.halves(n1, ub)
    ab = tie(ab, sent_up)
    sent_out, half_out = links.halves(mixed, ab)
    up = links.spread(half_up())
    up, sent = links.hop([up], links.near, 1)
    out = links.spread(half_out())
    ob = tie(ob, out, *sent)
    grad_packed, grad_scores = attend_back(qkv, probs, mixed, ob, size)
    sent_qkv, half_qkv = links.halves(tokens, grad_packed)
    qkv_part = links.spread(half_qkv())
    grad_scores = tie(grad_scores, qkv_part)
    g_table = table_grad(ids, grad_scores, table.shape[0])
    grad_packed = tie(grad_packed, g_table)
    tokens_grad, packed_sums = inputs_grad(units, grad_packed, back, w_qkv)

    got_down = down[-1]
    down, _ = links.hop(down, links.near, 0, up[-1])
    down, _ = links.hop(down, links.far, 0)
    up, _ = links.hop(up, links.shard, 0, got_down)
    got_up = up[-1]
    up, _ = links.hop(up, links.far, 0)
    out, _ = links.hop([out], links.shard, 0, got_up)
    qkv_terms, _ = links.hop([qkv_part], links.shard, 0, got_up)
    out, _ = links.hop(out, links.near, 0)
    out, _ = links.hop(out, links.far, 0)
    qkv_terms, _ = links.hop(qkv_terms, links.near, 0)
    qkv_terms, _ = links.hop(qkv_terms, links.far, 0)

    g_down = links.spread_out(links.settle(down))
    g_up = links.spread_out(links.settle(up))
    g_out = links.spread_out(links.settle(out))
    g_qkv = links.spread_out(links.settle(qkv_terms))

    early = links.reduce_vector(
        pack((sums_one[0], sums_one[1], sums_one[2], up_sum, sums_two[0], sums_two[1], sums_two[2]), fsdp)
    )
    late = links.reduce_vector(
        pack((g_table, packed_sums[0, :model], packed_sums[0, 2 * model :]), fsdp)
    )
    part = out_bias.size
    g_out_bias, g_gain_one, g_shift_one, g_up_bias, g_down_bias, g_gain_two, g_shift_two = split(
        early, (part, part, part, up_bias.size, part, part, part)
    )
    g_table, g_query_bias, g_value_bias = split(late, (bias_table.size, part, part))
    return (
        output,
        tokens_grad,
        g_qkv,
        g_query_bias,
        g_value_bias,
        g_out,
        g_out_bias,
        g_table.reshape(bias_table.shape),
        g_gain_one,
        g_shift_one,
        g_up,
        g_up_bias,
        g_down,
        g_down_bias,
        g_gain_two,
        g_shift_two,
    )


def solution(mesh):
    rows = P(("dp", "fsdp"), None)
    mat = P("fsdp", None)
    vec = P("fsdp")
    return jax.shard_map(
        functools.partial(per_device, mesh.shape["dp"], mesh.shape["fsdp"]),
        mesh=mesh,
        in_specs=(
            rows,
            P(("dp", "fsdp")),
            P(("dp", "fsdp"), None, None, None),
            mat,
            vec,
            vec,
            mat,
            vec,
            mat,
            vec,
            vec,
            mat,
            vec,
            mat,
            vec,
            vec,
            vec,
            rows,
        ),
        out_specs=(
            rows,
            rows,
            mat,
            vec,
            vec,
            mat,
            vec,
            mat,
            vec,
            vec,
            mat,
            vec,
            mat,
            vec,
            vec,
            vec,
        ),
        check_vma=False,
    )
```

```python
import functools

import jax
import jax.numpy as jnp
from jax import lax
from jax.experimental import pallas as pl
from jax.experimental.pallas import tpu as pltpu
from jax.sharding import PartitionSpec as P

EPSILON = 1e-05
MASKED = -1000000000.0
BF = jnp.bfloat16
F32 = jnp.float32
NN = (((1,), (0,)), ((), ()))
NT = (((1,), (1,)), ((), ()))
TN = (((0,), (0,)), ((), ()))
VMEM_LIMIT = 56 * 2**20
WIDE = 128
ANY = pl.BlockSpec(memory_space=pl.ANY)
SMEM = pl.BlockSpec(memory_space=pltpu.SMEM)
VMEM = pl.BlockSpec(memory_space=pltpu.VMEM)


def dg(left, right, dims):
    return lax.dot_general(left, right, dims, preferred_element_type=F32)


def params():
    return pltpu.CompilerParams(vmem_limit_bytes=VMEM_LIMIT)


def cost(micros):
    return pl.CostEstimate(flops=0, bytes_accessed=int(micros * 3e6), transcendentals=0)


def shaped(shape, dtype):
    return jax.ShapeDtypeStruct(shape, dtype)


def onehot_rows(ids, oh_ref, bucket_count):
    length = ids[0].shape[1]
    sub = lax.broadcasted_iota(jnp.int32, (16, length), 0)
    one = jnp.ones((16, length), BF)
    zero = jnp.zeros((16, length), BF)
    half = bucket_count // 2
    for kind in range(3):
        both = jnp.concatenate([ids[kind], ids[kind]], axis=0).astype(BF)
        for pair in range(half):
            level = jnp.where(sub < 8, 2 * pair, 2 * pair + 1).astype(F32).astype(BF)
            oh_ref[pl.ds((kind * half + pair) * 16, 16), :] = jnp.where(both == level, one, zero)


def iota2(shape, dim):
    return lax.broadcasted_iota(jnp.int32, shape, dim)


def bias_kernel(len_ref, ids_ref, table_ref, *rest, first):
    out_ref, turned_ref, spread_ref, held_ref, oh_ref = rest[-5:]
    step0 = pl.program_id(0)
    block = step0 + first
    heads, rows, length = out_ref.shape
    entries = table_ref.shape[0]
    valid = len_ref[0]

    @pl.when(step0 == 0)
    def _():
        pick_head = (iota2((heads * 8, heads), 0) >> 3) == iota2((heads * 8, heads), 1)
        rows_of = dg(pick_head.astype(F32).astype(BF), table_ref[...], NT).astype(BF)
        shape = (entries, entries * 8)
        pick_entry = iota2(shape, 0) == (iota2(shape, 1) >> 3)
        wide = dg(rows_of, pick_entry.astype(F32).astype(BF), NN)
        shape = (heads * 8, entries * 8)
        same = (iota2(shape, 0) & 7) == (iota2(shape, 1) & 7)
        spread_ref[...] = jnp.where(same, wide, 0.0).astype(BF)

    for kind in range(3):
        turned = ids_ref[0, kind].astype(F32).T
        held_ref[kind] = turned
        turned_ref[kind] = turned.astype(BF)

    def body(step, carry):
        parts = []
        for u in range(2):
            group = pl.ds(pl.multiple_of(step * 16 + u * 8, 8), 8)
            onehot_rows([held_ref[kind, group, :] for kind in range(3)], oh_ref.at[u], entries // 3)
            parts.append(dg(spread_ref[...], oh_ref[u], NN).reshape(heads, 8, length))
        bias = jnp.concatenate(parts, axis=1)
        key = iota2((1, 16, length), 1) + (block * rows + step * 16)
        out_ref[:, pl.ds(pl.multiple_of(step * 16, 16), 16), :] = jnp.where(
            key < valid, bias, MASKED
        ).astype(BF)
        return carry

    lax.fori_loop(0, rows // 16, body, 0, unroll=4)


def bias_scores(buckets, valid, table, part, parts, before=None, rows=128):
    length = buckets.shape[-1]
    entries, heads = table.shape
    steps = length // rows // parts
    first = part * steps
    held = () if before is None else tuple(before)
    return pl.pallas_call(
        functools.partial(bias_kernel, first=first),
        grid=(steps,),
        in_specs=[
            SMEM,
            pl.BlockSpec((1, 3, length, rows), lambda i: (0, 0, 0, first + i)),
            pl.BlockSpec((entries, heads), lambda i: (0, 0)),
        ]
        + [ANY] * len(held),
        out_specs=[
            pl.BlockSpec((heads, rows, length), lambda i: (0, first + i, 0)),
            pl.BlockSpec((3, rows, length), lambda i: (0, first + i, 0)),
        ],
        out_shape=[shaped((heads, length, length), BF), shaped((3, length, length), BF)],
        scratch_shapes=[
            pltpu.VMEM((heads * 8, entries * 8), BF),
            pltpu.VMEM((3, rows, length), F32),
            pltpu.VMEM((2, entries * 8, length), BF),
        ],
        input_output_aliases={3: 0, 4: 1} if held else {},
        compiler_params=params(),
        cost_estimate=cost(8),
        name="bias_scores",
    )(valid, buckets, table, *held)


def table_kernel(ids_ref, grad_ref, out_ref, acc_ref, oh_ref):
    heads, rows, length = grad_ref.shape
    entries = out_ref.shape[1]

    @pl.when(pl.program_id(0) == 0)
    def _():
        acc_ref[...] = jnp.zeros_like(acc_ref)

    def body(step, carry):
        tile = pl.ds(pl.multiple_of(step * 16, 16), 16)
        grads = grad_ref[:, tile, :].astype(F32)
        ids = [ids_ref[kind, tile, :].astype(F32) for kind in range(3)]
        total = None
        for u in range(2):
            part = slice(u * 8, (u + 1) * 8)
            onehot_rows([item[part] for item in ids], oh_ref.at[u], entries // 3)
            part = dg(oh_ref[u], grads[:, part, :].reshape(heads * 8, length).astype(BF), NT)
            total = part if total is None else total + part
        acc_ref[...] += total
        return carry

    lax.fori_loop(0, rows // 16, body, 0, unroll=4)

    @pl.when(pl.program_id(0) == pl.num_programs(0) - 1)
    def _():
        shape = acc_ref.shape
        same = (iota2(shape, 0) & 7) == (iota2(shape, 1) & 7)
        kept = jnp.where(same, acc_ref[...], 0.0)
        rows_in = kept.reshape(entries, 8, heads * 8).sum(axis=1)
        shape = (out_ref.shape[0], heads * 8)
        fold = (iota2(shape, 0) == (iota2(shape, 1) >> 3)).astype(F32)
        out_ref[...] = lax.dot_general(
            fold, rows_in, NT, precision=lax.Precision.HIGHEST, preferred_element_type=F32
        )


def table_grad(ids, grads, entries, part, parts, rows=64):
    heads, length, _ = grads.shape
    padded = -(-heads // 8) * 8
    steps = length // rows // parts
    first = part * steps
    return pl.pallas_call(
        table_kernel,
        grid=(steps,),
        in_specs=[
            pl.BlockSpec((3, rows, length), lambda i: (0, first + i, 0)),
            pl.BlockSpec((heads, rows, length), lambda i: (0, first + i, 0)),
        ],
        out_specs=pl.BlockSpec((padded, entries), lambda i: (0, 0)),
        out_shape=shaped((padded, entries), F32),
        scratch_shapes=[
            pltpu.VMEM((entries * 8, heads * 8), F32),
            pltpu.VMEM((2, entries * 8, length), BF),
        ],
        compiler_params=params(),
        cost_estimate=cost(9.5),
        name="table_grad",
    )(ids, grads)


class Place:
    def __init__(self, rows, blocks, begin=0, shard=0, unit=0, core=0, mate=0, which=None):
        self.rows = rows
        self.blocks = blocks
        self.begin = begin
        self.shard = shard
        self.unit = unit
        self.core = core
        self.mate = mate
        self.which = which

    def row(self, coords_ref):
        def at(index, step, size):
            return lax.rem(coords_ref[index] + step % size, size)

        row = at(3, self.shard, self.blocks) * self.rows + self.begin
        if not self.unit:
            return row
        spot = at(0, self.core, 2)
        if self.which is not None:
            spot = spot * 2 + at(self.which, self.mate, 2)
        return row + spot * self.unit


class Weight:
    def __init__(self, pieces, places, shape):
        self.pieces = pieces
        self.places = places
        self.shape = shape
        self.count = len(pieces)


def start_fetch(refs, places, coords_ref, whole_ref, sem_ref, first=0):
    copies = []
    for index, ref in enumerate(refs):
        begin = pl.multiple_of(places[index].row(coords_ref), 16)
        copy = pltpu.make_async_copy(
            ref, whole_ref.at[pl.ds(begin, ref.shape[0])], sem_ref.at[first + index]
        )
        copy.start()
        copies.append(copy)
    return copies


def finish(copies):
    for copy in copies:
        copy.wait()


def save_halves(core_ref, whole_ref, sent_ref, kept_ref, sem_ref, first, begin=0):
    columns = whole_ref.shape[1] // 2
    mine = core_ref[0]
    copies = []
    for index, (half, ref) in enumerate(((1 - mine, sent_ref), (mine, kept_ref))):
        cols = pl.ds(pl.multiple_of(half * columns, WIDE), columns)
        copy = pltpu.make_async_copy(
            whole_ref.at[:, cols], ref.at[:, pl.ds(begin, columns)], sem_ref.at[first + index]
        )
        copy.start()
        copies.append(copy)
    return copies


def attend_pair(q, k, v, bias_ref, p_ref, o_ref, ot_ref, size):
    width = q.shape[1]
    lane = iota2((1, width), 1)
    vt = v.T
    mixed = []
    for g in range(width // size):
        mine = (lane >= g * size) & (lane < (g + 1) * size)
        scores = dg(jnp.where(mine, k, jnp.zeros_like(k)), q, NT) + bias_ref[g].astype(F32)
        top = jnp.max(scores, axis=0, keepdims=True)
        shifted = jnp.exp(scores - top)
        norm = jnp.sum(shifted, axis=0, keepdims=True)
        probs = (shifted * (1.0 / norm)).astype(BF)
        p_ref[g] = probs
        mixed.append(dg(vt[g * size : (g + 1) * size], probs, NN))
    turned = jnp.concatenate(mixed, axis=0)
    ot_ref[...] = turned.astype(BF)
    o_ref[...] = turned.T.astype(BF)


def attend_first_kernel(*refs, size, places, factor):
    count = len(places)
    coords_ref, x_ref, shift_ref, bias_ref = refs[:4]
    pieces = refs[4 : 4 + count]
    qkv_ref, p_ref, o_ref, ot_ref, xt_ref, w_ref, sem_ref = refs[4 + count :]
    pair = pl.program_id(0)
    model = x_ref.shape[1]
    width = o_ref.shape[1]

    @pl.when(pair == 0)
    def _():
        copies = start_fetch(pieces, places, coords_ref, w_ref, sem_ref)
        xt_ref[...] = x_ref[...].T
        finish(copies)
        for part in range(3):
            cols = slice(part * model, (part + 1) * model)
            value = dg(x_ref[...], w_ref[:, cols], NN) + shift_ref[:, cols]
            if part == 0:
                value = value * factor
            qkv_ref[:, cols] = value.astype(BF)

    def block(part):
        return qkv_ref[:, pl.ds(pl.multiple_of(part * model + pair * width, width), width)]

    attend_pair(block(0), block(1), block(2), bias_ref, p_ref, o_ref, ot_ref, size)


def attend_rest_kernel(q_ref, k_ref, v_ref, bias_ref, _p, _o, _ot, p_ref, o_ref, ot_ref, *, size):
    attend_pair(q_ref[...], k_ref[...], v_ref[...], bias_ref, p_ref, o_ref, ot_ref, size)


def attend_first(coords, tokens, shift_row, weight, bias, size, steps):
    length, model = tokens.shape
    group = WIDE // size
    count = weight.count
    return pl.pallas_call(
        functools.partial(
            attend_first_kernel, size=size, places=weight.places, factor=size**-0.5
        ),
        grid=(steps,),
        in_specs=[
            SMEM,
            pl.BlockSpec((length, model), lambda i: (0, 0)),
            pl.BlockSpec((1, 3 * model), lambda i: (0, 0)),
            pl.BlockSpec((group, length, length), lambda i: (i, 0, 0)),
        ]
        + [ANY] * count,
        out_specs=[
            pl.BlockSpec((length, 3 * model), lambda i: (0, 0)),
            pl.BlockSpec((group, length, length), lambda i: (i, 0, 0)),
            pl.BlockSpec((length, WIDE), lambda i: (0, i)),
            pl.BlockSpec((WIDE, length), lambda i: (i, 0)),
            pl.BlockSpec((model, length), lambda i: (0, 0)),
        ],
        out_shape=[
            shaped((length, 3 * model), BF),
            shaped((model // size, length, length), BF),
            shaped((length, model), BF),
            shaped((model, length), BF),
            shaped((model, length), BF),
        ],
        scratch_shapes=[pltpu.VMEM(weight.shape, BF), pltpu.SemaphoreType.DMA((count,))],
        compiler_params=params(),
        cost_estimate=cost(11.5),
        name="attend_first",
    )(coords, tokens, shift_row, bias, *weight.pieces)


def attend_rest(qkv, bias, probs, mixed, turned, size, first):
    length, model = mixed.shape
    group = WIDE // size
    blocks = model // WIDE
    return pl.pallas_call(
        functools.partial(attend_rest_kernel, size=size),
        grid=(blocks - first,),
        in_specs=[
            pl.BlockSpec((length, WIDE), lambda i: (0, first + i)),
            pl.BlockSpec((length, WIDE), lambda i: (0, blocks + first + i)),
            pl.BlockSpec((length, WIDE), lambda i: (0, 2 * blocks + first + i)),
            pl.BlockSpec((group, length, length), lambda i: (first + i, 0, 0)),
            ANY,
            ANY,
            ANY,
        ],
        out_specs=[
            pl.BlockSpec((group, length, length), lambda i: (first + i, 0, 0)),
            pl.BlockSpec((length, WIDE), lambda i: (0, first + i)),
            pl.BlockSpec((WIDE, length), lambda i: (first + i, 0)),
        ],
        out_shape=[
            shaped(probs.shape, BF),
            shaped(mixed.shape, BF),
            shaped(turned.shape, BF),
        ],
        input_output_aliases={4: 0, 5: 1, 6: 2},
        compiler_params=params(),
        cost_estimate=cost(7),
        name="attend_rest",
    )(qkv, qkv, qkv, bias, probs, mixed, turned)


def attend_back_kernel(
    core_ref,
    q_ref,
    k_ref,
    v_ref,
    p_ref,
    o_ref,
    g_ref,
    xt_ref,
    prior_ref,
    out_ref,
    ds_ref,
    sent_ref,
    kept_ref,
    product_ref,
    sem_ref,
    *,
    size,
    factor,
):
    pair = pl.program_id(0)
    width = q_ref.shape[1]
    model = out_ref.shape[1] // 3
    count = width // size
    lane = iota2((1, width), 1)
    q = q_ref[...]
    v = v_ref[...]
    ob = g_ref[...]
    kt = k_ref[...].T
    product = o_ref[...].astype(F32) * ob.astype(F32)
    qs, ks, vs = [], [], []
    for g in range(count):
        mine = (lane >= g * size) & (lane < (g + 1) * size)
        spare = ((g + 1) % count) * size
        inner = jnp.sum(jnp.where(mine, product, 0.0), axis=1, keepdims=True)
        high = inner.astype(BF).astype(F32)
        extra = jnp.where(lane == spare, high, jnp.where(lane == spare + 1, inner - high, 0.0))
        minus = jnp.where((lane == spare) | (lane == spare + 1), -1.0, 0.0)
        left = jnp.where(mine, v, minus.astype(BF))
        right = jnp.where(mine, ob, extra.astype(BF))
        probs = p_ref[g]
        ds = (probs.astype(F32) * dg(left, right, NT)).astype(BF)
        ds_ref[g] = ds
        vs.append(dg(probs, ob, NN))
        ks.append(dg(ds, q, NN))
        qs.append(dg(kt[g * size : (g + 1) * size], ds, NN))

    def pick(items):
        chosen = items[0]
        for g in range(1, count):
            chosen = jnp.where(lane >= g * size, items[g], chosen)
        return chosen

    def place(start):
        return pl.ds(pl.multiple_of(start + pair * width, width), width)

    q_grad = jnp.concatenate(qs, axis=0).T.astype(BF).astype(F32) * factor
    out_ref[:, place(0)] = q_grad.astype(BF)
    out_ref[:, place(model)] = pick(ks).astype(BF)
    out_ref[:, place(2 * model)] = pick(vs).astype(BF)

    @pl.when(pair == pl.num_programs(0) - 1)
    def _():
        begin = prior_ref.shape[1] // 2
        copies = save_halves(core_ref, prior_ref, sent_ref, kept_ref, sem_ref, 0)
        for part in range(3):
            cols = slice(part * model, (part + 1) * model)
            product_ref[:, cols] = dg(xt_ref[...], out_ref[:, cols], NN).astype(BF)
        copies += save_halves(core_ref, product_ref, sent_ref, kept_ref, sem_ref, 2, begin)
        finish(copies)


def attend_back(core, qkv, probs, mixed, grad_mixed, turned, prior, size):
    length = qkv.shape[0]
    model = qkv.shape[1] // 3
    blocks = model // WIDE
    group = WIDE // size
    halves = shaped((model, (prior.shape[1] + 3 * model) // 2), BF)
    return pl.pallas_call(
        functools.partial(attend_back_kernel, size=size, factor=size**-0.5),
        grid=(blocks,),
        in_specs=[
            SMEM,
            pl.BlockSpec((length, WIDE), lambda i: (0, i)),
            pl.BlockSpec((length, WIDE), lambda i: (0, blocks + i)),
            pl.BlockSpec((length, WIDE), lambda i: (0, 2 * blocks + i)),
            pl.BlockSpec((group, length, length), lambda i: (i, 0, 0)),
            pl.BlockSpec((length, WIDE), lambda i: (0, i)),
            pl.BlockSpec((length, WIDE), lambda i: (0, i)),
            pl.BlockSpec((model, length), lambda i: (0, 0)),
            pl.BlockSpec(prior.shape, lambda i: (0, 0)),
        ],
        out_specs=[
            pl.BlockSpec((length, 3 * model), lambda i: (0, 0)),
            pl.BlockSpec((group, length, length), lambda i: (i, 0, 0)),
            ANY,
            ANY,
        ],
        out_shape=[
            shaped((length, 3 * model), BF),
            shaped((model // size, length, length), BF),
            halves,
            halves,
        ],
        scratch_shapes=[
            pltpu.VMEM((model, 3 * model), BF),
            pltpu.SemaphoreType.DMA((4,)),
        ],
        compiler_params=params(),
        cost_estimate=cost(17),
        name="attend_back",
    )(core, qkv, qkv, qkv, probs, mixed, grad_mixed, turned, prior)


def norm_forward(inputs, gain_vec, shift_vec):
    center = inputs - jnp.mean(inputs, axis=-1, keepdims=True)
    inverse = lax.rsqrt(jnp.mean(center * center, axis=-1, keepdims=True) + EPSILON)
    scaled = center * inverse
    return (scaled * gain_vec + shift_vec, scaled, inverse)


def norm_backward(grad_in, scaled, inverse, gain_vec):
    inner_term = grad_in * gain_vec
    centered = inner_term - jnp.mean(inner_term, axis=-1, keepdims=True)
    return inverse * (centered - scaled * jnp.mean(inner_term * scaled, axis=-1, keepdims=True))


def gelu_pair(u):
    square = jnp.exp(u * u * -0.5)
    t = 1.0 / (1.0 + jnp.abs(u) * (0.3275911 * 0.7071067811865476))
    poly = t * (
        0.254829592
        + t * (-0.284496736 + t * (1.421413741 + t * (-1.453152027 + t * 1.061405429)))
    )
    tail = 0.5 * poly * square
    below = jnp.where(u >= 0.0, 1.0 - tail, tail)
    return u * below, below + u * (square * 0.3989422804014327)


def column_sum(values):
    return jnp.sum(values, axis=0, keepdims=True)


OUT_B, GAIN1, SHIFT1, DOWN_B, GAIN2, SHIFT2 = range(2, 8)


def up_kernel(*refs, out_places, up_places, chunk):
    outs, ups = len(out_places), len(up_places)
    coords_ref, mixed_ref, x_ref, vec_ref, upb_ref = refs[:5]
    out_pieces = refs[5 : 5 + outs]
    up_pieces = refs[5 + outs : 5 + outs + ups]
    (
        n1_ref,
        n1t_ref,
        z1_ref,
        r1_ref,
        hidden_out,
        turned_out,
        slope_out,
        w_out,
        w_up,
        hidden,
        turned,
        slope,
        sem_ref,
        save_sem,
    ) = refs[5 + outs + ups :]
    first = start_fetch(out_pieces, out_places, coords_ref, w_out, sem_ref)
    second = start_fetch(up_pieces, up_places, coords_ref, w_up, sem_ref, outs)

    def vec(row):
        return vec_ref[row : row + 1, :]

    finish(first)
    summed = x_ref[...].astype(F32) + (dg(mixed_ref[...], w_out[...], NN) + vec(OUT_B))
    n1, z1, r1 = norm_forward(summed, vec(GAIN1), vec(SHIFT1))
    low = n1.astype(BF)
    n1_ref[...] = n1
    n1t_ref[...] = low.T
    z1_ref[...] = z1
    r1_ref[...] = r1
    finish(second)
    saves = []
    for index, begin in enumerate(range(0, hidden.shape[1], chunk)):
        cols = slice(begin, begin + chunk)
        h, s = gelu_pair(dg(low, w_up[:, cols], NN) + upb_ref[:, cols])
        h = h.astype(BF)
        hidden[:, cols] = h
        turned[cols, :] = h.T
        slope[:, cols] = s.astype(BF)
        part = pl.ds(begin, chunk)
        for kind, (left, right) in enumerate(
            (
                (hidden.at[:, part], hidden_out.at[:, part]),
                (turned.at[part, :], turned_out.at[part, :]),
                (slope.at[:, part], slope_out.at[:, part]),
            )
        ):
            save = pltpu.make_async_copy(left, right, save_sem.at[index * 3 + kind])
            save.start()
            saves.append(save)
    finish(saves)


def go_up(coords, mixed, tokens, vecs, up_bias, w_out, w_up, chunk=512):
    length, model = tokens.shape
    wide = up_bias.shape[1]
    return pl.pallas_call(
        functools.partial(
            up_kernel, out_places=w_out.places, up_places=w_up.places, chunk=chunk
        ),
        in_specs=[SMEM] + [VMEM] * 4 + [ANY] * (w_out.count + w_up.count),
        out_specs=[VMEM] * 4 + [ANY] * 3,
        out_shape=[
            shaped((length, model), F32),
            shaped((model, length), BF),
            shaped((length, model), F32),
            shaped((length, 1), F32),
            shaped((length, wide), BF),
            shaped((wide, length), BF),
            shaped((length, wide), BF),
        ],
        scratch_shapes=[
            pltpu.VMEM(w_out.shape, BF),
            pltpu.VMEM(w_up.shape, BF),
            pltpu.VMEM((length, wide), BF),
            pltpu.VMEM((wide, length), BF),
            pltpu.VMEM((length, wide), BF),
            pltpu.SemaphoreType.DMA((w_out.count + w_up.count,)),
            pltpu.SemaphoreType.DMA((3 * (wide // chunk),)),
        ],
        compiler_params=params(),
        cost_estimate=cost(14.5),
        name="go_up",
    )(coords, mixed, tokens, vecs, up_bias, *w_out.pieces, *w_up.pieces)


def down_kernel(*refs, places, chunk):
    count = len(places)
    coords_ref, len_ref, n1_ref, cot_ref, vec_ref, hidden_in, turned_in = refs[:7]
    pieces = refs[7 : 7 + count]
    (
        y_ref,
        fb_ref,
        r2_ref,
        sums_ref,
        sent_ref,
        kept_ref,
        w_ref,
        hidden,
        turned,
        product_ref,
        sem_ref,
        own_sem,
    ) = refs[7 + count :]
    load = pltpu.make_async_copy(hidden_in, hidden, own_sem.at[0])
    load.start()
    copies = start_fetch(pieces, places, coords_ref, w_ref, sem_ref)
    load_turned = pltpu.make_async_copy(turned_in, turned, own_sem.at[1])
    load_turned.start()

    def vec(row):
        return vec_ref[row : row + 1, :]

    load.wait()
    finish(copies)
    n2, z2, r2 = norm_forward(
        n1_ref[...] + (dg(hidden[...], w_ref[...], NN) + vec(DOWN_B)), vec(GAIN2), vec(SHIFT2)
    )
    rows = n1_ref.shape[0]
    valid = (iota2((rows, 1), 0) < len_ref[0]).astype(F32)
    y_ref[...] = (n2 * valid).astype(BF)
    g2 = cot_ref[...].astype(F32) * valid
    back = norm_backward(g2, z2, r2, vec(GAIN2))
    r2_ref[...] = back
    fb = back.astype(BF)
    fb_ref[...] = fb
    sums_ref[...] = jnp.concatenate(
        [column_sum(fb.astype(F32)), column_sum(g2 * z2), column_sum(g2)]
        + [jnp.zeros((5, n1_ref.shape[1]), F32)],
        axis=0,
    )
    load_turned.wait()
    saves = []
    for index, begin in enumerate(range(0, turned.shape[0], chunk)):
        part = pl.ds(begin, chunk)
        product_ref[part, :] = dg(turned[part, :], fb, NN).astype(BF)
        saves += save_halves(
            coords_ref, product_ref.at[part], sent_ref.at[part], kept_ref.at[part], own_sem, 2 + 2 * index
        )
    finish(saves)


def go_down(coords, lengths, n1, cotangent, vecs, hidden, turned, weight, chunk=1024):
    length, model = n1.shape
    wide = hidden.shape[1]
    return pl.pallas_call(
        functools.partial(down_kernel, places=weight.places, chunk=chunk),
        in_specs=[SMEM] * 2 + [VMEM] * 3 + [ANY] * (2 + weight.count),
        out_specs=[VMEM] * 4 + [ANY] * 2,
        out_shape=[
            shaped((length, model), BF),
            shaped((length, model), BF),
            shaped((length, model), F32),
            shaped((8, model), F32),
            shaped((wide, model // 2), BF),
            shaped((wide, model // 2), BF),
        ],
        scratch_shapes=[
            pltpu.VMEM(weight.shape, BF),
            pltpu.VMEM((length, wide), BF),
            pltpu.VMEM((wide, length), BF),
            pltpu.VMEM((wide, model), BF),
            pltpu.SemaphoreType.DMA((weight.count,)),
            pltpu.SemaphoreType.DMA((2 + 2 * (wide // chunk),)),
        ],
        compiler_params=params(),
        cost_estimate=cost(16),
        name="go_down",
    )(coords, lengths, n1, cotangent, vecs, hidden, turned, *weight.pieces)


def back_down_kernel(*refs, places, chunk):
    count = len(places)
    coords_ref, fb_ref, n1t_ref, slope_in = refs[:4]
    pieces = refs[4 : 4 + count]
    ub_out, upsum_ref, sent_ref, kept_ref, w_ref, slope, product_ref, sem_ref, own_sem = refs[
        4 + count :
    ]
    load = pltpu.make_async_copy(slope_in, slope, own_sem.at[0])
    copies = start_fetch(pieces, places, coords_ref, w_ref, sem_ref)
    load.start()
    fb = fb_ref[...]
    n1t = n1t_ref[...]
    upsum_ref[...] = jnp.zeros_like(upsum_ref)
    finish(copies)
    load.wait()
    saves = []
    for index, begin in enumerate(range(0, slope.shape[1], chunk)):
        cols = slice(begin, begin + chunk)
        ub = (slope[:, cols].astype(F32) * dg(fb, w_ref[cols, :], NT)).astype(BF)
        slope[:, cols] = ub
        upsum_ref[index : index + 1, :] = column_sum(ub.astype(F32))
        save = pltpu.make_async_copy(
            slope.at[:, pl.ds(begin, chunk)], ub_out.at[:, pl.ds(begin, chunk)], own_sem.at[3 + index]
        )
        save.start()
        saves.append(save)
        product_ref[:, cols] = dg(n1t, ub, NN).astype(BF)
    saves += save_halves(coords_ref, product_ref, sent_ref, kept_ref, own_sem, 1)
    finish(saves)


def back_down(coords, fb, n1t, slope, weight):
    length, model = fb.shape
    wide = slope.shape[1]
    chunk = model
    return pl.pallas_call(
        functools.partial(back_down_kernel, places=weight.places, chunk=chunk),
        in_specs=[SMEM] + [VMEM] * 2 + [ANY] * (1 + weight.count),
        out_specs=[ANY, VMEM, ANY, ANY],
        out_shape=[
            shaped((length, wide), BF),
            shaped((8, model), F32),
            shaped((model, wide // 2), BF),
            shaped((model, wide // 2), BF),
        ],
        scratch_shapes=[
            pltpu.VMEM(weight.shape, BF),
            pltpu.VMEM((length, wide), BF),
            pltpu.VMEM((model, wide), BF),
            pltpu.SemaphoreType.DMA((weight.count,)),
            pltpu.SemaphoreType.DMA((3 + wide // chunk,)),
        ],
        compiler_params=params(),
        cost_estimate=cost(13.5),
        name="back_down",
    )(coords, fb, n1t, slope, *weight.pieces)


def back_up_kernel(*refs, up_places, out_places):
    ups, outs = len(up_places), len(out_places)
    coords_ref, r2_ref, z1_ref, r1_ref, vec_ref, ot_ref, ub_in = refs[:7]
    up_pieces = refs[7 : 7 + ups]
    out_pieces = refs[7 + ups : 7 + ups + outs]
    back_ref, ob_ref, sums_ref, product_ref, w_up, w_out, ub, sem_ref, own_sem = refs[
        7 + ups + outs :
    ]
    load = pltpu.make_async_copy(ub_in, ub, own_sem.at[0])
    load.start()
    second = start_fetch(up_pieces, up_places, coords_ref, w_up, sem_ref)
    first = start_fetch(out_pieces, out_places, coords_ref, w_out, sem_ref, ups)
    load.wait()
    finish(second)
    n1b = r2_ref[...] + dg(ub[...], w_up[...], NT)
    z1 = z1_ref[...]
    back = norm_backward(n1b, z1, r1_ref[...], vec_ref[GAIN1 : GAIN1 + 1, :])
    back_ref[...] = back
    ab = back.astype(BF)
    sums_ref[...] = jnp.concatenate(
        [column_sum(ab.astype(F32)), column_sum(n1b * z1), column_sum(n1b)]
        + [jnp.zeros((5, z1.shape[1]), F32)],
        axis=0,
    )
    finish(first)
    ob_ref[...] = dg(ab, w_out[...], NT).astype(BF)
    product_ref[...] = dg(ot_ref[...], ab, NN).astype(BF)


def back_up(coords, ub, r2, z1, r1, vecs, turned, w_up, w_out):
    length, model = r2.shape
    wide = ub.shape[1]
    return pl.pallas_call(
        functools.partial(back_up_kernel, up_places=w_up.places, out_places=w_out.places),
        in_specs=[SMEM] + [VMEM] * 5 + [ANY] * (1 + w_up.count + w_out.count),
        out_specs=[VMEM] * 4,
        out_shape=[
            shaped((length, model), F32),
            shaped((length, model), BF),
            shaped((8, model), F32),
            shaped((model, model), BF),
        ],
        scratch_shapes=[
            pltpu.VMEM(w_up.shape, BF),
            pltpu.VMEM(w_out.shape, BF),
            pltpu.VMEM((length, wide), BF),
            pltpu.SemaphoreType.DMA((w_up.count + w_out.count,)),
            pltpu.SemaphoreType.DMA((1,)),
        ],
        compiler_params=params(),
        cost_estimate=cost(13.5),
        name="back_up",
    )(coords, r2, z1, r1, vecs, turned, ub, *w_up.pieces, *w_out.pieces)


def inputs_kernel(*refs, places):
    count = len(places)
    coords_ref, pb_ref, back_ref = refs[:3]
    pieces = refs[3 : 3 + count]
    out_ref, sums_ref, w_ref, sem_ref = refs[3 + count :]
    copies = start_fetch(pieces, places, coords_ref, w_ref, sem_ref)
    pb = pb_ref[...]
    flat = column_sum(pb.astype(F32))
    model = out_ref.shape[1]
    sums_ref[...] = jnp.zeros_like(sums_ref)
    for part in range(3):
        sums_ref[part : part + 1, :] = flat[:, part * model : (part + 1) * model]
    finish(copies)
    out_ref[...] = (back_ref[...] + dg(pb, w_ref[...], NT)).astype(BF)


def inputs_grad(coords, grad_packed, back, weight):
    length, model = back.shape
    count = weight.count
    return pl.pallas_call(
        functools.partial(inputs_kernel, places=weight.places),
        in_specs=[SMEM] + [VMEM] * 2 + [ANY] * count,
        out_specs=[VMEM] * 2,
        out_shape=[shaped((length, model), BF), shaped((8, model), F32)],
        scratch_shapes=[
            pltpu.VMEM(weight.shape, BF),
            pltpu.SemaphoreType.DMA((count,)),
        ],
        compiler_params=params(),
        cost_estimate=cost(7),
        name="inputs_grad",
    )(coords, grad_packed, back, *weight.pieces)


def finish_kernel(at_ref, mine_ref, theirs_ref, *out_refs):
    first = at_ref[0] == 0
    begin = 0
    for out_ref in out_refs:
        columns = out_ref.shape[1] // 2
        mine = mine_ref[:, begin : begin + columns]
        theirs = theirs_ref[:, begin : begin + columns]
        out_ref[:, :columns] = jnp.where(first, mine, theirs).astype(F32)
        out_ref[:, columns:] = jnp.where(first, theirs, mine).astype(F32)
        begin += columns


def finish_pair(core, mine, theirs, widths):
    rows, columns = mine.shape
    step = rows // 4 if (rows // 4) % 16 == 0 else rows
    spec = pl.BlockSpec((step, columns), lambda i: (i, 0))
    return pl.pallas_call(
        finish_kernel,
        grid=(rows // step,),
        in_specs=[SMEM, spec, spec],
        out_specs=[pl.BlockSpec((step, width), lambda i: (i, 0)) for width in widths],
        out_shape=[shaped((rows, width), F32) for width in widths],
        compiler_params=params(),
        cost_estimate=cost(4.4),
        name="finish_pair",
    )(core, mine, theirs)


class Axis:
    def __init__(self, name, total, stride, size):
        self.name = name
        self.total = total
        self.stride = stride
        self.size = size
        self.at = (lax.axis_index(name) // stride) % size

    def send(self, value, step):
        pairs = []
        for index in range(self.total):
            place = (index // self.stride) % self.size
            pairs.append((index, index + ((place + step) % self.size - place) * self.stride))
        return lax.ppermute(value, self.name, pairs)

    def peer(self, step):
        return (self.at + step) % self.size


def tie(value, *others):
    if not others:
        return value
    return lax.optimization_barrier((value,) + others)[0]


def take(stack, index, dim=0):
    return lax.dynamic_index_in_dim(stack, index, axis=dim, keepdims=False)


def arrange(axis, block, got, dim=0):
    if axis.size == 1:
        return jnp.expand_dims(block, dim)
    shape = [1] * (block.ndim + 1)
    shape[dim] = axis.size
    place = jnp.arange(axis.size, dtype=jnp.int32).reshape(shape)
    stack = jnp.expand_dims(block, dim)
    for step, value in enumerate(got):
        stack = jnp.where(place == axis.peer(-1 - step), jnp.expand_dims(value, dim), stack)
    return stack


def send_all(axis, block):
    return [axis.send(block, step) for step in range(1, axis.size)]


class Links:
    def __init__(self, dp, fsdp):
        core = 2
        rest = dp // core
        near = 2 if rest % 2 == 0 else 1
        self.core = Axis("dp", dp, 1, core)
        self.near = Axis("dp", dp, core, near)
        self.far = Axis("dp", dp, core * near, rest // near)
        self.pair = Axis("dp", dp, core * near, 2 if (rest // near) % 2 == 0 else 1)
        self.shard = Axis("fsdp", fsdp, 1, fsdp)


class Portion:
    def __init__(self, links, block, begin, count, mate):
        self.links = links
        self.mate = mate
        self.begin = begin
        self.rows = block.shape[0]
        parts = links.core.size * (mate.size if mate else 1)
        self.unit = count // parts
        self.mine = lax.dynamic_slice_in_dim(
            block, begin + self.spot(0, 0) * self.unit, self.unit, 0
        )

    def spot(self, s, t):
        core = self.links.core.peer(-s)
        return core * self.mate.size + self.mate.peer(-t) if self.mate else core

    def start(self, *after):
        self.mine = tie(self.mine, *after)
        self.got = send_all(self.links.shard, self.mine)
        return self.mine

    def hop(self, *after):
        core = self.links.core
        got = [tie(item, *after) for item in self.got]
        self.hops = [send_all(self.mate, item) for item in got] if self.mate else [[]] * len(got)
        self.across = [send_all(core, item) for item in got]
        self.got = got
        return got[0]

    def last(self, *after):
        core = self.links.core
        self.hops = [[tie(item, *after) for item in group] for group in self.hops]
        self.crossed = [[send_all(core, item) for item in group] for group in self.hops]
        return self.hops[0][0] if self.mate else self.got[0]

    def pieces(self):
        shard = self.links.shard
        which = None if self.mate is None else 1 if self.mate is self.links.near else 2
        found = []
        for index, item in enumerate(self.got):

            def add(value, s, t):
                place = Place(
                    self.rows, shard.size, self.begin, -1 - index, self.unit, -s, -t, which
                )
                found.append((value, place))

            add(item, 0, 0)
            for t, value in enumerate(self.hops[index]):
                add(value, 0, t + 1)
            for s, value in enumerate(self.across[index]):
                add(value, s + 1, 0)
            for t, group in enumerate(self.crossed[index]):
                for s, value in enumerate(group):
                    add(value, s + 1, t + 1)
        return found


class Fetch:
    def __init__(self, links, block):
        self.links = links
        self.block = block
        rows = block.shape[0]
        mates = (links.near, links.pair)
        if rows % 128 == 0 and all(mate.size == 2 for mate in mates):
            half = rows // 2
            self.parts = [
                Portion(links, block, index * half, half, mate) for index, mate in enumerate(mates)
            ]
        else:
            self.parts = [Portion(links, block, 0, rows, None)]

    def start(self, *after):
        return [part.start(*after) for part in self.parts]

    def hop(self, *after):
        return [part.hop(*after) for part in self.parts]

    def last(self, *after):
        return [part.last(*after) for part in self.parts]

    def weight(self):
        rows, columns = self.block.shape
        blocks = self.links.shard.size
        found = [(self.block, Place(rows, blocks))]
        for part in self.parts:
            found += part.pieces()
        return Weight(
            [item for item, _ in found], [place for _, place in found], (rows * blocks, columns)
        )


def add_up(terms):
    total = terms[0].astype(F32)
    for term in terms[1:]:
        total = total + term.astype(F32)
    return total


class Chain:
    def __init__(self, links, sent, kept, orders, line):
        self.links = links
        self.sent = sent
        self.kept = kept
        self.orders = orders
        self.line = line and links.far.size == 4
        rows, columns = kept.shape
        sizes = (links.shard.size, links.near.size, links.far.size, len(orders))
        whole = sizes[0] * sizes[1] * sizes[2] * sizes[3]
        self.shape = sizes + (rows // whole, columns)

    def cross(self, *after):
        sent = tie(self.sent, *after)
        self.other = self.links.core.send(sent, 1)
        return [sent]

    def hop(self, terms, axis, dim):
        sent = []
        for step in range(1, axis.size):
            pieces = [take(term, axis.peer(step), dim) for term in terms]
            sent.append(lax.optimization_barrier(add_up(pieces).astype(BF)))
        got = [axis.send(value, step + 1) for step, value in enumerate(sent)]
        return [take(term, axis.at, dim) for term in terms] + got, sent

    def scatter(self, order, terms, first):
        shard, near = self.links.shard, self.links.near
        if order == "shard":
            return self.hop(terms, shard, 0) if first else self.hop(terms, near, 0)
        return self.hop(terms, near, 1) if first else self.hop(terms, shard, 0)

    def first(self, *after):
        other = tie(self.other, *after).reshape(self.shape)
        kept = self.kept.reshape(self.shape)
        self.ways = []
        token = []
        for index, order in enumerate(self.orders):
            terms, sent = self.scatter(order, [term[:, :, :, index] for term in (kept, other)], True)
            self.ways.append(terms)
            token += sent
        return token

    def second(self, *after):
        token = []
        for index, order in enumerate(self.orders):
            terms = self.ways[index]
            terms = terms[:-1] + [tie(terms[-1], *after)]
            self.ways[index], sent = self.scatter(order, terms, False)
            token += sent
        return token

    def far_sum(self, *after):
        ways = [add_up(way[:-1] + [tie(way[-1], *after)]) for way in self.ways]
        return lax.optimization_barrier(jnp.stack(ways, axis=1).astype(BF))

    def third(self, *after):
        self.block = self.far_sum(*after)
        if self.line:
            self.got = self.line_send(self.block, ((0, 1), (3, 2)))
            return [self.block]
        self.terms, sent = self.hop([self.block], self.links.far, 0)
        return sent

    def line_send(self, value, moves):
        far = self.links.far
        pairs = []
        for index in range(far.total):
            place = (index // far.stride) % far.size
            pairs += [(index, index + (to - place) * far.stride) for at, to in moves if at == place]
        return lax.ppermute(value, far.name, pairs)

    def middle(self, *after):
        if not self.line:
            return list(after)
        got = tie(self.got, *after)
        self.block = lax.optimization_barrier(add_up([self.block, got]).astype(BF))
        self.got = self.line_send(self.block, ((1, 2), (2, 1)))
        return [self.block]

    def fourth(self, *after):
        if self.line:
            got = tie(self.got, *after)
            self.block = lax.optimization_barrier(add_up([self.block, got]).astype(BF))
            self.got = self.line_send(self.block, ((1, 0), (2, 3)))
            return [self.block]
        terms = self.terms[:-1] + [tie(self.terms[-1], *after)]
        self.block = lax.optimization_barrier(add_up(terms).astype(BF))
        self.got = send_all(self.links.far, self.block)
        return [self.block]

    def fifth(self, *after):
        far = self.links.far
        if self.line:
            outer = (far.at == 0) | (far.at == 3)
            block = jnp.where(outer, tie(self.got, *after), self.block)
        else:
            got = self.got
            block = arrange(far, self.block, got[:-1] + [tie(got[-1], *after)])
        self.block = lax.optimization_barrier(block)
        self.got = send_all(self.links.near, self.block)
        return [self.block]

    def sixth(self, *after):
        got = self.got
        block = arrange(self.links.near, self.block, got[:-1] + [tie(got[-1], *after)])
        self.block = lax.optimization_barrier(block.reshape(-1, block.shape[-1]))
        self.got = self.links.core.send(self.block, 1)
        return [self.block]

    def done(self, widths, *after):
        return finish_pair(
            self.links.coords, self.block, tie(self.got, *after), widths
        )


class Sums:
    def __init__(self, links, value):
        self.links = links
        self.total = value

    def step(self, name, *after):
        axis = getattr(self.links, name)
        total = tie(self.total, *after)
        self.total = functools.reduce(jnp.add, send_all(axis, total), total)
        return [total]


def per_device(
    dp,
    fsdp,
    tokens,
    lengths,
    buckets,
    qkv_weight,
    q_bias,
    v_bias,
    out_weight,
    out_bias,
    bias_table,
    norm1_gain,
    norm1_bias,
    up_weight,
    up_bias,
    down_weight,
    down_bias,
    norm2_gain,
    norm2_bias,
    cotangent,
):
    links = Links(dp, fsdp)
    model = tokens.shape[1]
    wide = up_weight.shape[1]
    heads = bias_table.shape[1]
    size = model // heads
    entries = bias_table.shape[0] * fsdp
    links.coords = coords = jnp.stack(
        [links.core.at, links.near.at, links.pair.at, links.shard.at]
    ).astype(jnp.int32)

    table_got = send_all(links.shard, bias_table)
    qkv, out, up, down = [
        Fetch(links, item) for item in (qkv_weight, out_weight, up_weight, down_weight)
    ]
    token = qkv.start(bias_table)
    narrow = (q_bias, v_bias, out_bias, norm1_gain, norm1_bias, down_bias, norm2_gain, norm2_bias)
    narrow = lax.optimization_barrier(narrow + tuple(token))[:8]
    row = jnp.arange(8, dtype=jnp.int32)[:, None]
    rows = jnp.broadcast_to(narrow[0][None], (8, narrow[0].size))
    for index in range(1, 8):
        rows = jnp.where(row == index, narrow[index][None], rows)
    rows = lax.optimization_barrier(rows)
    rows_got = send_all(links.shard, rows)
    up_bias_in = tie(up_bias, rows)
    up_got = send_all(links.shard, up_bias_in)
    table = arrange(links.shard, bias_table, table_got).reshape(entries, heads)
    bias = bias_scores(tie(buckets, up_bias_in), lengths, table, 0, 2)
    token = qkv.hop(bias[1])
    token = out.start(*token) + up.start(*token)
    bias = bias_scores(tie(buckets, *token), lengths, table, 1, 2, bias)
    token = qkv.last(bias[1])
    token = out.hop(*token) + up.hop(*token)
    token = down.start(*token)
    bias, ids = bias
    vecs = jnp.swapaxes(arrange(links.shard, rows, rows_got), 0, 1).reshape(8, model).astype(F32)
    up_vec = arrange(links.shard, up_bias, up_got).reshape(1, -1).astype(F32)
    shift_row = jnp.concatenate([vecs[0:1], jnp.zeros((1, model), F32), vecs[1:2]], axis=1)
    shift_row = tie(shift_row, up_vec, *token)
    w_qkv = qkv.weight()
    half = model // WIDE // 2
    packed, probs, mixed, mixed_t, tokens_t = attend_first(
        coords, tokens, shift_row, w_qkv, bias, size, half
    )
    token = out.last(mixed_t) + up.last(mixed_t)
    probs, mixed, mixed_t = attend_rest(
        packed, bias, tie(probs, *token), mixed, mixed_t, size, half
    )
    token = down.hop(mixed_t)
    w_out = out.weight()
    w_up = up.weight()
    n1, n1t, z1, r1, hidden, hidden_t, slope = go_up(
        coords, tie(mixed, *token), tokens, vecs, up_vec, w_out, w_up
    )
    token = down.last(r1)
    w_down = down.weight()
    output, fb, r2, sums_two, sent, kept = go_down(
        coords, lengths, tie(n1, *token), cotangent, vecs, hidden, hidden_t, w_down
    )

    both = ("shard", "near")
    chain_down = Chain(links, sent, kept, both, False)
    token = chain_down.cross()
    ub, up_sum, sent, kept = back_down(coords, tie(fb, *token), n1t, slope, w_down)
    chain_up = Chain(links, sent, kept, both, False)
    token = chain_down.first(ub)
    token = chain_up.cross(*token)
    back, ob, sums_one, out_product = back_up(
        coords, tie(ub, *token), r2, z1, r1, vecs, mixed_t, w_up, w_out
    )
    token = chain_down.second(sums_one)
    token = chain_up.first(*token)
    grad_packed, grad_scores, sent, kept = attend_back(
        coords, packed, probs, mixed, tie(ob, *token), tokens_t, out_product, size
    )
    chain_qkv = Chain(links, sent, kept, both, False)
    token = chain_down.third(grad_packed)
    token = chain_up.second(*token)
    token = chain_qkv.cross(*token)
    table_one = table_grad(ids, tie(grad_scores, *token), entries, 0, 2)
    token = chain_down.fourth(table_one)
    token = chain_up.third(*token)
    token = chain_qkv.first(*token)
    tokens_grad, packed_sums = inputs_grad(coords, tie(grad_packed, *token), back, w_qkv)
    table_two = table_grad(ids, tie(grad_scores, packed_sums), entries, 1, 2)
    table_sum = table_one + table_two
    sums = Sums(
        links,
        jnp.concatenate(
            [
                sums_one,
                sums_two,
                up_sum,
                packed_sums,
                jnp.pad(table_sum, ((0, 0), (0, model - entries))),
            ],
            axis=0,
        ),
    )
    token = chain_qkv.second(table_two)
    token = chain_down.fifth(*token)
    token = chain_up.fourth(*token)
    token = sums.step("shard", *token)
    token = chain_qkv.third(*token)
    token = chain_down.sixth(*token)
    token = chain_up.fifth(*token)
    token = sums.step("core", *token)
    (g_down,) = chain_down.done((model,), *token)
    token = sums.step("near", g_down)
    token = chain_qkv.fourth(*token)
    token = chain_up.sixth(*token)
    token = sums.step("far", *token)
    (g_up,) = chain_up.done((wide,), sums.total, *token)
    token = chain_qkv.fifth(g_up)
    token = chain_qkv.sixth(*token)
    g_out, g_qkv = chain_qkv.done((model, 3 * model), *token)

    total = sums.total
    part = model // fsdp
    place = links.shard.at

    def piece(row):
        return lax.dynamic_slice(total, (row, place * part), (1, part)).reshape(part)

    g_out_bias, g_gain_one, g_shift_one = [piece(row) for row in range(3)]
    g_down_bias, g_gain_two, g_shift_two = [piece(row) for row in range(8, 11)]
    up_flat = total[16 : 16 + wide // model].reshape(wide)
    g_up_bias = lax.dynamic_slice_in_dim(up_flat, place * up_bias.size, up_bias.size)
    g_query_bias = piece(24)
    g_value_bias = piece(26)
    g_table = lax.dynamic_slice(
        total, (32, place * bias_table.shape[0]), (heads, bias_table.shape[0])
    ).T
    return (
        output,
        tokens_grad,
        g_qkv,
        g_query_bias,
        g_value_bias,
        g_out,
        g_out_bias,
        g_table,
        g_gain_one,
        g_shift_one,
        g_up,
        g_up_bias,
        g_down,
        g_down_bias,
        g_gain_two,
        g_shift_two,
    )


def solution(mesh):
    rows = P(("dp", "fsdp"), None)
    mat = P("fsdp", None)
    vec = P("fsdp")
    return jax.shard_map(
        functools.partial(per_device, mesh.shape["dp"], mesh.shape["fsdp"]),
        mesh=mesh,
        in_specs=(
            rows,
            P(("dp", "fsdp")),
            P(("dp", "fsdp"), None, None, None),
            mat,
            vec,
            vec,
            mat,
            vec,
            mat,
            vec,
            vec,
            mat,
            vec,
            mat,
            vec,
            vec,
            vec,
            rows,
        ),
        out_specs=(
            rows,
            rows,
            mat,
            vec,
            vec,
            mat,
            vec,
            mat,
            vec,
            vec,
            mat,
            vec,
            mat,
            vec,
            vec,
            vec,
        ),
        check_vma=False,
    )
```

```python
import functools

import jax
import jax.numpy as jnp
from jax import lax
from jax.experimental import pallas as pl
from jax.experimental.pallas import tpu as pltpu
from jax.sharding import PartitionSpec as P

EPSILON = 1e-05
MASKED = -1000000000.0
BF = jnp.bfloat16
F32 = jnp.float32
NN = (((1,), (0,)), ((), ()))
NT = (((1,), (1,)), ((), ()))
TN = (((0,), (0,)), ((), ()))
WIDE = 128
ANY = pl.BlockSpec(memory_space=pl.ANY)
SMEM = pl.BlockSpec(memory_space=pltpu.SMEM)
VMEM = pl.BlockSpec(memory_space=pltpu.VMEM)


def dg(left, right, dims):
    return lax.dot_general(left, right, dims, preferred_element_type=F32)


def params(mebibytes):
    return pltpu.CompilerParams(vmem_limit_bytes=mebibytes * 2**20)


def cost(micros):
    return pl.CostEstimate(flops=0, bytes_accessed=int(micros * 3e6), transcendentals=0)


def shaped(shape, dtype):
    return jax.ShapeDtypeStruct(shape, dtype)


def onehot_rows(ids, oh_ref, bucket_count):
    length = ids[0].shape[1]
    sub = lax.broadcasted_iota(jnp.int32, (16, length), 0)
    one = jnp.ones((16, length), BF)
    zero = jnp.zeros((16, length), BF)
    half = bucket_count // 2
    for kind in range(3):
        both = jnp.concatenate([ids[kind], ids[kind]], axis=0).astype(BF)
        for pair in range(half):
            level = jnp.where(sub < 8, 2 * pair, 2 * pair + 1).astype(F32).astype(BF)
            oh_ref[pl.ds((kind * half + pair) * 16, 16), :] = jnp.where(both == level, one, zero)


def iota2(shape, dim):
    return lax.broadcasted_iota(jnp.int32, shape, dim)


def bias_kernel(len_ref, ids_ref, table_ref, *rest, first):
    out_ref, turned_ref, spread_ref, held_ref, oh_ref = rest[-5:]
    step0 = pl.program_id(0)
    block = step0 + first
    heads, rows, length = out_ref.shape
    entries = table_ref.shape[0]
    valid = len_ref[0]

    @pl.when(step0 == 0)
    def _():
        pick_head = (iota2((heads * 8, heads), 0) >> 3) == iota2((heads * 8, heads), 1)
        rows_of = dg(pick_head.astype(F32).astype(BF), table_ref[...], NT).astype(BF)
        shape = (entries, entries * 8)
        pick_entry = iota2(shape, 0) == (iota2(shape, 1) >> 3)
        wide = dg(rows_of, pick_entry.astype(F32).astype(BF), NN)
        shape = (heads * 8, entries * 8)
        same = (iota2(shape, 0) & 7) == (iota2(shape, 1) & 7)
        spread_ref[...] = jnp.where(same, wide, 0.0).astype(BF)

    for kind in range(3):
        turned = ids_ref[0, kind].astype(F32).T
        held_ref[kind] = turned
        turned_ref[kind] = turned.astype(BF)

    def body(step, carry):
        parts = []
        for u in range(2):
            group = pl.ds(pl.multiple_of(step * 16 + u * 8, 8), 8)
            onehot_rows([held_ref[kind, group, :] for kind in range(3)], oh_ref.at[u], entries // 3)
            parts.append(dg(spread_ref[...], oh_ref[u], NN).reshape(heads, 8, length))
        bias = jnp.concatenate(parts, axis=1)
        key = iota2((1, 16, length), 1) + (block * rows + step * 16)
        out_ref[:, pl.ds(pl.multiple_of(step * 16, 16), 16), :] = jnp.where(
            key < valid, bias, MASKED
        ).astype(BF)
        return carry

    lax.fori_loop(0, rows // 16, body, 0, unroll=4)


def bias_scores(buckets, valid, table, first, steps, before=None, rows=128):
    length = buckets.shape[-1]
    entries, heads = table.shape
    held = () if before is None else tuple(before)
    return pl.pallas_call(
        functools.partial(bias_kernel, first=first),
        grid=(steps,),
        in_specs=[
            SMEM,
            pl.BlockSpec((1, 3, length, rows), lambda i: (0, 0, 0, first + i)),
            pl.BlockSpec((entries, heads), lambda i: (0, 0)),
        ]
        + [ANY] * len(held),
        out_specs=[
            pl.BlockSpec((heads, rows, length), lambda i: (0, first + i, 0)),
            pl.BlockSpec((3, rows, length), lambda i: (0, first + i, 0)),
        ],
        out_shape=[shaped((heads, length, length), BF), shaped((3, length, length), BF)],
        scratch_shapes=[
            pltpu.VMEM((heads * 8, entries * 8), BF),
            pltpu.VMEM((3, rows, length), F32),
            pltpu.VMEM((2, entries * 8, length), BF),
        ],
        input_output_aliases={3: 0, 4: 1} if held else {},
        compiler_params=params(56),
        cost_estimate=cost(8),
        name="bias_scores",
    )(valid, buckets, table, *held)


def table_kernel(ids_ref, grad_ref, out_ref, acc_ref, oh_ref):
    heads, rows, length = grad_ref.shape
    entries = out_ref.shape[1]

    @pl.when(pl.program_id(0) == 0)
    def _():
        acc_ref[...] = jnp.zeros_like(acc_ref)

    def body(step, carry):
        tile = pl.ds(pl.multiple_of(step * 16, 16), 16)
        grads = grad_ref[:, tile, :].astype(F32)
        ids = [ids_ref[kind, tile, :].astype(F32) for kind in range(3)]
        total = None
        for u in range(2):
            part = slice(u * 8, (u + 1) * 8)
            onehot_rows([item[part] for item in ids], oh_ref.at[u], entries // 3)
            part = dg(oh_ref[u], grads[:, part, :].reshape(heads * 8, length).astype(BF), NT)
            total = part if total is None else total + part
        acc_ref[...] += total
        return carry

    lax.fori_loop(0, rows // 16, body, 0, unroll=4)

    @pl.when(pl.program_id(0) == pl.num_programs(0) - 1)
    def _():
        shape = acc_ref.shape
        same = (iota2(shape, 0) & 7) == (iota2(shape, 1) & 7)
        kept = jnp.where(same, acc_ref[...], 0.0)
        rows_in = kept.reshape(entries, 8, heads * 8).sum(axis=1)
        shape = (out_ref.shape[0], heads * 8)
        fold = (iota2(shape, 0) == (iota2(shape, 1) >> 3)).astype(F32)
        out_ref[...] = lax.dot_general(
            fold, rows_in, NT, precision=lax.Precision.HIGHEST, preferred_element_type=F32
        )


def table_grad(ids, grads, entries, part, parts, rows=64):
    heads, length, _ = grads.shape
    padded = -(-heads // 8) * 8
    steps = length // rows // parts
    first = part * steps
    return pl.pallas_call(
        table_kernel,
        grid=(steps,),
        in_specs=[
            pl.BlockSpec((3, rows, length), lambda i: (0, first + i, 0)),
            pl.BlockSpec((heads, rows, length), lambda i: (0, first + i, 0)),
        ],
        out_specs=pl.BlockSpec((padded, entries), lambda i: (0, 0)),
        out_shape=shaped((padded, entries), F32),
        scratch_shapes=[
            pltpu.VMEM((entries * 8, heads * 8), F32),
            pltpu.VMEM((2, entries * 8, length), BF),
        ],
        compiler_params=params(56),
        cost_estimate=cost(9.5),
        name="table_grad",
    )(ids, grads)


class Place:
    def __init__(
        self, rows, blocks, begin=0, shard=0, unit=0, core=0, mate=0, which=None, columns=None
    ):
        self.rows = rows
        self.blocks = blocks
        self.begin = begin
        self.shard = shard
        self.unit = unit
        self.core = core
        self.mate = mate
        self.which = which
        self.columns = columns

    def row(self, coords_ref):
        def at(index, step, size):
            return lax.rem(coords_ref[index] + step % size, size)

        row = at(3, self.shard, self.blocks) * self.rows + self.begin
        if not self.unit:
            return row
        spot = at(0, self.core, 2)
        if self.which is not None:
            spot = spot * 2 + at(self.which, self.mate, 2)
        return row + spot * self.unit


class Weight:
    def __init__(self, pieces, places, shape):
        self.pieces = pieces
        self.places = places
        self.shape = shape
        self.count = len(pieces)


def start_fetch(refs, places, coords_ref, whole_ref, sem_ref, first=0):
    copies = []
    for index, ref in enumerate(refs):
        begin = pl.multiple_of(places[index].row(coords_ref), 16)
        target = whole_ref.at[pl.ds(begin, ref.shape[0])]
        if places[index].columns is not None:
            ref = ref.at[:, pl.ds(places[index].columns, whole_ref.shape[1])]
        copy = pltpu.make_async_copy(ref, target, sem_ref.at[first + index])
        copy.start()
        copies.append(copy)
    return copies


def finish(copies):
    for copy in copies:
        copy.wait()


def save_halves(core_ref, whole_ref, sent_ref, kept_ref, sem_ref, first, begin=0):
    columns = whole_ref.shape[1] // 2
    mine = core_ref[0]
    copies = []
    for index, (half, ref) in enumerate(((1 - mine, sent_ref), (mine, kept_ref))):
        cols = pl.ds(pl.multiple_of(half * columns, WIDE), columns)
        copy = pltpu.make_async_copy(
            whole_ref.at[:, cols], ref.at[:, pl.ds(begin, columns)], sem_ref.at[first + index]
        )
        copy.start()
        copies.append(copy)
    return copies


def attend_pair(q, k, v, bias_ref, p_ref, o_ref, ot_ref, size):
    width = q.shape[1]
    lane = iota2((1, width), 1)
    vt = v.T
    mixed = []
    for g in range(width // size):
        mine = (lane >= g * size) & (lane < (g + 1) * size)
        scores = dg(jnp.where(mine, k, jnp.zeros_like(k)), q, NT) + bias_ref[g].astype(F32)
        top = jnp.max(scores, axis=0, keepdims=True)
        shifted = jnp.exp(scores - top)
        norm = jnp.sum(shifted, axis=0, keepdims=True)
        probs = (shifted * (1.0 / norm)).astype(BF)
        p_ref[g] = probs
        mixed.append(dg(vt[g * size : (g + 1) * size], probs, NN))
    turned = jnp.concatenate(mixed, axis=0)
    ot_ref[...] = turned.astype(BF)
    o_ref[...] = turned.T.astype(BF)


def attend_first_kernel(*refs, size, places, factor):
    count = len(places)
    coords_ref, x_ref, shift_ref, bias_ref = refs[:4]
    pieces = refs[4 : 4 + count]
    qkv_ref, p_ref, o_ref, ot_ref, xt_ref, w_ref, sem_ref = refs[4 + count :]
    pair = pl.program_id(0)
    model = x_ref.shape[1]
    width = o_ref.shape[1]

    @pl.when(pair == 0)
    def _():
        copies = start_fetch(pieces, places, coords_ref, w_ref, sem_ref)
        xt_ref[...] = x_ref[...].T
        finish(copies)
        for part in range(3):
            cols = slice(part * model, (part + 1) * model)
            value = dg(x_ref[...], w_ref[:, cols], NN) + shift_ref[:, cols]
            if part == 0:
                value = value * factor
            qkv_ref[:, cols] = value.astype(BF)

    def block(part):
        return qkv_ref[:, pl.ds(pl.multiple_of(part * model + pair * width, width), width)]

    attend_pair(block(0), block(1), block(2), bias_ref, p_ref, o_ref, ot_ref, size)


def attend_rest_kernel(q_ref, k_ref, v_ref, bias_ref, _p, _o, _ot, p_ref, o_ref, ot_ref, *, size):
    attend_pair(q_ref[...], k_ref[...], v_ref[...], bias_ref, p_ref, o_ref, ot_ref, size)


def attend_first(coords, tokens, shift_row, weight, bias, size, steps):
    length, model = tokens.shape
    group = WIDE // size
    count = weight.count
    return pl.pallas_call(
        functools.partial(
            attend_first_kernel, size=size, places=weight.places, factor=size**-0.5
        ),
        grid=(steps,),
        in_specs=[
            SMEM,
            pl.BlockSpec((length, model), lambda i: (0, 0)),
            pl.BlockSpec((1, 3 * model), lambda i: (0, 0)),
            pl.BlockSpec((group, length, length), lambda i: (i, 0, 0)),
        ]
        + [ANY] * count,
        out_specs=[
            pl.BlockSpec((length, 3 * model), lambda i: (0, 0)),
            pl.BlockSpec((group, length, length), lambda i: (i, 0, 0)),
            pl.BlockSpec((length, WIDE), lambda i: (0, i)),
            pl.BlockSpec((WIDE, length), lambda i: (i, 0)),
            pl.BlockSpec((model, length), lambda i: (0, 0)),
        ],
        out_shape=[
            shaped((length, 3 * model), BF),
            shaped((model // size, length, length), BF),
            shaped((length, model), BF),
            shaped((model, length), BF),
            shaped((model, length), BF),
        ],
        scratch_shapes=[pltpu.VMEM(weight.shape, BF), pltpu.SemaphoreType.DMA((count,))],
        compiler_params=params(56),
        cost_estimate=cost(11.5),
        name="attend_first",
    )(coords, tokens, shift_row, bias, *weight.pieces)


def attend_rest(qkv, bias, probs, mixed, turned, size, first):
    length, model = mixed.shape
    group = WIDE // size
    blocks = model // WIDE
    return pl.pallas_call(
        functools.partial(attend_rest_kernel, size=size),
        grid=(blocks - first,),
        in_specs=[
            pl.BlockSpec((length, WIDE), lambda i: (0, first + i)),
            pl.BlockSpec((length, WIDE), lambda i: (0, blocks + first + i)),
            pl.BlockSpec((length, WIDE), lambda i: (0, 2 * blocks + first + i)),
            pl.BlockSpec((group, length, length), lambda i: (first + i, 0, 0)),
            ANY,
            ANY,
            ANY,
        ],
        out_specs=[
            pl.BlockSpec((group, length, length), lambda i: (first + i, 0, 0)),
            pl.BlockSpec((length, WIDE), lambda i: (0, first + i)),
            pl.BlockSpec((WIDE, length), lambda i: (first + i, 0)),
        ],
        out_shape=[
            shaped(probs.shape, BF),
            shaped(mixed.shape, BF),
            shaped(turned.shape, BF),
        ],
        input_output_aliases={4: 0, 5: 1, 6: 2},
        compiler_params=params(56),
        cost_estimate=cost(7),
        name="attend_rest",
    )(qkv, qkv, qkv, bias, probs, mixed, turned)


def attend_back_kernel(
    core_ref,
    q_ref,
    k_ref,
    v_ref,
    p_ref,
    o_ref,
    g_ref,
    xt_ref,
    prior_ref,
    out_ref,
    ds_ref,
    sent_ref,
    kept_ref,
    product_ref,
    sem_ref,
    *,
    size,
    factor,
):
    pair = pl.program_id(0)
    width = q_ref.shape[1]
    model = out_ref.shape[1] // 3
    count = width // size
    lane = iota2((1, width), 1)
    q = q_ref[...]
    v = v_ref[...]
    ob = g_ref[...]
    kt = k_ref[...].T
    product = o_ref[...].astype(F32) * ob.astype(F32)
    qs, ks, vs = [], [], []
    for g in range(count):
        mine = (lane >= g * size) & (lane < (g + 1) * size)
        spare = ((g + 1) % count) * size
        inner = jnp.sum(jnp.where(mine, product, 0.0), axis=1, keepdims=True)
        high = inner.astype(BF).astype(F32)
        extra = jnp.where(lane == spare, high, jnp.where(lane == spare + 1, inner - high, 0.0))
        minus = jnp.where((lane == spare) | (lane == spare + 1), -1.0, 0.0)
        left = jnp.where(mine, v, minus.astype(BF))
        right = jnp.where(mine, ob, extra.astype(BF))
        probs = p_ref[g]
        ds = (probs.astype(F32) * dg(left, right, NT)).astype(BF)
        ds_ref[g] = ds
        vs.append(dg(probs, ob, NN))
        ks.append(dg(ds, q, NN))
        qs.append(dg(kt[g * size : (g + 1) * size], ds, NN))

    def pick(items):
        chosen = items[0]
        for g in range(1, count):
            chosen = jnp.where(lane >= g * size, items[g], chosen)
        return chosen

    def place(start):
        return pl.ds(pl.multiple_of(start + pair * width, width), width)

    q_grad = jnp.concatenate(qs, axis=0).T.astype(BF).astype(F32) * factor
    out_ref[:, place(0)] = q_grad.astype(BF)
    out_ref[:, place(model)] = pick(ks).astype(BF)
    out_ref[:, place(2 * model)] = pick(vs).astype(BF)

    @pl.when(pair == pl.num_programs(0) - 1)
    def _():
        begin = prior_ref.shape[1] // 2
        copies = save_halves(core_ref, prior_ref, sent_ref, kept_ref, sem_ref, 0)
        for part in range(3):
            cols = slice(part * model, (part + 1) * model)
            product_ref[:, cols] = dg(xt_ref[...], out_ref[:, cols], NN).astype(BF)
        copies += save_halves(core_ref, product_ref, sent_ref, kept_ref, sem_ref, 2, begin)
        finish(copies)


def attend_back(core, qkv, probs, mixed, grad_mixed, turned, prior, size):
    length = qkv.shape[0]
    model = qkv.shape[1] // 3
    blocks = model // WIDE
    group = WIDE // size
    halves = shaped((model, (prior.shape[1] + 3 * model) // 2), BF)
    return pl.pallas_call(
        functools.partial(attend_back_kernel, size=size, factor=size**-0.5),
        grid=(blocks,),
        in_specs=[
            SMEM,
            pl.BlockSpec((length, WIDE), lambda i: (0, i)),
            pl.BlockSpec((length, WIDE), lambda i: (0, blocks + i)),
            pl.BlockSpec((length, WIDE), lambda i: (0, 2 * blocks + i)),
            pl.BlockSpec((group, length, length), lambda i: (i, 0, 0)),
            pl.BlockSpec((length, WIDE), lambda i: (0, i)),
            pl.BlockSpec((length, WIDE), lambda i: (0, i)),
            pl.BlockSpec((model, length), lambda i: (0, 0)),
            pl.BlockSpec(prior.shape, lambda i: (0, 0)),
        ],
        out_specs=[
            pl.BlockSpec((length, 3 * model), lambda i: (0, 0)),
            pl.BlockSpec((group, length, length), lambda i: (i, 0, 0)),
            ANY,
            ANY,
        ],
        out_shape=[
            shaped((length, 3 * model), BF),
            shaped((model // size, length, length), BF),
            halves,
            halves,
        ],
        scratch_shapes=[
            pltpu.VMEM((model, 3 * model), BF),
            pltpu.SemaphoreType.DMA((4,)),
        ],
        compiler_params=params(30),
        cost_estimate=cost(17),
        name="attend_back",
    )(core, qkv, qkv, qkv, probs, mixed, grad_mixed, turned, prior)


def norm_forward(inputs, gain_vec, shift_vec):
    center = inputs - jnp.mean(inputs, axis=-1, keepdims=True)
    inverse = lax.rsqrt(jnp.mean(center * center, axis=-1, keepdims=True) + EPSILON)
    scaled = center * inverse
    return (scaled * gain_vec + shift_vec, scaled, inverse)


def norm_backward(grad_in, scaled, inverse, gain_vec):
    inner_term = grad_in * gain_vec
    centered = inner_term - jnp.mean(inner_term, axis=-1, keepdims=True)
    return inverse * (centered - scaled * jnp.mean(inner_term * scaled, axis=-1, keepdims=True))


def gelu_pair(u):
    square = jnp.exp(u * u * -0.5)
    t = 1.0 / (1.0 + jnp.abs(u) * (0.3275911 * 0.7071067811865476))
    poly = t * (
        0.254829592
        + t * (-0.284496736 + t * (1.421413741 + t * (-1.453152027 + t * 1.061405429)))
    )
    tail = 0.5 * poly * square
    below = jnp.where(u >= 0.0, 1.0 - tail, tail)
    return u * below, below + u * (square * 0.3989422804014327)


def column_sum(values):
    return jnp.sum(values, axis=0, keepdims=True)


OUT_B, GAIN1, SHIFT1, DOWN_B, GAIN2, SHIFT2 = range(2, 8)


def up_kernel(*refs, out_places, up_places, chunk):
    outs, ups = len(out_places), len(up_places)
    coords_ref, mixed_ref, x_ref, vec_ref, upb_ref = refs[:5]
    out_pieces = refs[5 : 5 + outs]
    up_pieces = refs[5 + outs : 5 + outs + ups]
    (
        n1_ref,
        n1t_ref,
        z1_ref,
        r1_ref,
        hidden_out,
        turned_out,
        slope_out,
        w_out,
        w_up,
        hidden,
        turned,
        slope,
        sem_ref,
        save_sem,
    ) = refs[5 + outs + ups :]
    first = start_fetch(out_pieces, out_places, coords_ref, w_out, sem_ref)
    second = start_fetch(up_pieces, up_places, coords_ref, w_up, sem_ref, outs)

    def vec(row):
        return vec_ref[row : row + 1, :]

    finish(first)
    summed = x_ref[...].astype(F32) + (dg(mixed_ref[...], w_out[...], NN) + vec(OUT_B))
    n1, z1, r1 = norm_forward(summed, vec(GAIN1), vec(SHIFT1))
    low = n1.astype(BF)
    n1_ref[...] = n1
    n1t_ref[...] = low.T
    z1_ref[...] = z1
    r1_ref[...] = r1
    finish(second)
    saves = []
    for index, begin in enumerate(range(0, hidden.shape[1], chunk)):
        cols = slice(begin, begin + chunk)
        h, s = gelu_pair(dg(low, w_up[:, cols], NN) + upb_ref[:, cols])
        h = h.astype(BF)
        hidden[:, cols] = h
        turned[cols, :] = h.T
        slope[:, cols] = s.astype(BF)
        part = pl.ds(begin, chunk)
        for kind, (left, right) in enumerate(
            (
                (hidden.at[:, part], hidden_out.at[:, part]),
                (turned.at[part, :], turned_out.at[part, :]),
                (slope.at[:, part], slope_out.at[:, part]),
            )
        ):
            save = pltpu.make_async_copy(left, right, save_sem.at[index * 3 + kind])
            save.start()
            saves.append(save)
    finish(saves)


def go_up(coords, mixed, tokens, vecs, up_bias, w_out, w_up, chunk=512):
    length, model = tokens.shape
    wide = up_bias.shape[1]
    return pl.pallas_call(
        functools.partial(
            up_kernel, out_places=w_out.places, up_places=w_up.places, chunk=chunk
        ),
        in_specs=[SMEM] + [VMEM] * 4 + [ANY] * (w_out.count + w_up.count),
        out_specs=[VMEM] * 4 + [ANY] * 3,
        out_shape=[
            shaped((length, model), F32),
            shaped((model, length), BF),
            shaped((length, model), F32),
            shaped((length, 1), F32),
            shaped((length, wide), BF),
            shaped((wide, length), BF),
            shaped((length, wide), BF),
        ],
        scratch_shapes=[
            pltpu.VMEM(w_out.shape, BF),
            pltpu.VMEM(w_up.shape, BF),
            pltpu.VMEM((length, wide), BF),
            pltpu.VMEM((wide, length), BF),
            pltpu.VMEM((length, wide), BF),
            pltpu.SemaphoreType.DMA((w_out.count + w_up.count,)),
            pltpu.SemaphoreType.DMA((3 * (wide // chunk),)),
        ],
        compiler_params=params(56),
        cost_estimate=cost(14.5),
        name="go_up",
    )(coords, mixed, tokens, vecs, up_bias, *w_out.pieces, *w_up.pieces)


def down_kernel(*refs, places, chunk):
    count = len(places)
    coords_ref, len_ref, n1_ref, cot_ref, vec_ref, hidden_in, turned_in = refs[:7]
    pieces = refs[7 : 7 + count]
    (
        y_ref,
        fb_ref,
        r2_ref,
        sums_ref,
        sent_ref,
        kept_ref,
        w_ref,
        hidden,
        turned,
        product_ref,
        sem_ref,
        own_sem,
    ) = refs[7 + count :]
    load = pltpu.make_async_copy(hidden_in, hidden, own_sem.at[0])
    load.start()
    copies = start_fetch(pieces, places, coords_ref, w_ref, sem_ref)
    load_turned = pltpu.make_async_copy(turned_in, turned, own_sem.at[1])
    load_turned.start()

    def vec(row):
        return vec_ref[row : row + 1, :]

    load.wait()
    finish(copies)
    n2, z2, r2 = norm_forward(
        n1_ref[...] + (dg(hidden[...], w_ref[...], NN) + vec(DOWN_B)), vec(GAIN2), vec(SHIFT2)
    )
    rows = n1_ref.shape[0]
    valid = (iota2((rows, 1), 0) < len_ref[0]).astype(F32)
    y_ref[...] = (n2 * valid).astype(BF)
    g2 = cot_ref[...].astype(F32) * valid
    back = norm_backward(g2, z2, r2, vec(GAIN2))
    r2_ref[...] = back
    fb = back.astype(BF)
    fb_ref[...] = fb
    sums_ref[...] = jnp.concatenate(
        [column_sum(fb.astype(F32)), column_sum(g2 * z2), column_sum(g2)]
        + [jnp.zeros((5, n1_ref.shape[1]), F32)],
        axis=0,
    )
    load_turned.wait()
    saves = []
    for index, begin in enumerate(range(0, turned.shape[0], chunk)):
        part = pl.ds(begin, chunk)
        product_ref[part, :] = dg(turned[part, :], fb, NN).astype(BF)
        saves += save_halves(
            coords_ref, product_ref.at[part], sent_ref.at[part], kept_ref.at[part], own_sem, 2 + 2 * index
        )
    finish(saves)


def go_down(coords, lengths, n1, cotangent, vecs, hidden, turned, weight, chunk=1024):
    length, model = n1.shape
    wide = hidden.shape[1]
    return pl.pallas_call(
        functools.partial(down_kernel, places=weight.places, chunk=chunk),
        in_specs=[SMEM] * 2 + [VMEM] * 3 + [ANY] * (2 + weight.count),
        out_specs=[VMEM] * 4 + [ANY] * 2,
        out_shape=[
            shaped((length, model), BF),
            shaped((length, model), BF),
            shaped((length, model), F32),
            shaped((8, model), F32),
            shaped((wide, model // 2), BF),
            shaped((wide, model // 2), BF),
        ],
        scratch_shapes=[
            pltpu.VMEM(weight.shape, BF),
            pltpu.VMEM((length, wide), BF),
            pltpu.VMEM((wide, length), BF),
            pltpu.VMEM((wide, model), BF),
            pltpu.SemaphoreType.DMA((weight.count,)),
            pltpu.SemaphoreType.DMA((2 + 2 * (wide // chunk),)),
        ],
        compiler_params=params(56),
        cost_estimate=cost(16),
        name="go_down",
    )(coords, lengths, n1, cotangent, vecs, hidden, turned, *weight.pieces)


def back_down_kernel(*refs, places, chunk):
    count = len(places)
    coords_ref, fb_ref, n1t_ref, slope_in = refs[:4]
    pieces = refs[4 : 4 + count]
    ub_out, upsum_ref, sent_ref, kept_ref, w_ref, slope, product_ref, sem_ref, own_sem = refs[
        4 + count :
    ]
    load = pltpu.make_async_copy(slope_in, slope, own_sem.at[0])
    copies = start_fetch(pieces, places, coords_ref, w_ref, sem_ref)
    load.start()
    fb = fb_ref[...]
    n1t = n1t_ref[...]
    upsum_ref[...] = jnp.zeros_like(upsum_ref)
    finish(copies)
    load.wait()
    saves = []
    for index, begin in enumerate(range(0, slope.shape[1], chunk)):
        cols = slice(begin, begin + chunk)
        ub = (slope[:, cols].astype(F32) * dg(fb, w_ref[cols, :], NT)).astype(BF)
        slope[:, cols] = ub
        upsum_ref[index : index + 1, :] = column_sum(ub.astype(F32))
        save = pltpu.make_async_copy(
            slope.at[:, pl.ds(begin, chunk)], ub_out.at[:, pl.ds(begin, chunk)], own_sem.at[3 + index]
        )
        save.start()
        saves.append(save)
        product_ref[:, cols] = dg(n1t, ub, NN).astype(BF)
    saves += save_halves(coords_ref, product_ref, sent_ref, kept_ref, own_sem, 1)
    finish(saves)


def back_down(coords, fb, n1t, slope, weight):
    length, model = fb.shape
    wide = slope.shape[1]
    chunk = model
    return pl.pallas_call(
        functools.partial(back_down_kernel, places=weight.places, chunk=chunk),
        in_specs=[SMEM] + [VMEM] * 2 + [ANY] * (1 + weight.count),
        out_specs=[ANY, VMEM, ANY, ANY],
        out_shape=[
            shaped((length, wide), BF),
            shaped((8, model), F32),
            shaped((model, wide // 2), BF),
            shaped((model, wide // 2), BF),
        ],
        scratch_shapes=[
            pltpu.VMEM(weight.shape, BF),
            pltpu.VMEM((length, wide), BF),
            pltpu.VMEM((model, wide), BF),
            pltpu.SemaphoreType.DMA((weight.count,)),
            pltpu.SemaphoreType.DMA((3 + wide // chunk,)),
        ],
        compiler_params=params(56),
        cost_estimate=cost(13.5),
        name="back_down",
    )(coords, fb, n1t, slope, *weight.pieces)


def back_up_kernel(*refs, up_places, out_places):
    ups, outs = len(up_places), len(out_places)
    coords_ref, r2_ref, z1_ref, r1_ref, vec_ref, ot_ref, ub_in = refs[:7]
    up_pieces = refs[7 : 7 + ups]
    out_pieces = refs[7 + ups : 7 + ups + outs]
    back_ref, ob_ref, sums_ref, product_ref, w_up, w_out, ub, sem_ref, own_sem = refs[
        7 + ups + outs :
    ]
    load = pltpu.make_async_copy(ub_in, ub, own_sem.at[0])
    load.start()
    second = start_fetch(up_pieces, up_places, coords_ref, w_up, sem_ref)
    first = start_fetch(out_pieces, out_places, coords_ref, w_out, sem_ref, ups)
    load.wait()
    finish(second)
    n1b = r2_ref[...] + dg(ub[...], w_up[...], NT)
    z1 = z1_ref[...]
    back = norm_backward(n1b, z1, r1_ref[...], vec_ref[GAIN1 : GAIN1 + 1, :])
    back_ref[...] = back
    ab = back.astype(BF)
    sums_ref[...] = jnp.concatenate(
        [column_sum(ab.astype(F32)), column_sum(n1b * z1), column_sum(n1b)]
        + [jnp.zeros((5, z1.shape[1]), F32)],
        axis=0,
    )
    finish(first)
    ob_ref[...] = dg(ab, w_out[...], NT).astype(BF)
    product_ref[...] = dg(ot_ref[...], ab, NN).astype(BF)


def back_up(coords, ub, r2, z1, r1, vecs, turned, w_up, w_out):
    length, model = r2.shape
    wide = ub.shape[1]
    return pl.pallas_call(
        functools.partial(back_up_kernel, up_places=w_up.places, out_places=w_out.places),
        in_specs=[SMEM] + [VMEM] * 5 + [ANY] * (1 + w_up.count + w_out.count),
        out_specs=[VMEM] * 4,
        out_shape=[
            shaped((length, model), F32),
            shaped((length, model), BF),
            shaped((8, model), F32),
            shaped((model, model), BF),
        ],
        scratch_shapes=[
            pltpu.VMEM(w_up.shape, BF),
            pltpu.VMEM(w_out.shape, BF),
            pltpu.VMEM((length, wide), BF),
            pltpu.SemaphoreType.DMA((w_up.count + w_out.count,)),
            pltpu.SemaphoreType.DMA((1,)),
        ],
        compiler_params=params(56),
        cost_estimate=cost(13.5),
        name="back_up",
    )(coords, r2, z1, r1, vecs, turned, ub, *w_up.pieces, *w_out.pieces)


def inputs_kernel(*refs, places):
    count = len(places)
    coords_ref, pb_ref, back_ref = refs[:3]
    pieces = refs[3 : 3 + count]
    out_ref, sums_ref, w_ref, sem_ref = refs[3 + count :]
    copies = start_fetch(pieces, places, coords_ref, w_ref, sem_ref)
    pb = pb_ref[...]
    flat = column_sum(pb.astype(F32))
    model = out_ref.shape[1]
    sums_ref[...] = jnp.zeros_like(sums_ref)
    for part in range(3):
        sums_ref[part : part + 1, :] = flat[:, part * model : (part + 1) * model]
    finish(copies)
    out_ref[...] = (back_ref[...] + dg(pb, w_ref[...], NT)).astype(BF)


def inputs_grad(coords, grad_packed, back, weight):
    length, model = back.shape
    count = weight.count
    return pl.pallas_call(
        functools.partial(inputs_kernel, places=weight.places),
        in_specs=[SMEM] + [VMEM] * 2 + [ANY] * count,
        out_specs=[VMEM] * 2,
        out_shape=[shaped((length, model), BF), shaped((8, model), F32)],
        scratch_shapes=[
            pltpu.VMEM(weight.shape, BF),
            pltpu.SemaphoreType.DMA((count,)),
        ],
        compiler_params=params(20),
        cost_estimate=cost(7),
        name="inputs_grad",
    )(coords, grad_packed, back, *weight.pieces)


def finish_kernel(at_ref, mine_ref, theirs_ref, *out_refs):
    first = at_ref[0] == 0
    begin = 0
    for out_ref in out_refs:
        columns = out_ref.shape[1] // 2
        mine = mine_ref[:, begin : begin + columns]
        theirs = theirs_ref[:, begin : begin + columns]
        out_ref[:, :columns] = jnp.where(first, mine, theirs).astype(F32)
        out_ref[:, columns:] = jnp.where(first, theirs, mine).astype(F32)
        begin += columns


def finish_pair(core, mine, theirs, widths):
    rows, columns = mine.shape
    step = rows // 4 if (rows // 4) % 16 == 0 else rows
    spec = pl.BlockSpec((step, columns), lambda i: (i, 0))
    return pl.pallas_call(
        finish_kernel,
        grid=(rows // step,),
        in_specs=[SMEM, spec, spec],
        out_specs=[pl.BlockSpec((step, width), lambda i: (i, 0)) for width in widths],
        out_shape=[shaped((rows, width), F32) for width in widths],
        compiler_params=params(16),
        cost_estimate=cost(4.4),
        name="finish_pair",
    )(core, mine, theirs)


class Axis:
    def __init__(self, name, total, stride, size):
        self.name = name
        self.total = total
        self.stride = stride
        self.size = size
        self.at = (lax.axis_index(name) // stride) % size

    def send(self, value, step):
        pairs = []
        for index in range(self.total):
            place = (index // self.stride) % self.size
            pairs.append((index, index + ((place + step) % self.size - place) * self.stride))
        return lax.ppermute(value, self.name, pairs)

    def peer(self, step):
        return (self.at + step) % self.size


def tie(value, *others):
    if not others:
        return value
    return lax.optimization_barrier((value,) + others)[0]


def take(stack, index, dim=0):
    return lax.dynamic_index_in_dim(stack, index, axis=dim, keepdims=False)


def arrange(axis, block, got, dim=0):
    if axis.size == 1:
        return jnp.expand_dims(block, dim)
    shape = [1] * (block.ndim + 1)
    shape[dim] = axis.size
    place = jnp.arange(axis.size, dtype=jnp.int32).reshape(shape)
    stack = jnp.expand_dims(block, dim)
    for step, value in enumerate(got):
        stack = jnp.where(place == axis.peer(-1 - step), jnp.expand_dims(value, dim), stack)
    return stack


def send_all(axis, block):
    return [axis.send(block, step) for step in range(1, axis.size)]


class Links:
    def __init__(self, dp, fsdp):
        core = 2
        rest = dp // core
        near = 2 if rest % 2 == 0 else 1
        self.core = Axis("dp", dp, 1, core)
        self.near = Axis("dp", dp, core, near)
        self.far = Axis("dp", dp, core * near, rest // near)
        self.pair = Axis("dp", dp, core * near, 2 if (rest // near) % 2 == 0 else 1)
        self.shard = Axis("fsdp", fsdp, 1, fsdp)


class Portion:
    def __init__(self, links, blocks, begin, count, mate):
        self.links = links
        self.mate = mate
        self.begin = begin
        self.rows = blocks[0].shape[0]
        parts = links.core.size * (mate.size if mate else 1)
        self.unit = count // parts
        self.blocks = blocks
        self.steps = []
        self.inbox = []

    def spot(self, s, t):
        core = self.links.core.peer(-s)
        return core * self.mate.size + self.mate.peer(-t) if self.mate else core

    def start(self, *after):
        begin = self.begin + self.spot(0, 0) * self.unit
        mine = [lax.dynamic_slice_in_dim(item, begin, self.unit, 0) for item in self.blocks]
        mine = tie(jnp.concatenate(mine, axis=1) if len(mine) > 1 else mine[0], *after)
        self.inbox = send_all(self.links.shard, mine)
        return [mine]

    def hop(self):
        self.got = self.inbox
        if self.mate:
            self.inbox = [self.mate.send(item, 1) for item in self.got]
        return list(self.got)

    def cross(self):
        self.crossed = [self.links.core.send(item, 1) for item in self.got]

    def last(self):
        self.hops = self.inbox if self.mate else []
        self.inbox = [self.links.core.send(item, 1) for item in self.hops]
        return list(self.hops) + list(self.crossed)

    def pieces(self):
        shard = self.links.shard
        which = None if self.mate is None else 1 if self.mate is self.links.near else 2
        found = []
        for index in range(len(self.got)):
            group = [(self.got[index], 0, 0), (self.crossed[index], 1, 0)]
            if self.mate:
                group += [(self.hops[index], 0, 1), (self.inbox[index], 1, 1)]
            for value, s, t in group:
                found.append(
                    (value, (self.rows, shard.size, self.begin, -1 - index, self.unit, -s, -t, which))
                )
        return found


class Fetch:
    def __init__(self, links, *blocks):
        self.links = links
        self.blocks = blocks
        rows = blocks[0].shape[0]
        mates = (links.near, links.pair)
        if rows % 128 == 0 and all(mate.size == 2 for mate in mates):
            half = rows // 2
            self.parts = [
                Portion(links, blocks, index * half, half, mate) for index, mate in enumerate(mates)
            ]
        else:
            self.parts = [Portion(links, blocks, 0, rows, None)]

    def do(self, name, *after):
        found = []
        for part in self.parts:
            found += getattr(part, name)(*after) or []
        return found

    def weights(self):
        rows = self.blocks[0].shape[0]
        count = self.links.shard.size
        found = []
        for part in self.parts:
            found += part.pieces()
        done = []
        begin = 0
        for block in self.blocks:
            columns = None if len(self.blocks) == 1 else begin
            done.append(
                Weight(
                    [block] + [item for item, _ in found],
                    [Place(rows, count)] + [Place(*place, columns=columns) for _, place in found],
                    (rows * count, block.shape[1]),
                )
            )
            begin += block.shape[1]
        return done


def meet(owners, *values):
    flat = [item for owner in owners for item in owner.inbox]
    flat = lax.optimization_barrier(tuple(flat) + tuple(values))
    begin = 0
    for owner in owners:
        count = len(owner.inbox)
        owner.inbox = list(flat[begin : begin + count])
        begin += count
    return list(flat[begin:])


def add_up(terms):
    total = terms[0].astype(F32)
    for term in terms[1:]:
        total = total + term.astype(F32)
    return total


class Chain:
    def __init__(self, links, sent, kept, line):
        self.links = links
        self.sent = sent
        self.line = line and links.far.size == 4
        rows, columns = kept.shape
        sizes = (links.shard.size, links.near.size, links.far.size, 2)
        whole = sizes[0] * sizes[1] * sizes[2] * sizes[3]
        self.shape = sizes + (rows // whole, columns)
        self.kept = kept

    def cross(self):
        self.inbox = [self.links.core.send(self.sent, 1)]
        return [self.sent]

    def hop(self, terms, axis, dim):
        sent = []
        for step in range(1, axis.size):
            pieces = [take(term, axis.peer(step), dim) for term in terms]
            sent.append(lax.optimization_barrier(add_up(pieces).astype(BF)))
        got = [axis.send(value, step + 1) for step, value in enumerate(sent)]
        kept = add_up([take(term, axis.at, dim) for term in terms]).astype(BF)
        return [lax.optimization_barrier(kept)], got, sent

    def first(self):
        other = self.inbox[0].reshape(self.shape)
        kept = self.kept.reshape(self.shape)
        halves = [[term[:, :, :, index] for term in (kept, other)] for index in range(2)]
        a, got_a, sent_a = self.hop(halves[0], self.links.shard, 0)
        b, got_b, sent_b = self.hop(halves[1], self.links.near, 1)
        self.terms = (a, b)
        self.inbox = got_a + got_b
        self.cut = len(got_a)
        return sent_a + sent_b

    def second(self):
        a = self.terms[0] + self.inbox[: self.cut]
        b = self.terms[1] + self.inbox[self.cut :]
        a, got_a, sent_a = self.hop(a, self.links.near, 0)
        b, got_b, sent_b = self.hop(b, self.links.shard, 0)
        self.terms = (a, b)
        self.inbox = got_a + got_b
        self.cut = len(got_a)
        return sent_a + sent_b

    def third(self):
        a = add_up(self.terms[0] + self.inbox[: self.cut])
        b = add_up(self.terms[1] + self.inbox[self.cut :])
        self.block = lax.optimization_barrier(jnp.stack([a, b], axis=1).astype(BF))
        if self.line:
            self.inbox = [self.line_send(self.block, ((0, 1), (3, 2)))]
            return [self.block]
        self.terms, self.inbox, sent = self.hop([self.block], self.links.far, 0)
        return sent

    def line_send(self, value, moves):
        far = self.links.far
        pairs = []
        for index in range(far.total):
            place = (index // far.stride) % far.size
            pairs += [(index, index + (to - place) * far.stride) for at, to in moves if at == place]
        return lax.ppermute(value, far.name, pairs)

    def middle(self):
        if not self.line:
            return []
        self.block = lax.optimization_barrier(add_up([self.block] + self.inbox).astype(BF))
        self.inbox = [self.line_send(self.block, ((1, 2), (2, 1)))]
        return [self.block]

    def fourth(self):
        if self.line:
            self.block = lax.optimization_barrier(add_up([self.block] + self.inbox).astype(BF))
            self.inbox = [self.line_send(self.block, ((1, 0), (2, 3)))]
            return [self.block]
        self.block = lax.optimization_barrier(add_up(self.terms + self.inbox).astype(BF))
        self.inbox = send_all(self.links.far, self.block)
        return [self.block]

    def fifth(self):
        far = self.links.far
        if self.line:
            outer = (far.at == 0) | (far.at == 3)
            block = jnp.where(outer, self.inbox[0], self.block)
        else:
            block = arrange(far, self.block, self.inbox)
        self.block = lax.optimization_barrier(block)
        self.inbox = send_all(self.links.near, self.block)
        return [self.block]

    def sixth(self):
        block = arrange(self.links.near, self.block, self.inbox)
        self.block = lax.optimization_barrier(block.reshape(-1, block.shape[-1]))
        self.inbox = [self.links.core.send(self.block, 1)]
        return [self.block]

    def done(self, widths):
        return finish_pair(self.links.coords, self.block, self.inbox[0], widths)


class Sums:
    def __init__(self, links, value):
        self.links = links
        self.total = value
        self.inbox = []

    def step(self, name):
        self.settle()
        self.inbox = send_all(getattr(self.links, name), self.total)
        return [self.total]

    def settle(self):
        self.total = functools.reduce(jnp.add, self.inbox, self.total)
        self.inbox = []


def per_device(
    dp,
    fsdp,
    tokens,
    lengths,
    buckets,
    qkv_weight,
    q_bias,
    v_bias,
    out_weight,
    out_bias,
    bias_table,
    norm1_gain,
    norm1_bias,
    up_weight,
    up_bias,
    down_weight,
    down_bias,
    norm2_gain,
    norm2_bias,
    cotangent,
):
    links = Links(dp, fsdp)
    model = tokens.shape[1]
    wide = up_weight.shape[1]
    heads = bias_table.shape[1]
    size = model // heads
    entries = bias_table.shape[0] * fsdp
    links.coords = coords = jnp.stack(
        [links.core.at, links.near.at, links.pair.at, links.shard.at]
    ).astype(jnp.int32)

    table_got = send_all(links.shard, bias_table)
    qkv = Fetch(links, qkv_weight)
    outup = Fetch(links, out_weight, up_weight)
    down = Fetch(links, down_weight)
    token = qkv.do("start", bias_table)
    narrow = (q_bias, v_bias, out_bias, norm1_gain, norm1_bias, down_bias, norm2_gain, norm2_bias)
    narrow = lax.optimization_barrier(narrow + (up_bias,) + tuple(token))
    row = jnp.arange(8, dtype=jnp.int32)[:, None]
    rows = jnp.broadcast_to(narrow[0][None], (8, narrow[0].size))
    for index in range(1, 8):
        rows = jnp.where(row == index, narrow[index][None], rows)
    part = out_bias.size
    rows = jnp.concatenate([rows, narrow[8].reshape(-1, part)], axis=0)
    rows = lax.optimization_barrier(rows)
    rows_got = send_all(links.shard, rows)
    table = arrange(links.shard, bias_table, table_got).reshape(entries, heads)
    bias = bias_scores(tie(buckets, rows, *token), lengths, table, 0, 1)
    tied = meet(qkv.parts, bias[0], bias[1], *rows_got)
    bias, rows_got = tied[:2], tied[2:]
    token = qkv.do("hop")
    qkv.do("cross")
    token = outup.do("start", *token)
    bias = bias_scores(tie(buckets, *token), lengths, table, 1, tokens.shape[0] // 128 - 1, bias)
    bias = meet(qkv.parts + outup.parts, *bias)
    token = qkv.do("last")
    token += outup.do("hop")
    token += down.do("start", *token)
    bias, ids = bias
    every = arrange(links.shard, rows, rows_got)
    vecs = jnp.swapaxes(every[:, :8], 0, 1).reshape(8, model).astype(F32)
    up_vec = every[:, 8:].reshape(1, -1).astype(F32)
    shift_row = jnp.concatenate([vecs[0:1], jnp.zeros((1, model), F32), vecs[1:2]], axis=1)
    shift_row, up_vec = lax.optimization_barrier((shift_row, up_vec) + tuple(token))[:2]
    (w_qkv,) = qkv.weights()
    half = model // WIDE // 2
    packed, probs, mixed, mixed_t, tokens_t = attend_first(
        coords, tokens, shift_row, w_qkv, bias, size, half
    )
    (mixed_t,) = meet(outup.parts + down.parts, mixed_t)
    outup.do("cross")
    token = outup.do("last")
    token += down.do("hop")
    probs, mixed, mixed_t = attend_rest(
        packed, bias, tie(probs, *token), mixed, mixed_t, size, half
    )
    (mixed,) = meet(outup.parts, mixed)
    w_out, w_up = outup.weights()
    n1, n1t, z1, r1, hidden, hidden_t, slope = go_up(
        coords, mixed, tokens, vecs, up_vec, w_out, w_up
    )
    (n1,) = meet(down.parts, n1)
    down.do("cross")
    token = down.do("last")
    (w_down,) = down.weights()
    output, fb, r2, sums_two, sent, kept = go_down(
        coords, lengths, tie(n1, *token), cotangent, vecs, hidden, hidden_t, w_down
    )

    chain_down = Chain(links, sent, kept, True)
    token = chain_down.cross()
    ub, up_sum, sent, kept = back_down(coords, tie(fb, *token), n1t, slope, w_down)
    ub, sent = meet([chain_down], ub, sent)
    chain_up = Chain(links, sent, kept, True)
    token = chain_down.first() + chain_up.cross()
    back, ob, sums_one, out_product = back_up(
        coords, tie(ub, *token), r2, z1, r1, vecs, mixed_t, w_up, w_out
    )
    (ob,) = meet([chain_down, chain_up], ob)
    token = chain_down.second() + chain_up.first()
    grad_packed, grad_scores, sent, kept = attend_back(
        coords, packed, probs, mixed, tie(ob, *token), tokens_t, out_product, size
    )
    sent, grad_scores, grad_packed = meet([chain_down, chain_up], sent, grad_scores, grad_packed)
    chain_qkv = Chain(links, sent, kept, False)
    token = chain_down.third() + chain_up.second() + chain_qkv.cross()
    table_one = table_grad(ids, tie(grad_scores, *token), entries, 0, 2)
    (table_one,) = meet([chain_down, chain_up, chain_qkv], table_one)
    token = chain_down.middle() + chain_up.third() + chain_qkv.first()
    table_two = table_grad(ids, tie(grad_scores, table_one, *token), entries, 1, 2)
    (table_two,) = meet([chain_down, chain_up, chain_qkv], table_two)
    token = chain_down.fourth() + chain_up.middle() + chain_qkv.second()
    tokens_grad, packed_sums = inputs_grad(coords, tie(grad_packed, table_two, *token), back, w_qkv)
    (packed_sums,) = meet([chain_down, chain_up, chain_qkv], packed_sums)
    sums = Sums(
        links,
        jnp.concatenate(
            [
                sums_one,
                sums_two,
                up_sum,
                packed_sums,
                jnp.pad(table_one + table_two, ((0, 0), (0, model - entries))),
            ],
            axis=0,
        ),
    )
    chain_down.fifth()
    chain_up.fourth()
    chain_qkv.third()
    sums.step("shard")
    meet([sums])
    sums.step("core")
    meet([chain_down, chain_up, chain_qkv, sums])
    chain_down.sixth()
    chain_up.fifth()
    chain_qkv.fourth()
    sums.step("near")
    meet([chain_down, sums])
    (g_down,) = chain_down.done((model,))
    (g_down,) = meet([chain_up, chain_qkv], g_down)
    chain_qkv.fifth()
    chain_up.sixth()
    sums.step("far")
    meet([chain_up, sums])
    sums.settle()
    (g_up,) = chain_up.done((wide,))
    (g_up,) = meet([chain_qkv], g_up)
    chain_qkv.sixth()
    g_out, g_qkv = chain_qkv.done((model, 3 * model))

    total = sums.total
    place = links.shard.at

    def piece(row):
        return lax.dynamic_slice(total, (row, place * part), (1, part)).reshape(part)

    g_out_bias, g_gain_one, g_shift_one = [piece(row) for row in range(3)]
    g_down_bias, g_gain_two, g_shift_two = [piece(row) for row in range(8, 11)]
    up_flat = total[16 : 16 + wide // model].reshape(wide)
    g_up_bias = lax.dynamic_slice_in_dim(up_flat, place * up_bias.size, up_bias.size)
    g_query_bias = piece(24)
    g_value_bias = piece(26)
    g_table = lax.dynamic_slice(
        total, (32, place * bias_table.shape[0]), (heads, bias_table.shape[0])
    ).T
    return (
        output,
        tokens_grad,
        g_qkv,
        g_query_bias,
        g_value_bias,
        g_out,
        g_out_bias,
        g_table,
        g_gain_one,
        g_shift_one,
        g_up,
        g_up_bias,
        g_down,
        g_down_bias,
        g_gain_two,
        g_shift_two,
    )


def solution(mesh):
    rows = P(("dp", "fsdp"), None)
    mat = P("fsdp", None)
    vec = P("fsdp")
    return jax.shard_map(
        functools.partial(per_device, mesh.shape["dp"], mesh.shape["fsdp"]),
        mesh=mesh,
        in_specs=(
            rows,
            P(("dp", "fsdp")),
            P(("dp", "fsdp"), None, None, None),
            mat,
            vec,
            vec,
            mat,
            vec,
            mat,
            vec,
            vec,
            mat,
            vec,
            mat,
            vec,
            vec,
            vec,
            rows,
        ),
        out_specs=(
            rows,
            rows,
            mat,
            vec,
            vec,
            mat,
            vec,
            mat,
            vec,
            vec,
            mat,
            vec,
            mat,
            vec,
            vec,
            vec,
        ),
        check_vma=False,
    )
```

```python
import functools

import jax
import jax.numpy as jnp
from jax import lax
from jax.experimental import pallas as pl
from jax.experimental.pallas import tpu as pltpu
from jax.sharding import PartitionSpec as P

EPSILON = 1e-05
MASKED = -1000000000.0
BF = jnp.bfloat16
F32 = jnp.float32
NN = (((1,), (0,)), ((), ()))
NT = (((1,), (1,)), ((), ()))
TN = (((0,), (0,)), ((), ()))
WIDE = 128
ANY = pl.BlockSpec(memory_space=pl.ANY)
SMEM = pl.BlockSpec(memory_space=pltpu.SMEM)
VMEM = pl.BlockSpec(memory_space=pltpu.VMEM)


def dg(left, right, dims):
    return lax.dot_general(left, right, dims, preferred_element_type=F32)


def params(mebibytes):
    return pltpu.CompilerParams(vmem_limit_bytes=mebibytes * 2**20)


def cost(micros):
    return pl.CostEstimate(flops=0, bytes_accessed=int(micros * 3e6), transcendentals=0)


def shaped(shape, dtype):
    return jax.ShapeDtypeStruct(shape, dtype)


def onehot_rows(ids, oh_ref, bucket_count):
    length = ids[0].shape[1]
    sub = lax.broadcasted_iota(jnp.int32, (16, length), 0)
    one = jnp.ones((16, length), BF)
    zero = jnp.zeros((16, length), BF)
    half = bucket_count // 2
    for kind in range(3):
        both = jnp.concatenate([ids[kind], ids[kind]], axis=0).astype(BF)
        for pair in range(half):
            level = jnp.where(sub < 8, 2 * pair, 2 * pair + 1).astype(F32).astype(BF)
            oh_ref[pl.ds((kind * half + pair) * 16, 16), :] = jnp.where(both == level, one, zero)


def iota2(shape, dim):
    return lax.broadcasted_iota(jnp.int32, shape, dim)


def bias_kernel(len_ref, ids_ref, table_ref, *rest, first):
    out_ref, turned_ref, spread_ref, held_ref, oh_ref = rest[-5:]
    step0 = pl.program_id(0)
    block = step0 + first
    heads, rows, length = out_ref.shape
    entries = table_ref.shape[0]
    valid = len_ref[0]

    @pl.when(step0 == 0)
    def _():
        pick_head = (iota2((heads * 8, heads), 0) >> 3) == iota2((heads * 8, heads), 1)
        rows_of = dg(pick_head.astype(F32).astype(BF), table_ref[...], NT).astype(BF)
        shape = (entries, entries * 8)
        pick_entry = iota2(shape, 0) == (iota2(shape, 1) >> 3)
        wide = dg(rows_of, pick_entry.astype(F32).astype(BF), NN)
        shape = (heads * 8, entries * 8)
        same = (iota2(shape, 0) & 7) == (iota2(shape, 1) & 7)
        spread_ref[...] = jnp.where(same, wide, 0.0).astype(BF)

    for kind in range(3):
        turned = ids_ref[0, kind].astype(F32).T
        held_ref[kind] = turned
        turned_ref[kind] = turned.astype(BF)

    def body(step, carry):
        parts = []
        for u in range(2):
            group = pl.ds(pl.multiple_of(step * 16 + u * 8, 8), 8)
            onehot_rows([held_ref[kind, group, :] for kind in range(3)], oh_ref.at[u], entries // 3)
            parts.append(dg(spread_ref[...], oh_ref[u], NN).reshape(heads, 8, length))
        bias = jnp.concatenate(parts, axis=1)
        key = iota2((1, 16, length), 1) + (block * rows + step * 16)
        out_ref[:, pl.ds(pl.multiple_of(step * 16, 16), 16), :] = jnp.where(
            key < valid, bias, MASKED
        ).astype(BF)
        return carry

    lax.fori_loop(0, rows // 16, body, 0, unroll=4)


def bias_scores(buckets, valid, table, first, steps, before=None, rows=128):
    length = buckets.shape[-1]
    entries, heads = table.shape
    held = () if before is None else tuple(before)
    return pl.pallas_call(
        functools.partial(bias_kernel, first=first),
        grid=(steps,),
        in_specs=[
            SMEM,
            pl.BlockSpec((1, 3, length, rows), lambda i: (0, 0, 0, first + i)),
            pl.BlockSpec((entries, heads), lambda i: (0, 0)),
        ]
        + [ANY] * len(held),
        out_specs=[
            pl.BlockSpec((heads, rows, length), lambda i: (0, first + i, 0)),
            pl.BlockSpec((3, rows, length), lambda i: (0, first + i, 0)),
        ],
        out_shape=[shaped((heads, length, length), BF), shaped((3, length, length), BF)],
        scratch_shapes=[
            pltpu.VMEM((heads * 8, entries * 8), BF),
            pltpu.VMEM((3, rows, length), F32),
            pltpu.VMEM((2, entries * 8, length), BF),
        ],
        input_output_aliases={3: 0, 4: 1} if held else {},
        compiler_params=params(56),
        cost_estimate=cost(8),
        name="bias_scores",
    )(valid, buckets, table, *held)


def table_kernel(ids_ref, grad_ref, out_ref, acc_ref, oh_ref):
    heads, rows, length = grad_ref.shape
    entries = out_ref.shape[1]

    @pl.when(pl.program_id(0) == 0)
    def _():
        acc_ref[...] = jnp.zeros_like(acc_ref)

    def body(step, carry):
        tile = pl.ds(pl.multiple_of(step * 16, 16), 16)
        grads = grad_ref[:, tile, :].astype(F32)
        ids = [ids_ref[kind, tile, :].astype(F32) for kind in range(3)]
        total = None
        for u in range(2):
            part = slice(u * 8, (u + 1) * 8)
            onehot_rows([item[part] for item in ids], oh_ref.at[u], entries // 3)
            part = dg(oh_ref[u], grads[:, part, :].reshape(heads * 8, length).astype(BF), NT)
            total = part if total is None else total + part
        acc_ref[...] += total
        return carry

    lax.fori_loop(0, rows // 16, body, 0, unroll=4)

    @pl.when(pl.program_id(0) == pl.num_programs(0) - 1)
    def _():
        shape = acc_ref.shape
        same = (iota2(shape, 0) & 7) == (iota2(shape, 1) & 7)
        kept = jnp.where(same, acc_ref[...], 0.0)
        rows_in = kept.reshape(entries, 8, heads * 8).sum(axis=1)
        shape = (out_ref.shape[0], heads * 8)
        fold = (iota2(shape, 0) == (iota2(shape, 1) >> 3)).astype(F32)
        out_ref[...] = lax.dot_general(
            fold, rows_in, NT, precision=lax.Precision.HIGHEST, preferred_element_type=F32
        )


def table_grad(ids, grads, entries, part, parts, rows=64):
    heads, length, _ = grads.shape
    padded = -(-heads // 8) * 8
    steps = length // rows // parts
    first = part * steps
    return pl.pallas_call(
        table_kernel,
        grid=(steps,),
        in_specs=[
            pl.BlockSpec((3, rows, length), lambda i: (0, first + i, 0)),
            pl.BlockSpec((heads, rows, length), lambda i: (0, first + i, 0)),
        ],
        out_specs=pl.BlockSpec((padded, entries), lambda i: (0, 0)),
        out_shape=shaped((padded, entries), F32),
        scratch_shapes=[
            pltpu.VMEM((entries * 8, heads * 8), F32),
            pltpu.VMEM((2, entries * 8, length), BF),
        ],
        compiler_params=params(30),
        cost_estimate=cost(9.5),
        name="table_grad",
    )(ids, grads)


class Place:
    def __init__(
        self, rows, blocks, begin=0, shard=0, unit=0, core=0, mate=0, which=None, columns=None
    ):
        self.rows = rows
        self.blocks = blocks
        self.begin = begin
        self.shard = shard
        self.unit = unit
        self.core = core
        self.mate = mate
        self.which = which
        self.columns = columns

    def row(self, coords_ref):
        def at(index, step, size):
            return lax.rem(coords_ref[index] + step % size, size)

        row = at(3, self.shard, self.blocks) * self.rows + self.begin
        if not self.unit:
            return row
        spot = at(0, self.core, 2)
        if self.which is not None:
            spot = spot * 2 + at(self.which, self.mate, 2)
        return row + spot * self.unit


class Weight:
    def __init__(self, pieces, places, shape):
        self.pieces = pieces
        self.places = places
        self.shape = shape
        self.count = len(pieces)


def start_fetch(refs, places, coords_ref, whole_ref, sem_ref, first=0):
    copies = []
    for index, ref in enumerate(refs):
        begin = pl.multiple_of(places[index].row(coords_ref), 16)
        target = whole_ref.at[pl.ds(begin, ref.shape[0])]
        if places[index].columns is not None:
            ref = ref.at[:, pl.ds(places[index].columns, whole_ref.shape[1])]
        copy = pltpu.make_async_copy(ref, target, sem_ref.at[first + index])
        copy.start()
        copies.append(copy)
    return copies


def finish(copies):
    for copy in copies:
        copy.wait()


def save_halves(core_ref, whole_ref, sent_ref, kept_ref, sem_ref, first, begin=0):
    columns = whole_ref.shape[1] // 2
    mine = core_ref[0]
    copies = []
    for index, (half, ref) in enumerate(((1 - mine, sent_ref), (mine, kept_ref))):
        cols = pl.ds(pl.multiple_of(half * columns, WIDE), columns)
        copy = pltpu.make_async_copy(
            whole_ref.at[:, cols], ref.at[:, pl.ds(begin, columns)], sem_ref.at[first + index]
        )
        copy.start()
        copies.append(copy)
    return copies


def attend_pair(q, k, v, bias_ref, p_ref, o_ref, ot_ref, size):
    width = q.shape[1]
    lane = iota2((1, width), 1)
    vt = v.T
    mixed = []
    for g in range(width // size):
        mine = (lane >= g * size) & (lane < (g + 1) * size)
        scores = dg(jnp.where(mine, k, jnp.zeros_like(k)), q, NT) + bias_ref[g].astype(F32)
        top = jnp.max(scores, axis=0, keepdims=True)
        shifted = jnp.exp(scores - top)
        norm = jnp.sum(shifted, axis=0, keepdims=True)
        probs = (shifted * (1.0 / norm)).astype(BF)
        p_ref[g] = probs
        mixed.append(dg(vt[g * size : (g + 1) * size], probs, NN))
    turned = jnp.concatenate(mixed, axis=0)
    ot_ref[...] = turned.astype(BF)
    o_ref[...] = turned.T.astype(BF)


def attend_first_kernel(*refs, size, places, factor):
    count = len(places)
    coords_ref, x_ref, shift_ref, bias_ref = refs[:4]
    pieces = refs[4 : 4 + count]
    qkv_ref, p_ref, o_ref, ot_ref, xt_ref, w_ref, sem_ref = refs[4 + count :]
    pair = pl.program_id(0)
    model = x_ref.shape[1]
    width = o_ref.shape[1]

    @pl.when(pair == 0)
    def _():
        copies = start_fetch(pieces, places, coords_ref, w_ref, sem_ref)
        xt_ref[...] = x_ref[...].T
        finish(copies)
        for part in range(3):
            cols = slice(part * model, (part + 1) * model)
            value = dg(x_ref[...], w_ref[:, cols], NN) + shift_ref[:, cols]
            if part == 0:
                value = value * factor
            qkv_ref[:, cols] = value.astype(BF)

    def block(part):
        return qkv_ref[:, pl.ds(pl.multiple_of(part * model + pair * width, width), width)]

    attend_pair(block(0), block(1), block(2), bias_ref, p_ref, o_ref, ot_ref, size)


def attend_rest_kernel(q_ref, k_ref, v_ref, bias_ref, _p, _o, _ot, p_ref, o_ref, ot_ref, *, size):
    attend_pair(q_ref[...], k_ref[...], v_ref[...], bias_ref, p_ref, o_ref, ot_ref, size)


def attend_first(coords, tokens, shift_row, weight, bias, size, steps):
    length, model = tokens.shape
    group = WIDE // size
    count = weight.count
    return pl.pallas_call(
        functools.partial(
            attend_first_kernel, size=size, places=weight.places, factor=size**-0.5
        ),
        grid=(steps,),
        in_specs=[
            SMEM,
            pl.BlockSpec((length, model), lambda i: (0, 0)),
            pl.BlockSpec((1, 3 * model), lambda i: (0, 0)),
            pl.BlockSpec((group, length, length), lambda i: (i, 0, 0)),
        ]
        + [ANY] * count,
        out_specs=[
            pl.BlockSpec((length, 3 * model), lambda i: (0, 0)),
            pl.BlockSpec((group, length, length), lambda i: (i, 0, 0)),
            pl.BlockSpec((length, WIDE), lambda i: (0, i)),
            pl.BlockSpec((WIDE, length), lambda i: (i, 0)),
            pl.BlockSpec((model, length), lambda i: (0, 0)),
        ],
        out_shape=[
            shaped((length, 3 * model), BF),
            shaped((model // size, length, length), BF),
            shaped((length, model), BF),
            shaped((model, length), BF),
            shaped((model, length), BF),
        ],
        scratch_shapes=[pltpu.VMEM(weight.shape, BF), pltpu.SemaphoreType.DMA((count,))],
        compiler_params=params(56),
        cost_estimate=cost(11.5),
        name="attend_first",
    )(coords, tokens, shift_row, bias, *weight.pieces)


def attend_rest(qkv, bias, probs, mixed, turned, size, first):
    length, model = mixed.shape
    group = WIDE // size
    blocks = model // WIDE
    return pl.pallas_call(
        functools.partial(attend_rest_kernel, size=size),
        grid=(blocks - first,),
        in_specs=[
            pl.BlockSpec((length, WIDE), lambda i: (0, first + i)),
            pl.BlockSpec((length, WIDE), lambda i: (0, blocks + first + i)),
            pl.BlockSpec((length, WIDE), lambda i: (0, 2 * blocks + first + i)),
            pl.BlockSpec((group, length, length), lambda i: (first + i, 0, 0)),
            ANY,
            ANY,
            ANY,
        ],
        out_specs=[
            pl.BlockSpec((group, length, length), lambda i: (first + i, 0, 0)),
            pl.BlockSpec((length, WIDE), lambda i: (0, first + i)),
            pl.BlockSpec((WIDE, length), lambda i: (first + i, 0)),
        ],
        out_shape=[
            shaped(probs.shape, BF),
            shaped(mixed.shape, BF),
            shaped(turned.shape, BF),
        ],
        input_output_aliases={4: 0, 5: 1, 6: 2},
        compiler_params=params(56),
        cost_estimate=cost(7),
        name="attend_rest",
    )(qkv, qkv, qkv, bias, probs, mixed, turned)


def attend_back_kernel(
    core_ref,
    q_ref,
    k_ref,
    v_ref,
    p_ref,
    o_ref,
    g_ref,
    xt_ref,
    prior_ref,
    out_ref,
    ds_ref,
    sent_ref,
    kept_ref,
    product_ref,
    sem_ref,
    *,
    size,
    factor,
):
    pair = pl.program_id(0)
    width = q_ref.shape[1]
    model = out_ref.shape[1] // 3
    count = width // size
    lane = iota2((1, width), 1)
    q = q_ref[...]
    v = v_ref[...]
    ob = g_ref[...]
    kt = k_ref[...].T
    product = o_ref[...].astype(F32) * ob.astype(F32)
    qs, ks, vs = [], [], []
    for g in range(count):
        mine = (lane >= g * size) & (lane < (g + 1) * size)
        spare = ((g + 1) % count) * size
        inner = jnp.sum(jnp.where(mine, product, 0.0), axis=1, keepdims=True)
        high = inner.astype(BF).astype(F32)
        extra = jnp.where(lane == spare, high, jnp.where(lane == spare + 1, inner - high, 0.0))
        minus = jnp.where((lane == spare) | (lane == spare + 1), -1.0, 0.0)
        left = jnp.where(mine, v, minus.astype(BF))
        right = jnp.where(mine, ob, extra.astype(BF))
        probs = p_ref[g]
        ds = (probs.astype(F32) * dg(left, right, NT)).astype(BF)
        ds_ref[g] = ds
        vs.append(dg(probs, ob, NN))
        ks.append(dg(ds, q, NN))
        qs.append(dg(kt[g * size : (g + 1) * size], ds, NN))

    def pick(items):
        chosen = items[0]
        for g in range(1, count):
            chosen = jnp.where(lane >= g * size, items[g], chosen)
        return chosen

    def place(start):
        return pl.ds(pl.multiple_of(start + pair * width, width), width)

    q_grad = jnp.concatenate(qs, axis=0).T.astype(BF).astype(F32) * factor
    out_ref[:, place(0)] = q_grad.astype(BF)
    out_ref[:, place(model)] = pick(ks).astype(BF)
    out_ref[:, place(2 * model)] = pick(vs).astype(BF)

    @pl.when(pair == pl.num_programs(0) - 1)
    def _():
        begin = prior_ref.shape[1] // 2
        copies = save_halves(core_ref, prior_ref, sent_ref, kept_ref, sem_ref, 0)
        for part in range(3):
            cols = slice(part * model, (part + 1) * model)
            product_ref[:, cols] = dg(xt_ref[...], out_ref[:, cols], NN).astype(BF)
        copies += save_halves(core_ref, product_ref, sent_ref, kept_ref, sem_ref, 2, begin)
        finish(copies)


def attend_back(core, qkv, probs, mixed, grad_mixed, turned, prior, size):
    length = qkv.shape[0]
    model = qkv.shape[1] // 3
    blocks = model // WIDE
    group = WIDE // size
    halves = shaped((model, (prior.shape[1] + 3 * model) // 2), BF)
    return pl.pallas_call(
        functools.partial(attend_back_kernel, size=size, factor=size**-0.5),
        grid=(blocks,),
        in_specs=[
            SMEM,
            pl.BlockSpec((length, WIDE), lambda i: (0, i)),
            pl.BlockSpec((length, WIDE), lambda i: (0, blocks + i)),
            pl.BlockSpec((length, WIDE), lambda i: (0, 2 * blocks + i)),
            pl.BlockSpec((group, length, length), lambda i: (i, 0, 0)),
            pl.BlockSpec((length, WIDE), lambda i: (0, i)),
            pl.BlockSpec((length, WIDE), lambda i: (0, i)),
            pl.BlockSpec((model, length), lambda i: (0, 0)),
            pl.BlockSpec(prior.shape, lambda i: (0, 0)),
        ],
        out_specs=[
            pl.BlockSpec((length, 3 * model), lambda i: (0, 0)),
            pl.BlockSpec((group, length, length), lambda i: (i, 0, 0)),
            ANY,
            ANY,
        ],
        out_shape=[
            shaped((length, 3 * model), BF),
            shaped((model // size, length, length), BF),
            halves,
            halves,
        ],
        scratch_shapes=[
            pltpu.VMEM((model, 3 * model), BF),
            pltpu.SemaphoreType.DMA((4,)),
        ],
        compiler_params=params(30),
        cost_estimate=cost(17),
        name="attend_back",
    )(core, qkv, qkv, qkv, probs, mixed, grad_mixed, turned, prior)


def norm_forward(inputs, gain_vec, shift_vec):
    center = inputs - jnp.mean(inputs, axis=-1, keepdims=True)
    inverse = lax.rsqrt(jnp.mean(center * center, axis=-1, keepdims=True) + EPSILON)
    scaled = center * inverse
    return (scaled * gain_vec + shift_vec, scaled, inverse)


def norm_backward(grad_in, scaled, inverse, gain_vec):
    inner_term = grad_in * gain_vec
    centered = inner_term - jnp.mean(inner_term, axis=-1, keepdims=True)
    return inverse * (centered - scaled * jnp.mean(inner_term * scaled, axis=-1, keepdims=True))


def gelu_pair(u):
    square = jnp.exp(u * u * -0.5)
    t = 1.0 / (1.0 + jnp.abs(u) * (0.3275911 * 0.7071067811865476))
    poly = t * (
        0.254829592
        + t * (-0.284496736 + t * (1.421413741 + t * (-1.453152027 + t * 1.061405429)))
    )
    tail = 0.5 * poly * square
    below = jnp.where(u >= 0.0, 1.0 - tail, tail)
    return u * below, below + u * (square * 0.3989422804014327)


def column_sum(values):
    return jnp.sum(values, axis=0, keepdims=True)


OUT_B, GAIN1, SHIFT1, DOWN_B, GAIN2, SHIFT2 = range(2, 8)


def up_kernel(*refs, out_places, up_places, chunk):
    outs, ups = len(out_places), len(up_places)
    coords_ref, mixed_ref, x_ref, vec_ref, upb_ref = refs[:5]
    out_pieces = refs[5 : 5 + outs]
    up_pieces = refs[5 + outs : 5 + outs + ups]
    (
        n1t_out,
        z1_out,
        r1_ref,
        hidden_out,
        turned_out,
        slope_out,
        w_out,
        w_up,
        n1t,
        z1_low,
        hidden,
        turned,
        slope,
        sem_ref,
        save_sem,
    ) = refs[5 + outs + ups :]
    first = start_fetch(out_pieces, out_places, coords_ref, w_out, sem_ref)
    second = start_fetch(up_pieces, up_places, coords_ref, w_up, sem_ref, outs)

    def vec(row):
        return vec_ref[row : row + 1, :]

    finish(first)
    summed = x_ref[...].astype(F32) + (dg(mixed_ref[...], w_out[...], NN) + vec(OUT_B))
    n1, z1, r1 = norm_forward(summed, vec(GAIN1), vec(SHIFT1))
    low = n1.astype(BF)
    n1t[...] = low.T
    z1_low[...] = z1.astype(BF)
    r1_ref[...] = r1
    saves = [
        pltpu.make_async_copy(n1t, n1t_out, save_sem.at[0]),
        pltpu.make_async_copy(z1_low, z1_out, save_sem.at[1]),
    ]
    for save in saves:
        save.start()
    finish(second)
    for index, begin in enumerate(range(0, hidden.shape[1], chunk)):
        cols = slice(begin, begin + chunk)
        h, s = gelu_pair(dg(low, w_up[:, cols], NN) + upb_ref[:, cols])
        h = h.astype(BF)
        hidden[:, cols] = h
        turned[cols, :] = h.T
        slope[:, cols] = s.astype(BF)
        part = pl.ds(begin, chunk)
        for kind, (left, right) in enumerate(
            (
                (hidden.at[:, part], hidden_out.at[:, part]),
                (turned.at[part, :], turned_out.at[part, :]),
                (slope.at[:, part], slope_out.at[:, part]),
            )
        ):
            save = pltpu.make_async_copy(left, right, save_sem.at[2 + index * 3 + kind])
            save.start()
            saves.append(save)
    finish(saves)


def go_up(coords, mixed, tokens, vecs, up_bias, w_out, w_up, chunk=512):
    length, model = tokens.shape
    wide = up_bias.shape[1]
    return pl.pallas_call(
        functools.partial(
            up_kernel, out_places=w_out.places, up_places=w_up.places, chunk=chunk
        ),
        in_specs=[SMEM] + [VMEM] * 4 + [ANY] * (w_out.count + w_up.count),
        out_specs=[ANY] * 2 + [VMEM] + [ANY] * 3,
        out_shape=[
            shaped((model, length), BF),
            shaped((length, model), BF),
            shaped((length, 1), F32),
            shaped((length, wide), BF),
            shaped((wide, length), BF),
            shaped((length, wide), BF),
        ],
        scratch_shapes=[
            pltpu.VMEM(w_out.shape, BF),
            pltpu.VMEM(w_up.shape, BF),
            pltpu.VMEM((model, length), BF),
            pltpu.VMEM((length, model), BF),
            pltpu.VMEM((length, wide), BF),
            pltpu.VMEM((wide, length), BF),
            pltpu.VMEM((length, wide), BF),
            pltpu.SemaphoreType.DMA((w_out.count + w_up.count,)),
            pltpu.SemaphoreType.DMA((2 + 3 * (wide // chunk),)),
        ],
        compiler_params=params(56),
        cost_estimate=cost(14.5),
        name="go_up",
    )(coords, mixed, tokens, vecs, up_bias, *w_out.pieces, *w_up.pieces)


def down_kernel(*refs, places, chunk):
    count = len(places)
    coords_ref, len_ref, z1_ref, vec_ref, cot_in, hidden_in, turned_in = refs[:7]
    pieces = refs[7 : 7 + count]
    (
        y_out,
        fb_out,
        sums_ref,
        sent_ref,
        kept_ref,
        w_ref,
        cot,
        y_low,
        fb_low,
        hidden,
        turned,
        product_ref,
        sem_ref,
        own_sem,
    ) = refs[7 + count :]
    load = pltpu.make_async_copy(hidden_in, hidden, own_sem.at[0])
    load.start()
    copies = start_fetch(pieces, places, coords_ref, w_ref, sem_ref)
    load_cot = pltpu.make_async_copy(cot_in, cot, own_sem.at[2])
    load_cot.start()
    load_turned = pltpu.make_async_copy(turned_in, turned, own_sem.at[1])
    load_turned.start()

    def vec(row):
        return vec_ref[row : row + 1, :]

    n1 = z1_ref[...].astype(F32) * vec(GAIN1) + vec(SHIFT1)
    load.wait()
    finish(copies)
    n2, z2, r2 = norm_forward(
        n1 + (dg(hidden[...], w_ref[...], NN) + vec(DOWN_B)), vec(GAIN2), vec(SHIFT2)
    )
    rows = z1_ref.shape[0]
    valid = (iota2((rows, 1), 0) < len_ref[0]).astype(F32)
    y_low[...] = (n2 * valid).astype(BF)
    load_cot.wait()
    g2 = cot[...].astype(F32) * valid
    back = norm_backward(g2, z2, r2, vec(GAIN2))
    fb = back.astype(BF)
    fb_low[...] = fb
    saves = [
        pltpu.make_async_copy(y_low, y_out, own_sem.at[3]),
        pltpu.make_async_copy(fb_low, fb_out, own_sem.at[4]),
    ]
    for save in saves:
        save.start()
    sums_ref[...] = jnp.concatenate(
        [column_sum(fb.astype(F32)), column_sum(g2 * z2), column_sum(g2)]
        + [jnp.zeros((5, z1_ref.shape[1]), F32)],
        axis=0,
    )
    load_turned.wait()
    for index, begin in enumerate(range(0, turned.shape[0], chunk)):
        part = pl.ds(begin, chunk)
        product_ref[part, :] = dg(turned[part, :], fb, NN).astype(BF)
        saves += save_halves(
            coords_ref, product_ref.at[part], sent_ref.at[part], kept_ref.at[part], own_sem, 5 + 2 * index
        )
    finish(saves)


def go_down(coords, lengths, z1, cotangent, vecs, hidden, turned, weight, chunk=1024):
    length, model = z1.shape
    wide = hidden.shape[1]
    return pl.pallas_call(
        functools.partial(down_kernel, places=weight.places, chunk=chunk),
        in_specs=[SMEM] * 2 + [VMEM] * 2 + [ANY] * (3 + weight.count),
        out_specs=[ANY] * 2 + [VMEM] + [ANY] * 2,
        out_shape=[
            shaped((length, model), BF),
            shaped((length, model), BF),
            shaped((8, model), F32),
            shaped((wide, model // 2), BF),
            shaped((wide, model // 2), BF),
        ],
        scratch_shapes=[
            pltpu.VMEM(weight.shape, BF),
            pltpu.VMEM((length, model), BF),
            pltpu.VMEM((length, model), BF),
            pltpu.VMEM((length, model), BF),
            pltpu.VMEM((length, wide), BF),
            pltpu.VMEM((wide, length), BF),
            pltpu.VMEM((wide, model), BF),
            pltpu.SemaphoreType.DMA((weight.count,)),
            pltpu.SemaphoreType.DMA((5 + 2 * (wide // chunk),)),
        ],
        compiler_params=params(56),
        cost_estimate=cost(16),
        name="go_down",
    )(coords, lengths, z1, vecs, cotangent, hidden, turned, *weight.pieces)


def back_down_kernel(*refs, places, chunk):
    count = len(places)
    coords_ref, fb_ref, n1t_ref, slope_in = refs[:4]
    pieces = refs[4 : 4 + count]
    ub_out, upsum_ref, sent_ref, kept_ref, w_ref, slope, product_ref, sem_ref, own_sem = refs[
        4 + count :
    ]
    load = pltpu.make_async_copy(slope_in, slope, own_sem.at[0])
    copies = start_fetch(pieces, places, coords_ref, w_ref, sem_ref)
    load.start()
    fb = fb_ref[...]
    n1t = n1t_ref[...]
    upsum_ref[...] = jnp.zeros_like(upsum_ref)
    finish(copies)
    load.wait()
    saves = []
    for index, begin in enumerate(range(0, slope.shape[1], chunk)):
        cols = slice(begin, begin + chunk)
        ub = (slope[:, cols].astype(F32) * dg(fb, w_ref[cols, :], NT)).astype(BF)
        slope[:, cols] = ub
        upsum_ref[index : index + 1, :] = column_sum(ub.astype(F32))
        save = pltpu.make_async_copy(
            slope.at[:, pl.ds(begin, chunk)], ub_out.at[:, pl.ds(begin, chunk)], own_sem.at[3 + index]
        )
        save.start()
        saves.append(save)
        product_ref[:, cols] = dg(n1t, ub, NN).astype(BF)
    saves += save_halves(coords_ref, product_ref, sent_ref, kept_ref, own_sem, 1)
    finish(saves)


def back_down(coords, fb, n1t, slope, weight):
    length, model = fb.shape
    wide = slope.shape[1]
    chunk = model
    return pl.pallas_call(
        functools.partial(back_down_kernel, places=weight.places, chunk=chunk),
        in_specs=[SMEM] + [VMEM] * 2 + [ANY] * (1 + weight.count),
        out_specs=[ANY, VMEM, ANY, ANY],
        out_shape=[
            shaped((length, wide), BF),
            shaped((8, model), F32),
            shaped((model, wide // 2), BF),
            shaped((model, wide // 2), BF),
        ],
        scratch_shapes=[
            pltpu.VMEM(weight.shape, BF),
            pltpu.VMEM((length, wide), BF),
            pltpu.VMEM((model, wide), BF),
            pltpu.SemaphoreType.DMA((weight.count,)),
            pltpu.SemaphoreType.DMA((3 + wide // chunk,)),
        ],
        compiler_params=params(56),
        cost_estimate=cost(13.5),
        name="back_down",
    )(coords, fb, n1t, slope, *weight.pieces)


def back_up_kernel(*refs, up_places, out_places):
    ups, outs = len(up_places), len(out_places)
    coords_ref, fb_ref, r1_ref, vec_ref, z1_in, ot_in, ub_in = refs[:7]
    up_pieces = refs[7 : 7 + ups]
    out_pieces = refs[7 + ups : 7 + ups + outs]
    (
        ab_out,
        ob_out,
        sums_ref,
        product_ref,
        w_up,
        w_out,
        ub,
        z1_low,
        ot,
        ab_low,
        ob_low,
        sem_ref,
        own_sem,
    ) = refs[7 + ups + outs :]
    load = pltpu.make_async_copy(ub_in, ub, own_sem.at[0])
    load.start()
    second = start_fetch(up_pieces, up_places, coords_ref, w_up, sem_ref)
    load_z1 = pltpu.make_async_copy(z1_in, z1_low, own_sem.at[1])
    load_z1.start()
    first = start_fetch(out_pieces, out_places, coords_ref, w_out, sem_ref, ups)
    load_ot = pltpu.make_async_copy(ot_in, ot, own_sem.at[2])
    load_ot.start()
    load.wait()
    finish(second)
    n1b = fb_ref[...].astype(F32) + dg(ub[...], w_up[...], NT)
    load_z1.wait()
    z1 = z1_low[...].astype(F32)
    back = norm_backward(n1b, z1, r1_ref[...], vec_ref[GAIN1 : GAIN1 + 1, :])
    ab = back.astype(BF)
    ab_low[...] = ab
    save_ab = pltpu.make_async_copy(ab_low, ab_out, own_sem.at[3])
    save_ab.start()
    sums_ref[...] = jnp.concatenate(
        [column_sum(ab.astype(F32)), column_sum(n1b * z1), column_sum(n1b)]
        + [jnp.zeros((5, z1.shape[1]), F32)],
        axis=0,
    )
    finish(first)
    ob_low[...] = dg(ab, w_out[...], NT).astype(BF)
    save_ob = pltpu.make_async_copy(ob_low, ob_out, own_sem.at[4])
    save_ob.start()
    load_ot.wait()
    product_ref[...] = dg(ot[...], ab, NN).astype(BF)
    save_ab.wait()
    save_ob.wait()


def back_up(coords, ub, fb, z1, r1, vecs, turned, w_up, w_out):
    length, model = fb.shape
    wide = ub.shape[1]
    return pl.pallas_call(
        functools.partial(back_up_kernel, up_places=w_up.places, out_places=w_out.places),
        in_specs=[SMEM] + [VMEM] * 3 + [ANY] * (3 + w_up.count + w_out.count),
        out_specs=[ANY] * 2 + [VMEM] * 2,
        out_shape=[
            shaped((length, model), BF),
            shaped((length, model), BF),
            shaped((8, model), F32),
            shaped((model, model), BF),
        ],
        scratch_shapes=[
            pltpu.VMEM(w_up.shape, BF),
            pltpu.VMEM(w_out.shape, BF),
            pltpu.VMEM((length, wide), BF),
            pltpu.VMEM((length, model), BF),
            pltpu.VMEM((model, length), BF),
            pltpu.VMEM((length, model), BF),
            pltpu.VMEM((length, model), BF),
            pltpu.SemaphoreType.DMA((w_up.count + w_out.count,)),
            pltpu.SemaphoreType.DMA((5,)),
        ],
        compiler_params=params(56),
        cost_estimate=cost(13.5),
        name="back_up",
    )(coords, fb, r1, vecs, z1, turned, ub, *w_up.pieces, *w_out.pieces)


def inputs_kernel(*refs, places):
    count = len(places)
    coords_ref, pb_ref, back_ref = refs[:3]
    pieces = refs[3 : 3 + count]
    out_ref, sums_ref, w_ref, sem_ref = refs[3 + count :]
    copies = start_fetch(pieces, places, coords_ref, w_ref, sem_ref)
    pb = pb_ref[...]
    flat = column_sum(pb.astype(F32))
    model = out_ref.shape[1]
    sums_ref[...] = jnp.zeros_like(sums_ref)
    for part in range(3):
        sums_ref[part : part + 1, :] = flat[:, part * model : (part + 1) * model]
    finish(copies)
    out_ref[...] = (back_ref[...].astype(F32) + dg(pb, w_ref[...], NT)).astype(BF)


def inputs_grad(coords, grad_packed, back, weight):
    length, model = back.shape
    count = weight.count
    return pl.pallas_call(
        functools.partial(inputs_kernel, places=weight.places),
        in_specs=[SMEM] + [VMEM] * 2 + [ANY] * count,
        out_specs=[VMEM] * 2,
        out_shape=[shaped((length, model), BF), shaped((8, model), F32)],
        scratch_shapes=[
            pltpu.VMEM(weight.shape, BF),
            pltpu.SemaphoreType.DMA((count,)),
        ],
        compiler_params=params(20),
        cost_estimate=cost(7),
        name="inputs_grad",
    )(coords, grad_packed, back, *weight.pieces)


def finish_kernel(at_ref, mine_ref, theirs_ref, *out_refs):
    first = at_ref[0] == 0
    begin = 0
    for out_ref in out_refs:
        columns = out_ref.shape[1] // 2
        mine = mine_ref[:, begin : begin + columns]
        theirs = theirs_ref[:, begin : begin + columns]
        out_ref[:, :columns] = jnp.where(first, mine, theirs).astype(F32)
        out_ref[:, columns:] = jnp.where(first, theirs, mine).astype(F32)
        begin += columns


def finish_pair(core, mine, theirs, widths):
    rows, columns = mine.shape
    step = rows // 4 if (rows // 4) % 16 == 0 else rows
    spec = pl.BlockSpec((step, columns), lambda i: (i, 0))
    return pl.pallas_call(
        finish_kernel,
        grid=(rows // step,),
        in_specs=[SMEM, spec, spec],
        out_specs=[pl.BlockSpec((step, width), lambda i: (i, 0)) for width in widths],
        out_shape=[shaped((rows, width), F32) for width in widths],
        compiler_params=params(16),
        cost_estimate=cost(4.4),
        name="finish_pair",
    )(core, mine, theirs)


class Axis:
    def __init__(self, name, total, stride, size):
        self.name = name
        self.total = total
        self.stride = stride
        self.size = size
        self.at = (lax.axis_index(name) // stride) % size

    def send(self, value, step):
        pairs = []
        for index in range(self.total):
            place = (index // self.stride) % self.size
            pairs.append((index, index + ((place + step) % self.size - place) * self.stride))
        return lax.ppermute(value, self.name, pairs)

    def peer(self, step):
        return (self.at + step) % self.size


def tie(value, *others):
    if not others:
        return value
    return lax.optimization_barrier((value,) + others)[0]


def take(stack, index, dim=0):
    return lax.dynamic_index_in_dim(stack, index, axis=dim, keepdims=False)


def arrange(axis, block, got, dim=0):
    if axis.size == 1:
        return jnp.expand_dims(block, dim)
    shape = [1] * (block.ndim + 1)
    shape[dim] = axis.size
    place = jnp.arange(axis.size, dtype=jnp.int32).reshape(shape)
    stack = jnp.expand_dims(block, dim)
    for step, value in enumerate(got):
        stack = jnp.where(place == axis.peer(-1 - step), jnp.expand_dims(value, dim), stack)
    return stack


def send_all(axis, block):
    return [axis.send(block, step) for step in range(1, axis.size)]


class Links:
    def __init__(self, dp, fsdp):
        core = 2
        rest = dp // core
        near = 2 if rest % 2 == 0 else 1
        self.core = Axis("dp", dp, 1, core)
        self.near = Axis("dp", dp, core, near)
        self.far = Axis("dp", dp, core * near, rest // near)
        self.pair = Axis("dp", dp, core * near, 2 if (rest // near) % 2 == 0 else 1)
        self.shard = Axis("fsdp", fsdp, 1, fsdp)


class Portion:
    def __init__(self, links, blocks, begin, count, mate):
        self.links = links
        self.mate = mate
        self.begin = begin
        self.rows = blocks[0].shape[0]
        parts = links.core.size * (mate.size if mate else 1)
        self.unit = count // parts
        self.blocks = blocks
        self.inbox = []
        self.held = []

    def spot(self, s, t):
        core = self.links.core.peer(-s)
        return core * self.mate.size + self.mate.peer(-t) if self.mate else core

    def start(self, *after):
        begin = self.begin + self.spot(0, 0) * self.unit
        mine = [lax.dynamic_slice_in_dim(item, begin, self.unit, 0) for item in self.blocks]
        mine = tie(jnp.concatenate(mine, axis=1) if len(mine) > 1 else mine[0], *after)
        self.inbox = send_all(self.links.shard, mine)
        return [mine]

    def hop(self):
        self.got = self.inbox
        if self.mate:
            self.inbox = [self.mate.send(item, 1) for item in self.got]
        return list(self.got)

    def cross(self, *after):
        self.crossed = [self.links.core.send(tie(item, *after), 1) for item in self.got]

    def last(self):
        self.hops = self.inbox if self.mate else []
        self.inbox = [self.links.core.send(item, 1) for item in self.hops]
        return list(self.hops) + list(self.crossed)

    def pieces(self):
        shard = self.links.shard
        which = None if self.mate is None else 1 if self.mate is self.links.near else 2
        found = []
        for index in range(len(self.got)):
            group = [(self.got[index], 0, 0), (self.crossed[index], 1, 0)]
            if self.mate:
                group += [(self.hops[index], 0, 1), (self.inbox[index], 1, 1)]
            for value, s, t in group:
                found.append(
                    (value, (self.rows, shard.size, self.begin, -1 - index, self.unit, -s, -t, which))
                )
        return found


class Fetch:
    def __init__(self, links, *blocks):
        self.links = links
        self.blocks = blocks
        rows = blocks[0].shape[0]
        mates = (links.near, links.pair)
        if rows % 128 == 0 and all(mate.size == 2 for mate in mates):
            half = rows // 2
            self.parts = [
                Portion(links, blocks, index * half, half, mate) for index, mate in enumerate(mates)
            ]
        else:
            self.parts = [Portion(links, blocks, 0, rows, None)]

    def do(self, name, *after):
        found = []
        for part in self.parts:
            found += getattr(part, name)(*after) or []
        return found

    def weights(self):
        rows = self.blocks[0].shape[0]
        count = self.links.shard.size
        found = []
        for part in self.parts:
            found += part.pieces()
        done = []
        begin = 0
        for block in self.blocks:
            columns = None if len(self.blocks) == 1 else begin
            done.append(
                Weight(
                    [block] + [item for item, _ in found],
                    [Place(rows, count)] + [Place(*place, columns=columns) for _, place in found],
                    (rows * count, block.shape[1]),
                )
            )
            begin += block.shape[1]
        return done


def meet(owners, *values):
    flat = [item for owner in owners for item in owner.inbox + owner.held]
    flat = lax.optimization_barrier(tuple(flat) + tuple(values))
    begin = 0
    for owner in owners:
        count = len(owner.inbox)
        owner.inbox = list(flat[begin : begin + count])
        begin += count
        count = len(owner.held)
        owner.held = list(flat[begin : begin + count])
        begin += count
    return list(flat[begin:])


def add_up(terms):
    total = terms[0].astype(F32)
    for term in terms[1:]:
        total = total + term.astype(F32)
    return total


class Chain:
    def __init__(self, links, sent, kept, line):
        self.links = links
        self.sent = sent
        self.line = line and links.far.size == 4
        rows, columns = kept.shape
        sizes = (links.shard.size, links.near.size, links.far.size, 2)
        whole = sizes[0] * sizes[1] * sizes[2] * sizes[3]
        self.shape = sizes + (rows // whole, columns)
        self.kept = kept

    def cross(self):
        self.inbox = [self.links.core.send(self.sent, 1)]
        self.held = [self.kept]
        return [self.sent]

    def hop(self, terms, axis):
        sent = []
        for step in range(1, axis.size):
            pieces = [term(axis.peer(step)) for term in terms]
            sent.append(lax.optimization_barrier(add_up(pieces).astype(BF)))
        return [axis.send(value, step + 1) for step, value in enumerate(sent)], sent

    def parts(self, way):
        def part(term):
            half = term.reshape(self.shape)[:, :, :, way]
            return lambda x, y: take(half if x is None else take(half, x), y, 0 if x is not None else 1)

        def row(term):
            half = term.reshape(self.shape)[:, :, :, way]
            return lambda x: take(half, x)

        return [part(term) for term in self.held[:2]], [row(term) for term in self.held[:2]]

    def first(self):
        self.held = self.held + self.inbox
        _, rows = self.parts(0)
        a, sent_a = self.hop(rows, self.links.shard)
        both, _ = self.parts(1)
        b, sent_b = self.hop([lambda y, f=f: f(None, y) for f in both], self.links.near)
        self.inbox = a + b
        self.cut = len(a)
        return sent_a + sent_b

    def second(self):
        x, y = self.links.shard.at, self.links.near.at
        got_a, got_b = self.inbox[: self.cut], self.inbox[self.cut :]
        parts, _ = self.parts(0)
        terms = [lambda to, f=f: f(x, to) for f in parts]
        terms += [lambda to, v=v: take(v, to) for v in got_a]
        a, sent_a = self.hop(terms, self.links.near)
        parts, _ = self.parts(1)
        terms = [lambda to, f=f: f(to, y) for f in parts]
        terms += [lambda to, v=v: take(v, to) for v in got_b]
        b, sent_b = self.hop(terms, self.links.shard)
        self.held = self.held[:2] + got_a + got_b
        self.inbox = a + b
        self.last_cut = len(a)
        return sent_a + sent_b

    def third(self):
        x, y = self.links.shard.at, self.links.near.at
        got = self.held[2:]
        halves = []
        for way, (early, at) in enumerate(((got[: self.cut], y), (got[self.cut :], x))):
            late = self.inbox[: self.last_cut] if way == 0 else self.inbox[self.last_cut :]
            parts, _ = self.parts(way)
            halves.append(add_up([f(x, y) for f in parts] + [take(v, at) for v in early] + late))
        self.held = []
        self.block = lax.optimization_barrier(jnp.stack(halves, axis=1).astype(BF))
        if self.line:
            self.inbox = [self.line_send(self.block, ((0, 1), (3, 2)))]
            return [self.block]
        far = self.links.far
        self.inbox, sent = self.hop([lambda to: take(self.block, to)], far)
        self.kept_block = self.block
        return sent

    def line_send(self, value, moves):
        far = self.links.far
        pairs = []
        for index in range(far.total):
            place = (index // far.stride) % far.size
            pairs += [(index, index + (to - place) * far.stride) for at, to in moves if at == place]
        return lax.ppermute(value, far.name, pairs)

    def middle(self):
        if not self.line:
            return []
        self.block = lax.optimization_barrier(add_up([self.block] + self.inbox).astype(BF))
        self.inbox = [self.line_send(self.block, ((1, 2), (2, 1)))]
        return [self.block]

    def fourth(self):
        if self.line:
            self.block = lax.optimization_barrier(add_up([self.block] + self.inbox).astype(BF))
            self.inbox = [self.line_send(self.block, ((1, 0), (2, 3)))]
            return [self.block]
        mine = take(self.kept_block, self.links.far.at)
        self.block = lax.optimization_barrier(add_up([mine] + self.inbox).astype(BF))
        self.inbox = send_all(self.links.far, self.block)
        return [self.block]

    def fifth(self):
        far = self.links.far
        if self.line:
            outer = (far.at == 0) | (far.at == 3)
            block = jnp.where(outer, self.inbox[0], self.block)
        else:
            block = arrange(far, self.block, self.inbox)
        self.block = lax.optimization_barrier(block)
        self.inbox = send_all(self.links.near, self.block)
        return [self.block]

    def sixth(self):
        block = arrange(self.links.near, self.block, self.inbox)
        self.block = lax.optimization_barrier(block.reshape(-1, block.shape[-1]))
        self.inbox = [self.links.core.send(self.block, 1)]
        return [self.block]

    def done(self, widths):
        return finish_pair(self.links.coords, self.block, self.inbox[0], widths)


class Sums:
    def __init__(self, links, value):
        self.links = links
        self.total = value
        self.inbox = []
        self.held = []

    def step(self, name):
        self.settle()
        self.inbox = send_all(getattr(self.links, name), self.total)
        return [self.total]

    def settle(self):
        self.total = functools.reduce(jnp.add, self.inbox, self.total)
        self.inbox = []


def per_device(
    dp,
    fsdp,
    tokens,
    lengths,
    buckets,
    qkv_weight,
    q_bias,
    v_bias,
    out_weight,
    out_bias,
    bias_table,
    norm1_gain,
    norm1_bias,
    up_weight,
    up_bias,
    down_weight,
    down_bias,
    norm2_gain,
    norm2_bias,
    cotangent,
):
    links = Links(dp, fsdp)
    model = tokens.shape[1]
    wide = up_weight.shape[1]
    heads = bias_table.shape[1]
    size = model // heads
    entries = bias_table.shape[0] * fsdp
    links.coords = coords = jnp.stack(
        [links.core.at, links.near.at, links.pair.at, links.shard.at]
    ).astype(jnp.int32)

    table_got = send_all(links.shard, bias_table)
    qkv = Fetch(links, qkv_weight)
    outup = Fetch(links, out_weight, up_weight)
    down = Fetch(links, down_weight)
    token = qkv.do("start", bias_table)
    narrow = (q_bias, v_bias, out_bias, norm1_gain, norm1_bias, down_bias, norm2_gain, norm2_bias)
    narrow = lax.optimization_barrier(narrow + (up_bias,) + tuple(token))
    row = jnp.arange(8, dtype=jnp.int32)[:, None]
    rows = jnp.broadcast_to(narrow[0][None], (8, narrow[0].size))
    for index in range(1, 8):
        rows = jnp.where(row == index, narrow[index][None], rows)
    part = out_bias.size
    rows = jnp.concatenate([rows, narrow[8].reshape(-1, part)], axis=0)
    rows = lax.optimization_barrier(rows)
    rows_got = send_all(links.shard, rows)
    table = arrange(links.shard, bias_table, table_got).reshape(entries, heads)
    bias = bias_scores(tie(buckets, rows, *token), lengths, table, 0, 1)
    tied = meet(qkv.parts, bias[0], bias[1], *rows_got)
    bias, rows_got = tied[:2], tied[2:]
    token = qkv.do("hop")
    qkv.do("cross")
    token = outup.do("start", *token)
    bias = bias_scores(tie(buckets, *token), lengths, table, 1, tokens.shape[0] // 128 - 1, bias)
    bias = meet(qkv.parts + outup.parts, *bias)
    token = qkv.do("last")
    token += outup.do("hop")
    token += down.do("start", *token)
    bias, ids = bias
    every = arrange(links.shard, rows, rows_got)
    vecs = jnp.swapaxes(every[:, :8], 0, 1).reshape(8, model).astype(F32)
    up_vec = every[:, 8:].reshape(1, -1).astype(F32)
    shift_row = jnp.concatenate([vecs[0:1], jnp.zeros((1, model), F32), vecs[1:2]], axis=1)
    shift_row, up_vec = lax.optimization_barrier((shift_row, up_vec) + tuple(token))[:2]
    (w_qkv,) = qkv.weights()
    half = model // WIDE // 2
    packed, probs, mixed, mixed_t, tokens_t = attend_first(
        coords, tokens, shift_row, w_qkv, bias, size, half
    )
    (mixed_t,) = meet(outup.parts + down.parts, mixed_t)
    outup.do("cross", mixed_t)
    token = outup.do("last")
    token += down.do("hop")
    probs, mixed, mixed_t = attend_rest(
        packed, bias, tie(probs, *token), mixed, mixed_t, size, half
    )
    (mixed,) = meet(outup.parts, mixed)
    w_out, w_up = outup.weights()
    n1t, z1, r1, hidden, hidden_t, slope = go_up(
        coords, mixed, tokens, vecs, up_vec, w_out, w_up
    )
    (z1,) = meet(down.parts, z1)
    down.do("cross", z1)
    token = down.do("last")
    (w_down,) = down.weights()
    output, fb, sums_two, sent, kept = go_down(
        coords, lengths, tie(z1, *token), cotangent, vecs, hidden, hidden_t, w_down
    )

    chain_down = Chain(links, sent, kept, True)
    token = chain_down.cross()
    ub, up_sum, sent, kept = back_down(coords, tie(fb, *token), n1t, slope, w_down)
    ub, sent = meet([chain_down], ub, sent)
    chain_up = Chain(links, sent, kept, True)
    token = chain_down.first() + chain_up.cross()
    back, ob, sums_one, out_product = back_up(
        coords, tie(ub, *token), fb, z1, r1, vecs, mixed_t, w_up, w_out
    )
    (ob,) = meet([chain_down, chain_up], ob)
    token = chain_down.second() + chain_up.first()
    grad_packed, grad_scores, sent, kept = attend_back(
        coords, packed, probs, mixed, tie(ob, *token), tokens_t, out_product, size
    )
    sent, grad_scores, grad_packed = meet([chain_down, chain_up], sent, grad_scores, grad_packed)
    chain_qkv = Chain(links, sent, kept, False)
    token = chain_down.third() + chain_up.second() + chain_qkv.cross()
    table_one = table_grad(ids, tie(grad_scores, *token), entries, 0, 2)
    (table_one,) = meet([chain_down, chain_up, chain_qkv], table_one)
    token = chain_down.middle() + chain_up.third() + chain_qkv.first()
    table_two = table_grad(ids, tie(grad_scores, table_one, *token), entries, 1, 2)
    (table_two,) = meet([chain_down, chain_up, chain_qkv], table_two)
    token = chain_down.fourth() + chain_up.middle() + chain_qkv.second()
    tokens_grad, packed_sums = inputs_grad(coords, tie(grad_packed, table_two, *token), back, w_qkv)
    (packed_sums,) = meet([chain_down, chain_up, chain_qkv], packed_sums)
    sums = Sums(
        links,
        jnp.concatenate(
            [
                sums_one,
                sums_two,
                up_sum,
                packed_sums,
                jnp.pad(table_one + table_two, ((0, 0), (0, model - entries))),
            ],
            axis=0,
        ),
    )
    chain_down.fifth()
    chain_up.fourth()
    chain_qkv.third()
    sums.step("shard")
    meet([sums])
    sums.step("core")
    meet([chain_down, chain_up, chain_qkv, sums])
    chain_down.sixth()
    chain_up.fifth()
    chain_qkv.fourth()
    sums.step("near")
    meet([chain_down, sums])
    (g_down,) = chain_down.done((model,))
    (g_down,) = meet([chain_up, chain_qkv], g_down)
    chain_qkv.fifth()
    chain_up.sixth()
    sums.step("far")
    meet([chain_up, sums])
    sums.settle()
    (g_up,) = chain_up.done((wide,))
    (g_up,) = meet([chain_qkv], g_up)
    chain_qkv.sixth()
    g_out, g_qkv = chain_qkv.done((model, 3 * model))

    total = sums.total
    place = links.shard.at

    def piece(row):
        return lax.dynamic_slice(total, (row, place * part), (1, part)).reshape(part)

    g_out_bias, g_gain_one, g_shift_one = [piece(row) for row in range(3)]
    g_down_bias, g_gain_two, g_shift_two = [piece(row) for row in range(8, 11)]
    up_flat = total[16 : 16 + wide // model].reshape(wide)
    g_up_bias = lax.dynamic_slice_in_dim(up_flat, place * up_bias.size, up_bias.size)
    g_query_bias = piece(24)
    g_value_bias = piece(26)
    g_table = lax.dynamic_slice(
        total, (32, place * bias_table.shape[0]), (heads, bias_table.shape[0])
    ).T
    return (
        output,
        tokens_grad,
        g_qkv,
        g_query_bias,
        g_value_bias,
        g_out,
        g_out_bias,
        g_table,
        g_gain_one,
        g_shift_one,
        g_up,
        g_up_bias,
        g_down,
        g_down_bias,
        g_gain_two,
        g_shift_two,
    )


def solution(mesh):
    rows = P(("dp", "fsdp"), None)
    mat = P("fsdp", None)
    vec = P("fsdp")
    return jax.shard_map(
        functools.partial(per_device, mesh.shape["dp"], mesh.shape["fsdp"]),
        mesh=mesh,
        in_specs=(
            rows,
            P(("dp", "fsdp")),
            P(("dp", "fsdp"), None, None, None),
            mat,
            vec,
            vec,
            mat,
            vec,
            mat,
            vec,
            vec,
            mat,
            vec,
            mat,
            vec,
            vec,
            vec,
            rows,
        ),
        out_specs=(
            rows,
            rows,
            mat,
            vec,
            vec,
            mat,
            vec,
            mat,
            vec,
            vec,
            mat,
            vec,
            mat,
            vec,
            vec,
            vec,
        ),
        check_vma=False,
    )
```

```python
import functools

import jax
import jax.numpy as jnp
from jax import lax
from jax.experimental import pallas as pl
from jax.experimental.pallas import tpu as pltpu
from jax.sharding import PartitionSpec as P

EPSILON = 1e-05
MASKED = -1000000000.0
BF = jnp.bfloat16
F32 = jnp.float32
NN = (((1,), (0,)), ((), ()))
NT = (((1,), (1,)), ((), ()))
TN = (((0,), (0,)), ((), ()))
WIDE = 128
ANY = pl.BlockSpec(memory_space=pl.ANY)
SMEM = pl.BlockSpec(memory_space=pltpu.SMEM)
VMEM = pl.BlockSpec(memory_space=pltpu.VMEM)


def dg(left, right, dims):
    return lax.dot_general(left, right, dims, preferred_element_type=F32)


def params(mebibytes):
    return pltpu.CompilerParams(vmem_limit_bytes=mebibytes * 2**20)


def cost(micros):
    return pl.CostEstimate(flops=0, bytes_accessed=int(micros * 3e6), transcendentals=0)


def shaped(shape, dtype):
    return jax.ShapeDtypeStruct(shape, dtype)


def onehot_rows(ids, oh_ref, bucket_count):
    length = ids[0].shape[1]
    sub = lax.broadcasted_iota(jnp.int32, (16, length), 0)
    one = jnp.ones((16, length), BF)
    zero = jnp.zeros((16, length), BF)
    half = bucket_count // 2
    for kind in range(3):
        both = jnp.concatenate([ids[kind], ids[kind]], axis=0).astype(BF)
        for pair in range(half):
            level = jnp.where(sub < 8, 2 * pair, 2 * pair + 1).astype(F32).astype(BF)
            oh_ref[pl.ds((kind * half + pair) * 16, 16), :] = jnp.where(both == level, one, zero)


def iota2(shape, dim):
    return lax.broadcasted_iota(jnp.int32, shape, dim)


def bias_kernel(len_ref, ids_ref, table_ref, *rest, first):
    out_ref, turned_ref, spread_ref, held_ref, oh_ref = rest[-5:]
    step0 = pl.program_id(0)
    block = step0 + first
    heads, rows, length = out_ref.shape
    entries = table_ref.shape[0]
    valid = len_ref[0]

    @pl.when(step0 == 0)
    def _():
        pick_head = (iota2((heads * 8, heads), 0) >> 3) == iota2((heads * 8, heads), 1)
        rows_of = dg(pick_head.astype(F32).astype(BF), table_ref[...], NT).astype(BF)
        shape = (entries, entries * 8)
        pick_entry = iota2(shape, 0) == (iota2(shape, 1) >> 3)
        wide = dg(rows_of, pick_entry.astype(F32).astype(BF), NN)
        shape = (heads * 8, entries * 8)
        same = (iota2(shape, 0) & 7) == (iota2(shape, 1) & 7)
        spread_ref[...] = jnp.where(same, wide, 0.0).astype(BF)

    for kind in range(3):
        turned = ids_ref[0, kind].astype(F32).T
        held_ref[kind] = turned
        turned_ref[kind] = turned.astype(BF)

    def body(step, carry):
        parts = []
        for u in range(2):
            group = pl.ds(pl.multiple_of(step * 16 + u * 8, 8), 8)
            onehot_rows([held_ref[kind, group, :] for kind in range(3)], oh_ref.at[u], entries // 3)
            parts.append(dg(spread_ref[...], oh_ref[u], NN).reshape(heads, 8, length))
        bias = jnp.concatenate(parts, axis=1)
        key = iota2((1, 16, length), 1) + (block * rows + step * 16)
        out_ref[:, pl.ds(pl.multiple_of(step * 16, 16), 16), :] = jnp.where(
            key < valid, bias, MASKED
        ).astype(BF)
        return carry

    lax.fori_loop(0, rows // 16, body, 0, unroll=4)


def bias_scores(buckets, valid, table, first, steps, before=None, rows=128):
    length = buckets.shape[-1]
    entries, heads = table.shape
    held = () if before is None else tuple(before)
    return pl.pallas_call(
        functools.partial(bias_kernel, first=first),
        grid=(steps,),
        in_specs=[
            SMEM,
            pl.BlockSpec((1, 3, length, rows), lambda i: (0, 0, 0, first + i)),
            pl.BlockSpec((entries, heads), lambda i: (0, 0)),
        ]
        + [ANY] * len(held),
        out_specs=[
            pl.BlockSpec((heads, rows, length), lambda i: (0, first + i, 0)),
            pl.BlockSpec((3, rows, length), lambda i: (0, first + i, 0)),
        ],
        out_shape=[shaped((heads, length, length), BF), shaped((3, length, length), BF)],
        scratch_shapes=[
            pltpu.VMEM((heads * 8, entries * 8), BF),
            pltpu.VMEM((3, rows, length), F32),
            pltpu.VMEM((2, entries * 8, length), BF),
        ],
        input_output_aliases={3: 0, 4: 1} if held else {},
        compiler_params=params(56),
        cost_estimate=cost(8),
        name="bias_scores",
    )(valid, buckets, table, *held)


def table_kernel(ids_ref, grad_ref, out_ref, acc_ref, oh_ref):
    heads, rows, length = grad_ref.shape
    entries = out_ref.shape[1]

    @pl.when(pl.program_id(0) == 0)
    def _():
        acc_ref[...] = jnp.zeros_like(acc_ref)

    def body(step, carry):
        tile = pl.ds(pl.multiple_of(step * 16, 16), 16)
        grads = grad_ref[:, tile, :].astype(F32)
        ids = [ids_ref[kind, tile, :].astype(F32) for kind in range(3)]
        total = None
        for u in range(2):
            part = slice(u * 8, (u + 1) * 8)
            onehot_rows([item[part] for item in ids], oh_ref.at[u], entries // 3)
            part = dg(oh_ref[u], grads[:, part, :].reshape(heads * 8, length).astype(BF), NT)
            total = part if total is None else total + part
        acc_ref[...] += total
        return carry

    lax.fori_loop(0, rows // 16, body, 0, unroll=4)

    @pl.when(pl.program_id(0) == pl.num_programs(0) - 1)
    def _():
        shape = acc_ref.shape
        same = (iota2(shape, 0) & 7) == (iota2(shape, 1) & 7)
        kept = jnp.where(same, acc_ref[...], 0.0)
        rows_in = kept.reshape(entries, 8, heads * 8).sum(axis=1)
        shape = (out_ref.shape[0], heads * 8)
        fold = (iota2(shape, 0) == (iota2(shape, 1) >> 3)).astype(F32)
        out_ref[...] = lax.dot_general(
            fold, rows_in, NT, precision=lax.Precision.HIGHEST, preferred_element_type=F32
        )


def table_grad(ids, grads, entries, part, parts, rows=64):
    heads, length, _ = grads.shape
    padded = -(-heads // 8) * 8
    steps = length // rows // parts
    first = part * steps
    return pl.pallas_call(
        table_kernel,
        grid=(steps,),
        in_specs=[
            pl.BlockSpec((3, rows, length), lambda i: (0, first + i, 0)),
            pl.BlockSpec((heads, rows, length), lambda i: (0, first + i, 0)),
        ],
        out_specs=pl.BlockSpec((padded, entries), lambda i: (0, 0)),
        out_shape=shaped((padded, entries), F32),
        scratch_shapes=[
            pltpu.VMEM((entries * 8, heads * 8), F32),
            pltpu.VMEM((2, entries * 8, length), BF),
        ],
        compiler_params=params(30),
        cost_estimate=cost(9.5),
        name="table_grad",
    )(ids, grads)


class Place:
    def __init__(
        self, rows, blocks, begin=0, shard=0, unit=0, core=0, mate=0, which=None, columns=None
    ):
        self.rows = rows
        self.blocks = blocks
        self.begin = begin
        self.shard = shard
        self.unit = unit
        self.core = core
        self.mate = mate
        self.which = which
        self.columns = columns

    def row(self, coords_ref):
        def at(index, step, size):
            return lax.rem(coords_ref[index] + step % size, size)

        row = at(3, self.shard, self.blocks) * self.rows + self.begin
        if not self.unit:
            return row
        spot = at(0, self.core, 2)
        if self.which is not None:
            spot = spot * 2 + at(self.which, self.mate, 2)
        return row + spot * self.unit


class Weight:
    def __init__(self, pieces, places, shape):
        self.pieces = pieces
        self.places = places
        self.shape = shape
        self.count = len(pieces)


def start_fetch(refs, places, coords_ref, whole_ref, sem_ref, first=0):
    copies = []
    for index, ref in enumerate(refs):
        begin = pl.multiple_of(places[index].row(coords_ref), 16)
        target = whole_ref.at[pl.ds(begin, ref.shape[0])]
        if places[index].columns is not None:
            ref = ref.at[:, pl.ds(places[index].columns, whole_ref.shape[1])]
        copy = pltpu.make_async_copy(ref, target, sem_ref.at[first + index])
        copy.start()
        copies.append(copy)
    return copies


def finish(copies):
    for copy in copies:
        copy.wait()


def save_halves(core_ref, whole_ref, sent_ref, kept_ref, sem_ref, first, begin=0):
    columns = whole_ref.shape[1] // 2
    mine = core_ref[0]
    copies = []
    for index, (half, ref) in enumerate(((1 - mine, sent_ref), (mine, kept_ref))):
        cols = pl.ds(pl.multiple_of(half * columns, WIDE), columns)
        copy = pltpu.make_async_copy(
            whole_ref.at[:, cols], ref.at[:, pl.ds(begin, columns)], sem_ref.at[first + index]
        )
        copy.start()
        copies.append(copy)
    return copies


def attend_pair(q, k, v, bias_ref, p_ref, o_ref, ot_ref, size):
    width = q.shape[1]
    lane = iota2((1, width), 1)
    vt = v.T
    mixed = []
    for g in range(width // size):
        mine = (lane >= g * size) & (lane < (g + 1) * size)
        scores = dg(jnp.where(mine, k, jnp.zeros_like(k)), q, NT) + bias_ref[g].astype(F32)
        top = jnp.max(scores, axis=0, keepdims=True)
        shifted = jnp.exp(scores - top)
        norm = jnp.sum(shifted, axis=0, keepdims=True)
        probs = (shifted * (1.0 / norm)).astype(BF)
        p_ref[g] = probs
        mixed.append(dg(vt[g * size : (g + 1) * size], probs, NN))
    turned = jnp.concatenate(mixed, axis=0)
    ot_ref[...] = turned.astype(BF)
    o_ref[...] = turned.T.astype(BF)


def attend_first_kernel(*refs, size, places, factor):
    count = len(places)
    coords_ref, x_ref, shift_ref, bias_ref = refs[:4]
    pieces = refs[4 : 4 + count]
    qkv_ref, p_ref, o_ref, ot_ref, xt_ref, w_ref, sem_ref = refs[4 + count :]
    pair = pl.program_id(0)
    model = x_ref.shape[1]
    width = o_ref.shape[1]

    @pl.when(pair == 0)
    def _():
        copies = start_fetch(pieces, places, coords_ref, w_ref, sem_ref)
        xt_ref[...] = x_ref[...].T
        finish(copies)
        for part in range(3):
            cols = slice(part * model, (part + 1) * model)
            value = dg(x_ref[...], w_ref[:, cols], NN) + shift_ref[:, cols]
            if part == 0:
                value = value * factor
            qkv_ref[:, cols] = value.astype(BF)

    def block(part):
        return qkv_ref[:, pl.ds(pl.multiple_of(part * model + pair * width, width), width)]

    attend_pair(block(0), block(1), block(2), bias_ref, p_ref, o_ref, ot_ref, size)


def attend_rest_kernel(q_ref, k_ref, v_ref, bias_ref, _p, _o, _ot, p_ref, o_ref, ot_ref, *, size):
    attend_pair(q_ref[...], k_ref[...], v_ref[...], bias_ref, p_ref, o_ref, ot_ref, size)


def attend_first(coords, tokens, shift_row, weight, bias, size, steps):
    length, model = tokens.shape
    group = WIDE // size
    count = weight.count
    return pl.pallas_call(
        functools.partial(
            attend_first_kernel, size=size, places=weight.places, factor=size**-0.5
        ),
        grid=(steps,),
        in_specs=[
            SMEM,
            pl.BlockSpec((length, model), lambda i: (0, 0)),
            pl.BlockSpec((1, 3 * model), lambda i: (0, 0)),
            pl.BlockSpec((group, length, length), lambda i: (i, 0, 0)),
        ]
        + [ANY] * count,
        out_specs=[
            pl.BlockSpec((length, 3 * model), lambda i: (0, 0)),
            pl.BlockSpec((group, length, length), lambda i: (i, 0, 0)),
            pl.BlockSpec((length, WIDE), lambda i: (0, i)),
            pl.BlockSpec((WIDE, length), lambda i: (i, 0)),
            pl.BlockSpec((model, length), lambda i: (0, 0)),
        ],
        out_shape=[
            shaped((length, 3 * model), BF),
            shaped((model // size, length, length), BF),
            shaped((length, model), BF),
            shaped((model, length), BF),
            shaped((model, length), BF),
        ],
        scratch_shapes=[pltpu.VMEM(weight.shape, BF), pltpu.SemaphoreType.DMA((count,))],
        compiler_params=params(56),
        cost_estimate=cost(11.5),
        name="attend_first",
    )(coords, tokens, shift_row, bias, *weight.pieces)


def attend_rest(qkv, bias, probs, mixed, turned, size, first):
    length, model = mixed.shape
    group = WIDE // size
    blocks = model // WIDE
    return pl.pallas_call(
        functools.partial(attend_rest_kernel, size=size),
        grid=(blocks - first,),
        in_specs=[
            pl.BlockSpec((length, WIDE), lambda i: (0, first + i)),
            pl.BlockSpec((length, WIDE), lambda i: (0, blocks + first + i)),
            pl.BlockSpec((length, WIDE), lambda i: (0, 2 * blocks + first + i)),
            pl.BlockSpec((group, length, length), lambda i: (first + i, 0, 0)),
            ANY,
            ANY,
            ANY,
        ],
        out_specs=[
            pl.BlockSpec((group, length, length), lambda i: (first + i, 0, 0)),
            pl.BlockSpec((length, WIDE), lambda i: (0, first + i)),
            pl.BlockSpec((WIDE, length), lambda i: (first + i, 0)),
        ],
        out_shape=[
            shaped(probs.shape, BF),
            shaped(mixed.shape, BF),
            shaped(turned.shape, BF),
        ],
        input_output_aliases={4: 0, 5: 1, 6: 2},
        compiler_params=params(56),
        cost_estimate=cost(7),
        name="attend_rest",
    )(qkv, qkv, qkv, bias, probs, mixed, turned)


def attend_back_kernel(
    core_ref,
    q_ref,
    k_ref,
    v_ref,
    p_ref,
    o_ref,
    g_ref,
    xt_ref,
    prior_ref,
    out_ref,
    ds_ref,
    sent_ref,
    kept_ref,
    product_ref,
    sem_ref,
    *,
    size,
    factor,
):
    pair = pl.program_id(0)
    width = q_ref.shape[1]
    model = out_ref.shape[1] // 3
    count = width // size
    lane = iota2((1, width), 1)
    q = q_ref[...]
    v = v_ref[...]
    ob = g_ref[...]
    kt = k_ref[...].T
    product = o_ref[...].astype(F32) * ob.astype(F32)
    qs, ks, vs = [], [], []
    for g in range(count):
        mine = (lane >= g * size) & (lane < (g + 1) * size)
        spare = ((g + 1) % count) * size
        inner = jnp.sum(jnp.where(mine, product, 0.0), axis=1, keepdims=True)
        high = inner.astype(BF).astype(F32)
        extra = jnp.where(lane == spare, high, jnp.where(lane == spare + 1, inner - high, 0.0))
        minus = jnp.where((lane == spare) | (lane == spare + 1), -1.0, 0.0)
        left = jnp.where(mine, v, minus.astype(BF))
        right = jnp.where(mine, ob, extra.astype(BF))
        probs = p_ref[g]
        ds = (probs.astype(F32) * dg(left, right, NT)).astype(BF)
        ds_ref[g] = ds
        vs.append(dg(probs, ob, NN))
        ks.append(dg(ds, q, NN))
        qs.append(dg(kt[g * size : (g + 1) * size], ds, NN))

    def pick(items):
        chosen = items[0]
        for g in range(1, count):
            chosen = jnp.where(lane >= g * size, items[g], chosen)
        return chosen

    def place(start):
        return pl.ds(pl.multiple_of(start + pair * width, width), width)

    q_grad = jnp.concatenate(qs, axis=0).T.astype(BF).astype(F32) * factor
    out_ref[:, place(0)] = q_grad.astype(BF)
    out_ref[:, place(model)] = pick(ks).astype(BF)
    out_ref[:, place(2 * model)] = pick(vs).astype(BF)

    @pl.when(pair == pl.num_programs(0) - 1)
    def _():
        begin = prior_ref.shape[1] // 2
        copies = save_halves(core_ref, prior_ref, sent_ref, kept_ref, sem_ref, 0)
        for part in range(3):
            cols = slice(part * model, (part + 1) * model)
            product_ref[:, cols] = dg(xt_ref[...], out_ref[:, cols], NN).astype(BF)
        copies += save_halves(core_ref, product_ref, sent_ref, kept_ref, sem_ref, 2, begin)
        finish(copies)


def attend_back(core, qkv, probs, mixed, grad_mixed, turned, prior, size):
    length = qkv.shape[0]
    model = qkv.shape[1] // 3
    blocks = model // WIDE
    group = WIDE // size
    halves = shaped((model, (prior.shape[1] + 3 * model) // 2), BF)
    return pl.pallas_call(
        functools.partial(attend_back_kernel, size=size, factor=size**-0.5),
        grid=(blocks,),
        in_specs=[
            SMEM,
            pl.BlockSpec((length, WIDE), lambda i: (0, i)),
            pl.BlockSpec((length, WIDE), lambda i: (0, blocks + i)),
            pl.BlockSpec((length, WIDE), lambda i: (0, 2 * blocks + i)),
            pl.BlockSpec((group, length, length), lambda i: (i, 0, 0)),
            pl.BlockSpec((length, WIDE), lambda i: (0, i)),
            pl.BlockSpec((length, WIDE), lambda i: (0, i)),
            pl.BlockSpec((model, length), lambda i: (0, 0)),
            pl.BlockSpec(prior.shape, lambda i: (0, 0)),
        ],
        out_specs=[
            pl.BlockSpec((length, 3 * model), lambda i: (0, 0)),
            pl.BlockSpec((group, length, length), lambda i: (i, 0, 0)),
            ANY,
            ANY,
        ],
        out_shape=[
            shaped((length, 3 * model), BF),
            shaped((model // size, length, length), BF),
            halves,
            halves,
        ],
        scratch_shapes=[
            pltpu.VMEM((model, 3 * model), BF),
            pltpu.SemaphoreType.DMA((4,)),
        ],
        compiler_params=params(30),
        cost_estimate=cost(17),
        name="attend_back",
    )(core, qkv, qkv, qkv, probs, mixed, grad_mixed, turned, prior)


def norm_forward(inputs, gain_vec, shift_vec):
    center = inputs - jnp.mean(inputs, axis=-1, keepdims=True)
    inverse = lax.rsqrt(jnp.mean(center * center, axis=-1, keepdims=True) + EPSILON)
    scaled = center * inverse
    return (scaled * gain_vec + shift_vec, scaled, inverse)


def norm_backward(grad_in, scaled, inverse, gain_vec):
    inner_term = grad_in * gain_vec
    centered = inner_term - jnp.mean(inner_term, axis=-1, keepdims=True)
    return inverse * (centered - scaled * jnp.mean(inner_term * scaled, axis=-1, keepdims=True))


def gelu_pair(u):
    square = jnp.exp(u * u * -0.5)
    t = 1.0 / (1.0 + jnp.abs(u) * (0.3275911 * 0.7071067811865476))
    poly = t * (
        0.254829592
        + t * (-0.284496736 + t * (1.421413741 + t * (-1.453152027 + t * 1.061405429)))
    )
    tail = 0.5 * poly * square
    below = jnp.where(u >= 0.0, 1.0 - tail, tail)
    return u * below, below + u * (square * 0.3989422804014327)


def column_sum(values):
    return jnp.sum(values, axis=0, keepdims=True)


OUT_B, GAIN1, SHIFT1, DOWN_B, GAIN2, SHIFT2 = range(2, 8)


def up_kernel(*refs, out_places, up_places, chunk):
    outs, ups = len(out_places), len(up_places)
    coords_ref, mixed_ref, x_ref, vec_ref, upb_ref = refs[:5]
    out_pieces = refs[5 : 5 + outs]
    up_pieces = refs[5 + outs : 5 + outs + ups]
    (
        n1t_out,
        z1_out,
        r1_ref,
        hidden_out,
        turned_out,
        slope_out,
        w_out,
        w_up,
        n1t,
        z1_low,
        hidden,
        turned,
        slope,
        sem_ref,
        save_sem,
    ) = refs[5 + outs + ups :]
    first = start_fetch(out_pieces, out_places, coords_ref, w_out, sem_ref)
    second = start_fetch(up_pieces, up_places, coords_ref, w_up, sem_ref, outs)

    def vec(row):
        return vec_ref[row : row + 1, :]

    finish(first)
    summed = x_ref[...].astype(F32) + (dg(mixed_ref[...], w_out[...], NN) + vec(OUT_B))
    n1, z1, r1 = norm_forward(summed, vec(GAIN1), vec(SHIFT1))
    low = n1.astype(BF)
    n1t[...] = low.T
    z1_low[...] = z1.astype(BF)
    r1_ref[...] = r1
    saves = [
        pltpu.make_async_copy(n1t, n1t_out, save_sem.at[0]),
        pltpu.make_async_copy(z1_low, z1_out, save_sem.at[1]),
    ]
    for save in saves:
        save.start()
    finish(second)
    for index, begin in enumerate(range(0, hidden.shape[1], chunk)):
        cols = slice(begin, begin + chunk)
        h, s = gelu_pair(dg(low, w_up[:, cols], NN) + upb_ref[:, cols])
        h = h.astype(BF)
        hidden[:, cols] = h
        turned[cols, :] = h.T
        slope[:, cols] = s.astype(BF)
        part = pl.ds(begin, chunk)
        for kind, (left, right) in enumerate(
            (
                (hidden.at[:, part], hidden_out.at[:, part]),
                (turned.at[part, :], turned_out.at[part, :]),
                (slope.at[:, part], slope_out.at[:, part]),
            )
        ):
            save = pltpu.make_async_copy(left, right, save_sem.at[2 + index * 3 + kind])
            save.start()
            saves.append(save)
    finish(saves)


def go_up(coords, mixed, tokens, vecs, up_bias, w_out, w_up, chunk=512):
    length, model = tokens.shape
    wide = up_bias.shape[1]
    return pl.pallas_call(
        functools.partial(
            up_kernel, out_places=w_out.places, up_places=w_up.places, chunk=chunk
        ),
        in_specs=[SMEM] + [VMEM] * 4 + [ANY] * (w_out.count + w_up.count),
        out_specs=[ANY] * 2 + [VMEM] + [ANY] * 3,
        out_shape=[
            shaped((model, length), BF),
            shaped((length, model), BF),
            shaped((length, 1), F32),
            shaped((length, wide), BF),
            shaped((wide, length), BF),
            shaped((length, wide), BF),
        ],
        scratch_shapes=[
            pltpu.VMEM(w_out.shape, BF),
            pltpu.VMEM(w_up.shape, BF),
            pltpu.VMEM((model, length), BF),
            pltpu.VMEM((length, model), BF),
            pltpu.VMEM((length, wide), BF),
            pltpu.VMEM((wide, length), BF),
            pltpu.VMEM((length, wide), BF),
            pltpu.SemaphoreType.DMA((w_out.count + w_up.count,)),
            pltpu.SemaphoreType.DMA((2 + 3 * (wide // chunk),)),
        ],
        compiler_params=params(56),
        cost_estimate=cost(14.5),
        name="go_up",
    )(coords, mixed, tokens, vecs, up_bias, *w_out.pieces, *w_up.pieces)


def down_kernel(*refs, places, chunk):
    count = len(places)
    coords_ref, len_ref, z1_ref, vec_ref, cot_in, hidden_in, turned_in = refs[:7]
    pieces = refs[7 : 7 + count]
    (
        y_out,
        fb_out,
        sums_ref,
        sent_ref,
        kept_ref,
        w_ref,
        cot,
        y_low,
        fb_low,
        hidden,
        turned,
        product_ref,
        sem_ref,
        own_sem,
    ) = refs[7 + count :]
    load = pltpu.make_async_copy(hidden_in, hidden, own_sem.at[0])
    load.start()
    copies = start_fetch(pieces, places, coords_ref, w_ref, sem_ref)
    load_cot = pltpu.make_async_copy(cot_in, cot, own_sem.at[2])
    load_cot.start()
    load_turned = pltpu.make_async_copy(turned_in, turned, own_sem.at[1])
    load_turned.start()

    def vec(row):
        return vec_ref[row : row + 1, :]

    n1 = z1_ref[...].astype(F32) * vec(GAIN1) + vec(SHIFT1)
    load.wait()
    finish(copies)
    n2, z2, r2 = norm_forward(
        n1 + (dg(hidden[...], w_ref[...], NN) + vec(DOWN_B)), vec(GAIN2), vec(SHIFT2)
    )
    rows = z1_ref.shape[0]
    valid = (iota2((rows, 1), 0) < len_ref[0]).astype(F32)
    y_low[...] = (n2 * valid).astype(BF)
    load_cot.wait()
    g2 = cot[...].astype(F32) * valid
    back = norm_backward(g2, z2, r2, vec(GAIN2))
    fb = back.astype(BF)
    fb_low[...] = fb
    saves = [
        pltpu.make_async_copy(y_low, y_out, own_sem.at[3]),
        pltpu.make_async_copy(fb_low, fb_out, own_sem.at[4]),
    ]
    for save in saves:
        save.start()
    sums_ref[...] = jnp.concatenate(
        [column_sum(fb.astype(F32)), column_sum(g2 * z2), column_sum(g2)]
        + [jnp.zeros((5, z1_ref.shape[1]), F32)],
        axis=0,
    )
    load_turned.wait()
    for index, begin in enumerate(range(0, turned.shape[0], chunk)):
        part = pl.ds(begin, chunk)
        product_ref[part, :] = dg(turned[part, :], fb, NN).astype(BF)
        saves += save_halves(
            coords_ref, product_ref.at[part], sent_ref.at[part], kept_ref.at[part], own_sem, 5 + 2 * index
        )
    finish(saves)


def go_down(coords, lengths, z1, cotangent, vecs, hidden, turned, weight, chunk=1024):
    length, model = z1.shape
    wide = hidden.shape[1]
    return pl.pallas_call(
        functools.partial(down_kernel, places=weight.places, chunk=chunk),
        in_specs=[SMEM] * 2 + [VMEM] * 2 + [ANY] * (3 + weight.count),
        out_specs=[ANY] * 2 + [VMEM] + [ANY] * 2,
        out_shape=[
            shaped((length, model), BF),
            shaped((length, model), BF),
            shaped((8, model), F32),
            shaped((wide, model // 2), BF),
            shaped((wide, model // 2), BF),
        ],
        scratch_shapes=[
            pltpu.VMEM(weight.shape, BF),
            pltpu.VMEM((length, model), BF),
            pltpu.VMEM((length, model), BF),
            pltpu.VMEM((length, model), BF),
            pltpu.VMEM((length, wide), BF),
            pltpu.VMEM((wide, length), BF),
            pltpu.VMEM((wide, model), BF),
            pltpu.SemaphoreType.DMA((weight.count,)),
            pltpu.SemaphoreType.DMA((5 + 2 * (wide // chunk),)),
        ],
        compiler_params=params(56),
        cost_estimate=cost(16),
        name="go_down",
    )(coords, lengths, z1, vecs, cotangent, hidden, turned, *weight.pieces)


def back_down_kernel(*refs, places, chunk):
    count = len(places)
    coords_ref, fb_ref, n1t_ref, slope_in = refs[:4]
    pieces = refs[4 : 4 + count]
    ub_out, upsum_ref, sent_ref, kept_ref, w_ref, slope, product_ref, sem_ref, own_sem = refs[
        4 + count :
    ]
    load = pltpu.make_async_copy(slope_in, slope, own_sem.at[0])
    copies = start_fetch(pieces, places, coords_ref, w_ref, sem_ref)
    load.start()
    fb = fb_ref[...]
    n1t = n1t_ref[...]
    upsum_ref[...] = jnp.zeros_like(upsum_ref)
    finish(copies)
    load.wait()
    saves = []
    for index, begin in enumerate(range(0, slope.shape[1], chunk)):
        cols = slice(begin, begin + chunk)
        ub = (slope[:, cols].astype(F32) * dg(fb, w_ref[cols, :], NT)).astype(BF)
        slope[:, cols] = ub
        upsum_ref[index : index + 1, :] = column_sum(ub.astype(F32))
        save = pltpu.make_async_copy(
            slope.at[:, pl.ds(begin, chunk)], ub_out.at[:, pl.ds(begin, chunk)], own_sem.at[3 + index]
        )
        save.start()
        saves.append(save)
        product_ref[:, cols] = dg(n1t, ub, NN).astype(BF)
    saves += save_halves(coords_ref, product_ref, sent_ref, kept_ref, own_sem, 1)
    finish(saves)


def back_down(coords, fb, n1t, slope, weight):
    length, model = fb.shape
    wide = slope.shape[1]
    chunk = model
    return pl.pallas_call(
        functools.partial(back_down_kernel, places=weight.places, chunk=chunk),
        in_specs=[SMEM] + [VMEM] * 2 + [ANY] * (1 + weight.count),
        out_specs=[ANY, VMEM, ANY, ANY],
        out_shape=[
            shaped((length, wide), BF),
            shaped((8, model), F32),
            shaped((model, wide // 2), BF),
            shaped((model, wide // 2), BF),
        ],
        scratch_shapes=[
            pltpu.VMEM(weight.shape, BF),
            pltpu.VMEM((length, wide), BF),
            pltpu.VMEM((model, wide), BF),
            pltpu.SemaphoreType.DMA((weight.count,)),
            pltpu.SemaphoreType.DMA((3 + wide // chunk,)),
        ],
        compiler_params=params(56),
        cost_estimate=cost(13.5),
        name="back_down",
    )(coords, fb, n1t, slope, *weight.pieces)


def back_up_kernel(*refs, up_places, out_places):
    ups, outs = len(up_places), len(out_places)
    coords_ref, fb_ref, r1_ref, vec_ref, z1_in, ot_in, ub_in = refs[:7]
    up_pieces = refs[7 : 7 + ups]
    out_pieces = refs[7 + ups : 7 + ups + outs]
    (
        ab_out,
        ob_out,
        sums_ref,
        product_ref,
        w_up,
        w_out,
        ub,
        z1_low,
        ot,
        ab_low,
        ob_low,
        sem_ref,
        own_sem,
    ) = refs[7 + ups + outs :]
    load = pltpu.make_async_copy(ub_in, ub, own_sem.at[0])
    load.start()
    second = start_fetch(up_pieces, up_places, coords_ref, w_up, sem_ref)
    load_z1 = pltpu.make_async_copy(z1_in, z1_low, own_sem.at[1])
    load_z1.start()
    first = start_fetch(out_pieces, out_places, coords_ref, w_out, sem_ref, ups)
    load_ot = pltpu.make_async_copy(ot_in, ot, own_sem.at[2])
    load_ot.start()
    load.wait()
    finish(second)
    n1b = fb_ref[...].astype(F32) + dg(ub[...], w_up[...], NT)
    load_z1.wait()
    z1 = z1_low[...].astype(F32)
    back = norm_backward(n1b, z1, r1_ref[...], vec_ref[GAIN1 : GAIN1 + 1, :])
    ab = back.astype(BF)
    ab_low[...] = ab
    save_ab = pltpu.make_async_copy(ab_low, ab_out, own_sem.at[3])
    save_ab.start()
    sums_ref[...] = jnp.concatenate(
        [column_sum(ab.astype(F32)), column_sum(n1b * z1), column_sum(n1b)]
        + [jnp.zeros((5, z1.shape[1]), F32)],
        axis=0,
    )
    finish(first)
    ob_low[...] = dg(ab, w_out[...], NT).astype(BF)
    save_ob = pltpu.make_async_copy(ob_low, ob_out, own_sem.at[4])
    save_ob.start()
    load_ot.wait()
    product_ref[...] = dg(ot[...], ab, NN).astype(BF)
    save_ab.wait()
    save_ob.wait()


def back_up(coords, ub, fb, z1, r1, vecs, turned, w_up, w_out):
    length, model = fb.shape
    wide = ub.shape[1]
    return pl.pallas_call(
        functools.partial(back_up_kernel, up_places=w_up.places, out_places=w_out.places),
        in_specs=[SMEM] + [VMEM] * 3 + [ANY] * (3 + w_up.count + w_out.count),
        out_specs=[ANY] * 2 + [VMEM] * 2,
        out_shape=[
            shaped((length, model), BF),
            shaped((length, model), BF),
            shaped((8, model), F32),
            shaped((model, model), BF),
        ],
        scratch_shapes=[
            pltpu.VMEM(w_up.shape, BF),
            pltpu.VMEM(w_out.shape, BF),
            pltpu.VMEM((length, wide), BF),
            pltpu.VMEM((length, model), BF),
            pltpu.VMEM((model, length), BF),
            pltpu.VMEM((length, model), BF),
            pltpu.VMEM((length, model), BF),
            pltpu.SemaphoreType.DMA((w_up.count + w_out.count,)),
            pltpu.SemaphoreType.DMA((5,)),
        ],
        compiler_params=params(56),
        cost_estimate=cost(13.5),
        name="back_up",
    )(coords, fb, r1, vecs, z1, turned, ub, *w_up.pieces, *w_out.pieces)


def inputs_kernel(*refs, places, counts):
    count = len(places)
    coords_ref, pb_ref, back_ref = refs[:3]
    vectors = refs[3 : 3 + len(counts)]
    tables = refs[3 + len(counts) : 5 + len(counts)]
    pieces = refs[5 + len(counts) : 5 + len(counts) + count]
    out_ref, sums_ref, w_ref, sem_ref = refs[5 + len(counts) + count :]
    copies = start_fetch(pieces, places, coords_ref, w_ref, sem_ref)
    pb = pb_ref[...]
    flat = column_sum(pb.astype(F32))
    model = out_ref.shape[1]
    sums_ref[...] = jnp.zeros_like(sums_ref)
    begin = 0
    for rows, ref in zip(counts, vectors):
        sums_ref[begin : begin + rows, :] = ref[:rows, :]
        begin += rows
    for part in range(3):
        sums_ref[begin : begin + 1, :] = flat[:, part * model : (part + 1) * model]
        begin += 1
    table = tables[0][...] + tables[1][...]
    for head in range(table.shape[0]):
        row = begin + head // (model // WIDE)
        lane = head % (model // WIDE) * WIDE
        if row < sums_ref.shape[0]:
            sums_ref[row : row + 1, lane : lane + table.shape[1]] = table[head : head + 1, :]
    finish(copies)
    out_ref[...] = (back_ref[...].astype(F32) + dg(pb, w_ref[...], NT)).astype(BF)


def inputs_grad(coords, grad_packed, back, vectors, counts, tables, heads, weight):
    length, model = back.shape
    count = weight.count
    rows = sum(counts) + 3 + -(-heads // (model // WIDE))
    rows = -(-rows // 8) * 8
    return pl.pallas_call(
        functools.partial(inputs_kernel, places=weight.places, counts=counts),
        in_specs=[SMEM] + [VMEM] * (4 + len(counts)) + [ANY] * count,
        out_specs=[VMEM] * 2,
        out_shape=[shaped((length, model), BF), shaped((rows, model), F32)],
        scratch_shapes=[
            pltpu.VMEM(weight.shape, BF),
            pltpu.SemaphoreType.DMA((count,)),
        ],
        compiler_params=params(20),
        cost_estimate=cost(7),
        name="inputs_grad",
    )(coords, grad_packed, back, *vectors, *tables, *weight.pieces)


def finish_kernel(at_ref, mine_ref, theirs_ref, *out_refs):
    first = at_ref[0] == 0
    begin = 0
    for out_ref in out_refs:
        columns = out_ref.shape[1] // 2
        mine = mine_ref[:, begin : begin + columns]
        theirs = theirs_ref[:, begin : begin + columns]
        out_ref[:, :columns] = jnp.where(first, mine, theirs).astype(F32)
        out_ref[:, columns:] = jnp.where(first, theirs, mine).astype(F32)
        begin += columns


def finish_pair(core, mine, theirs, widths):
    rows, columns = mine.shape
    step = rows // 4 if (rows // 4) % 16 == 0 else rows
    spec = pl.BlockSpec((step, columns), lambda i: (i, 0))
    return pl.pallas_call(
        finish_kernel,
        grid=(rows // step,),
        in_specs=[SMEM, spec, spec],
        out_specs=[pl.BlockSpec((step, width), lambda i: (i, 0)) for width in widths],
        out_shape=[shaped((rows, width), F32) for width in widths],
        compiler_params=params(16),
        cost_estimate=cost(4.4),
        name="finish_pair",
    )(core, mine, theirs)


class Axis:
    def __init__(self, name, total, stride, size):
        self.name = name
        self.total = total
        self.stride = stride
        self.size = size
        self.at = (lax.axis_index(name) // stride) % size

    def send(self, value, step):
        pairs = []
        for index in range(self.total):
            place = (index // self.stride) % self.size
            pairs.append((index, index + ((place + step) % self.size - place) * self.stride))
        return lax.ppermute(value, self.name, pairs)

    def peer(self, step):
        return (self.at + step) % self.size


def tie(value, *others):
    if not others:
        return value
    return lax.optimization_barrier((value,) + others)[0]


def take(stack, index, dim=0):
    return lax.dynamic_index_in_dim(stack, index, axis=dim, keepdims=False)


def arrange(axis, block, got, dim=0):
    if axis.size == 1:
        return jnp.expand_dims(block, dim)
    shape = [1] * (block.ndim + 1)
    shape[dim] = axis.size
    place = jnp.arange(axis.size, dtype=jnp.int32).reshape(shape)
    stack = jnp.expand_dims(block, dim)
    for step, value in enumerate(got):
        stack = jnp.where(place == axis.peer(-1 - step), jnp.expand_dims(value, dim), stack)
    return stack


def send_all(axis, block):
    return [axis.send(block, step) for step in range(1, axis.size)]


class Links:
    def __init__(self, dp, fsdp):
        core = 2
        rest = dp // core
        near = 2 if rest % 2 == 0 else 1
        self.core = Axis("dp", dp, 1, core)
        self.near = Axis("dp", dp, core, near)
        self.far = Axis("dp", dp, core * near, rest // near)
        self.pair = Axis("dp", dp, core * near, 2 if (rest // near) % 2 == 0 else 1)
        self.shard = Axis("fsdp", fsdp, 1, fsdp)


class Portion:
    def __init__(self, links, blocks, begin, count, mate):
        self.links = links
        self.mate = mate
        self.begin = begin
        self.rows = blocks[0].shape[0]
        parts = links.core.size * (mate.size if mate else 1)
        self.unit = count // parts
        self.blocks = blocks
        self.inbox = []
        self.held = []

    def spot(self, s, t):
        core = self.links.core.peer(-s)
        return core * self.mate.size + self.mate.peer(-t) if self.mate else core

    def start(self, *after):
        begin = self.begin + self.spot(0, 0) * self.unit
        mine = [lax.dynamic_slice_in_dim(item, begin, self.unit, 0) for item in self.blocks]
        mine = tie(jnp.concatenate(mine, axis=1) if len(mine) > 1 else mine[0], *after)
        self.inbox = send_all(self.links.shard, mine)
        return [mine]

    def hop(self):
        self.got = self.inbox
        if self.mate:
            self.inbox = [self.mate.send(item, 1) for item in self.got]
        return list(self.got)

    def cross(self, *after):
        self.crossed = [self.links.core.send(tie(item, *after), 1) for item in self.got]

    def last(self):
        self.hops = self.inbox if self.mate else []
        self.inbox = [self.links.core.send(item, 1) for item in self.hops]
        return list(self.hops) + list(self.crossed)

    def pieces(self):
        shard = self.links.shard
        which = None if self.mate is None else 1 if self.mate is self.links.near else 2
        found = []
        for index in range(len(self.got)):
            group = [(self.got[index], 0, 0), (self.crossed[index], 1, 0)]
            if self.mate:
                group += [(self.hops[index], 0, 1), (self.inbox[index], 1, 1)]
            for value, s, t in group:
                found.append(
                    (value, (self.rows, shard.size, self.begin, -1 - index, self.unit, -s, -t, which))
                )
        return found


class Fetch:
    def __init__(self, links, *blocks):
        self.links = links
        self.blocks = blocks
        rows = blocks[0].shape[0]
        mates = (links.near, links.pair)
        if rows % 128 == 0 and all(mate.size == 2 for mate in mates):
            half = rows // 2
            self.parts = [
                Portion(links, blocks, index * half, half, mate) for index, mate in enumerate(mates)
            ]
        else:
            self.parts = [Portion(links, blocks, 0, rows, None)]

    def do(self, name, *after):
        found = []
        for part in self.parts:
            found += getattr(part, name)(*after) or []
        return found

    def weights(self):
        rows = self.blocks[0].shape[0]
        count = self.links.shard.size
        found = []
        for part in self.parts:
            found += part.pieces()
        done = []
        begin = 0
        for block in self.blocks:
            columns = None if len(self.blocks) == 1 else begin
            done.append(
                Weight(
                    [block] + [item for item, _ in found],
                    [Place(rows, count)] + [Place(*place, columns=columns) for _, place in found],
                    (rows * count, block.shape[1]),
                )
            )
            begin += block.shape[1]
        return done


def meet(owners, *values):
    flat = [item for owner in owners for item in owner.inbox + owner.held]
    flat = lax.optimization_barrier(tuple(flat) + tuple(values))
    begin = 0
    for owner in owners:
        count = len(owner.inbox)
        owner.inbox = list(flat[begin : begin + count])
        begin += count
        count = len(owner.held)
        owner.held = list(flat[begin : begin + count])
        begin += count
    return list(flat[begin:])


def add_up(terms):
    total = terms[0].astype(F32)
    for term in terms[1:]:
        total = total + term.astype(F32)
    return total


class Chain:
    def __init__(self, links, sent, kept, line):
        self.links = links
        self.sent = sent
        self.line = line and links.far.size == 4
        rows, columns = kept.shape
        sizes = (links.shard.size, links.near.size, links.far.size, 2)
        whole = sizes[0] * sizes[1] * sizes[2] * sizes[3]
        self.shape = sizes + (rows // whole, columns)
        self.kept = kept

    def cross(self):
        self.inbox = [self.links.core.send(self.sent, 1)]
        self.held = [self.kept]
        return [self.sent]

    def hop(self, terms, axis):
        sent = []
        for step in range(1, axis.size):
            pieces = [term(axis.peer(step)) for term in terms]
            sent.append(lax.optimization_barrier(add_up(pieces).astype(BF)))
        return [axis.send(value, step + 1) for step, value in enumerate(sent)], sent

    def piece(self, term, way, x=None, y=None):
        shard, near, far, _, rows, columns = self.shape
        begin = [0 if x is None else x, 0 if y is None else y, 0, way, 0, 0]
        sizes = [shard if x is None else 1, near if y is None else 1, far, 1, rows, columns]
        keep = [size for at, size in zip((x, y), sizes[:2]) if at is None]
        part = lax.dynamic_slice(term.reshape(self.shape), begin, sizes)
        return part.reshape(*keep, far, rows, columns)

    def first(self):
        self.held = self.held + self.inbox
        held = self.held
        a, sent_a = self.hop(
            [lambda to, f=f: self.piece(f, 0, x=to) for f in held], self.links.shard
        )
        b, sent_b = self.hop([lambda to, f=f: self.piece(f, 1, y=to) for f in held], self.links.near)
        self.inbox = a + b
        self.cut = len(a)
        return sent_a + sent_b

    def second(self):
        x, y = self.links.shard.at, self.links.near.at
        got_a, got_b = self.inbox[: self.cut], self.inbox[self.cut :]
        held = self.held[:2]
        terms = [lambda to, f=f: self.piece(f, 0, x, to) for f in held]
        terms += [lambda to, v=v: take(v, to) for v in got_a]
        a, sent_a = self.hop(terms, self.links.near)
        terms = [lambda to, f=f: self.piece(f, 1, to, y) for f in held]
        terms += [lambda to, v=v: take(v, to) for v in got_b]
        b, sent_b = self.hop(terms, self.links.shard)
        self.held = held + got_a + got_b
        self.inbox = a + b
        self.last_cut = len(a)
        return sent_a + sent_b

    def third(self):
        x, y = self.links.shard.at, self.links.near.at
        got = self.held[2:]
        halves = []
        for way, (early, at) in enumerate(((got[: self.cut], y), (got[self.cut :], x))):
            late = self.inbox[: self.last_cut] if way == 0 else self.inbox[self.last_cut :]
            own = [self.piece(f, way, x, y) for f in self.held[:2]]
            halves.append(add_up(own + [take(v, at) for v in early] + late))
        self.held = []
        self.block = lax.optimization_barrier(jnp.stack(halves, axis=1).astype(BF))
        if self.line:
            self.inbox = [self.line_send(self.block, ((0, 1), (3, 2)))]
            return [self.block]
        far = self.links.far
        self.inbox, sent = self.hop([lambda to: take(self.block, to)], far)
        self.kept_block = self.block
        return sent

    def line_send(self, value, moves):
        far = self.links.far
        pairs = []
        for index in range(far.total):
            place = (index // far.stride) % far.size
            pairs += [(index, index + (to - place) * far.stride) for at, to in moves if at == place]
        return lax.ppermute(value, far.name, pairs)

    def middle(self):
        if not self.line:
            return []
        self.block = lax.optimization_barrier(add_up([self.block] + self.inbox).astype(BF))
        self.inbox = [self.line_send(self.block, ((1, 2), (2, 1)))]
        return [self.block]

    def fourth(self):
        if self.line:
            self.block = lax.optimization_barrier(add_up([self.block] + self.inbox).astype(BF))
            self.inbox = [self.line_send(self.block, ((1, 0), (2, 3)))]
            return [self.block]
        mine = take(self.kept_block, self.links.far.at)
        self.block = lax.optimization_barrier(add_up([mine] + self.inbox).astype(BF))
        self.inbox = send_all(self.links.far, self.block)
        return [self.block]

    def fifth(self):
        far = self.links.far
        if self.line:
            outer = (far.at == 0) | (far.at == 3)
            block = jnp.where(outer, self.inbox[0], self.block)
        else:
            block = arrange(far, self.block, self.inbox)
        self.block = lax.optimization_barrier(block)
        self.inbox = send_all(self.links.near, self.block)
        return [self.block]

    def sixth(self):
        block = arrange(self.links.near, self.block, self.inbox)
        self.block = lax.optimization_barrier(block.reshape(-1, block.shape[-1]))
        self.inbox = [self.links.core.send(self.block, 1)]
        return [self.block]

    def done(self, widths):
        return finish_pair(self.links.coords, self.block, self.inbox[0], widths)


class Sums:
    def __init__(self, links, value):
        self.links = links
        self.total = value
        self.inbox = []
        self.held = []

    def step(self, name):
        self.settle()
        self.inbox = send_all(getattr(self.links, name), self.total)
        return [self.total]

    def settle(self):
        self.total = functools.reduce(jnp.add, self.inbox, self.total)
        self.inbox = []


def per_device(
    dp,
    fsdp,
    tokens,
    lengths,
    buckets,
    qkv_weight,
    q_bias,
    v_bias,
    out_weight,
    out_bias,
    bias_table,
    norm1_gain,
    norm1_bias,
    up_weight,
    up_bias,
    down_weight,
    down_bias,
    norm2_gain,
    norm2_bias,
    cotangent,
):
    links = Links(dp, fsdp)
    model = tokens.shape[1]
    wide = up_weight.shape[1]
    heads = bias_table.shape[1]
    size = model // heads
    entries = bias_table.shape[0] * fsdp
    links.coords = coords = jnp.stack(
        [links.core.at, links.near.at, links.pair.at, links.shard.at]
    ).astype(jnp.int32)

    table_got = send_all(links.shard, bias_table)
    qkv = Fetch(links, qkv_weight)
    outup = Fetch(links, out_weight, up_weight)
    down = Fetch(links, down_weight)
    token = qkv.do("start", bias_table)
    narrow = (q_bias, v_bias, out_bias, norm1_gain, norm1_bias, down_bias, norm2_gain, norm2_bias)
    narrow = lax.optimization_barrier(narrow + (up_bias,) + tuple(token))
    row = jnp.arange(8, dtype=jnp.int32)[:, None]
    rows = jnp.broadcast_to(narrow[0][None], (8, narrow[0].size))
    for index in range(1, 8):
        rows = jnp.where(row == index, narrow[index][None], rows)
    part = out_bias.size
    rows = jnp.concatenate([rows, narrow[8].reshape(-1, part)], axis=0)
    rows = lax.optimization_barrier(rows)
    rows_got = send_all(links.shard, rows)
    table = arrange(links.shard, bias_table, table_got).reshape(entries, heads)
    bias = bias_scores(tie(buckets, rows, *token), lengths, table, 0, 1)
    tied = meet(qkv.parts, bias[0], bias[1], *rows_got)
    bias, rows_got = tied[:2], tied[2:]
    token = qkv.do("hop")
    qkv.do("cross")
    token = outup.do("start", *token)
    bias = bias_scores(tie(buckets, *token), lengths, table, 1, tokens.shape[0] // 128 - 1, bias)
    bias = meet(qkv.parts + outup.parts, *bias)
    token = qkv.do("last")
    token += outup.do("hop")
    token += down.do("start", *token)
    bias, ids = bias
    every = arrange(links.shard, rows, rows_got)
    vecs = jnp.swapaxes(every[:, :8], 0, 1).reshape(8, model).astype(F32)
    up_vec = every[:, 8:].reshape(1, -1).astype(F32)
    shift_row = jnp.concatenate([vecs[0:1], jnp.zeros((1, model), F32), vecs[1:2]], axis=1)
    shift_row, up_vec = lax.optimization_barrier((shift_row, up_vec) + tuple(token))[:2]
    (w_qkv,) = qkv.weights()
    half = model // WIDE * 2 // 3
    packed, probs, mixed, mixed_t, tokens_t = attend_first(
        coords, tokens, shift_row, w_qkv, bias, size, half
    )
    (mixed_t,) = meet(outup.parts + down.parts, mixed_t)
    outup.do("cross", mixed_t)
    token = outup.do("last")
    token += down.do("hop")
    probs, mixed, mixed_t = attend_rest(
        packed, bias, tie(probs, *token), mixed, mixed_t, size, half
    )
    (mixed,) = meet(outup.parts, mixed)
    w_out, w_up = outup.weights()
    n1t, z1, r1, hidden, hidden_t, slope = go_up(
        coords, mixed, tokens, vecs, up_vec, w_out, w_up
    )
    (z1,) = meet(down.parts, z1)
    down.do("cross", z1)
    token = down.do("last")
    (w_down,) = down.weights()
    output, fb, sums_two, sent, kept = go_down(
        coords, lengths, tie(z1, *token), cotangent, vecs, hidden, hidden_t, w_down
    )

    chain_down = Chain(links, sent, kept, True)
    token = chain_down.cross()
    ub, up_sum, sent, kept = back_down(coords, tie(fb, *token), n1t, slope, w_down)
    ub, sent = meet([chain_down], ub, sent)
    chain_up = Chain(links, sent, kept, True)
    token = chain_down.first() + chain_up.cross()
    back, ob, sums_one, out_product = back_up(
        coords, tie(ub, *token), fb, z1, r1, vecs, mixed_t, w_up, w_out
    )
    (ob,) = meet([chain_down, chain_up], ob)
    token = chain_down.second() + chain_up.first()
    grad_packed, grad_scores, sent, kept = attend_back(
        coords, packed, probs, mixed, tie(ob, *token), tokens_t, out_product, size
    )
    sent, grad_scores, grad_packed = meet([chain_down, chain_up], sent, grad_scores, grad_packed)
    chain_qkv = Chain(links, sent, kept, False)
    token = chain_down.third() + chain_up.second() + chain_qkv.cross()
    table_one = table_grad(ids, tie(grad_scores, *token), entries, 0, 2)
    (table_one,) = meet([chain_down, chain_up, chain_qkv], table_one)
    token = chain_down.middle() + chain_up.third() + chain_qkv.first()
    table_two = table_grad(ids, tie(grad_scores, table_one, *token), entries, 1, 2)
    (table_two,) = meet([chain_down, chain_up, chain_qkv], table_two)
    token = chain_down.fourth() + chain_up.middle() + chain_qkv.second()
    counts = (3, 3, wide // model)
    tokens_grad, packed_sums = inputs_grad(
        coords,
        tie(grad_packed, table_two, *token),
        back,
        (sums_one, sums_two, up_sum),
        counts,
        (table_one, table_two),
        heads,
        w_qkv,
    )
    (packed_sums,) = meet([chain_down, chain_up, chain_qkv], packed_sums)
    sums = Sums(links, packed_sums)
    chain_down.fifth()
    chain_up.fourth()
    chain_qkv.third()
    sums.step("shard")
    meet([sums])
    sums.step("core")
    meet([chain_down, chain_up, chain_qkv, sums])
    chain_down.sixth()
    chain_up.fifth()
    chain_qkv.fourth()
    sums.step("near")
    meet([chain_down, sums])
    (g_down,) = chain_down.done((model,))
    (g_down,) = meet([chain_up, chain_qkv], g_down)
    chain_qkv.fifth()
    chain_up.sixth()
    sums.step("far")
    meet([chain_up])
    (g_up,) = chain_up.done((wide,))
    (g_up,) = meet([chain_qkv, sums], g_up)
    sums.settle()
    chain_qkv.sixth()
    g_out, g_qkv = chain_qkv.done((model, 3 * model))

    total = sums.total
    place = links.shard.at

    def piece(row):
        return lax.dynamic_slice(total, (row, place * part), (1, part)).reshape(part)

    g_out_bias, g_gain_one, g_shift_one = [piece(row) for row in range(3)]
    g_down_bias, g_gain_two, g_shift_two = [piece(row) for row in range(3, 6)]
    row = 6 + wide // model
    up_flat = total[6:row].reshape(wide)
    g_up_bias = lax.dynamic_slice_in_dim(up_flat, place * up_bias.size, up_bias.size)
    g_query_bias = piece(row)
    g_value_bias = piece(row + 2)
    count = -(-heads // (model // WIDE))
    g_table = lax.dynamic_slice_in_dim(
        total[row + 3 : row + 3 + count].reshape(-1, WIDE)[:heads],
        place * bias_table.shape[0],
        bias_table.shape[0],
        1,
    ).T
    return (
        output,
        tokens_grad,
        g_qkv,
        g_query_bias,
        g_value_bias,
        g_out,
        g_out_bias,
        g_table,
        g_gain_one,
        g_shift_one,
        g_up,
        g_up_bias,
        g_down,
        g_down_bias,
        g_gain_two,
        g_shift_two,
    )


def solution(mesh):
    rows = P(("dp", "fsdp"), None)
    mat = P("fsdp", None)
    vec = P("fsdp")
    return jax.shard_map(
        functools.partial(per_device, mesh.shape["dp"], mesh.shape["fsdp"]),
        mesh=mesh,
        in_specs=(
            rows,
            P(("dp", "fsdp")),
            P(("dp", "fsdp"), None, None, None),
            mat,
            vec,
            vec,
            mat,
            vec,
            mat,
            vec,
            vec,
            mat,
            vec,
            mat,
            vec,
            vec,
            vec,
            rows,
        ),
        out_specs=(
            rows,
            rows,
            mat,
            vec,
            vec,
            mat,
            vec,
            mat,
            vec,
            vec,
            mat,
            vec,
            mat,
            vec,
            vec,
            vec,
        ),
        check_vma=False,
    )
```

```python
import functools

import jax
import jax.numpy as jnp
from jax import lax
from jax.experimental import pallas as pl
from jax.experimental.pallas import tpu as pltpu
from jax.sharding import PartitionSpec as P

EPSILON = 1e-05
MASKED = -1000000000.0
BF = jnp.bfloat16
F32 = jnp.float32
NN = (((1,), (0,)), ((), ()))
NT = (((1,), (1,)), ((), ()))
TN = (((0,), (0,)), ((), ()))
WIDE = 128
ANY = pl.BlockSpec(memory_space=pl.ANY)
SMEM = pl.BlockSpec(memory_space=pltpu.SMEM)
VMEM = pl.BlockSpec(memory_space=pltpu.VMEM)


def dg(left, right, dims):
    return lax.dot_general(left, right, dims, preferred_element_type=F32)


def params(mebibytes):
    return pltpu.CompilerParams(vmem_limit_bytes=mebibytes * 2**20)


def cost(micros):
    return pl.CostEstimate(flops=0, bytes_accessed=int(micros * 3e6), transcendentals=0)


def shaped(shape, dtype):
    return jax.ShapeDtypeStruct(shape, dtype)


def onehot_rows(ids, oh_ref, bucket_count):
    length = ids[0].shape[1]
    sub = lax.broadcasted_iota(jnp.int32, (16, length), 0)
    one = jnp.ones((16, length), BF)
    zero = jnp.zeros((16, length), BF)
    half = bucket_count // 2
    for kind in range(3):
        both = jnp.concatenate([ids[kind], ids[kind]], axis=0).astype(BF)
        for pair in range(half):
            level = jnp.where(sub < 8, 2 * pair, 2 * pair + 1).astype(F32).astype(BF)
            oh_ref[pl.ds((kind * half + pair) * 16, 16), :] = jnp.where(both == level, one, zero)


def iota2(shape, dim):
    return lax.broadcasted_iota(jnp.int32, shape, dim)


def bias_kernel(len_ref, ids_ref, table_ref, *rest, first):
    out_ref, turned_ref, spread_ref, held_ref, oh_ref = rest[-5:]
    step0 = pl.program_id(0)
    block = step0 + first
    heads, rows, length = out_ref.shape
    entries = table_ref.shape[0]
    valid = len_ref[0]

    @pl.when(step0 == 0)
    def _():
        pick_head = (iota2((heads * 8, heads), 0) >> 3) == iota2((heads * 8, heads), 1)
        rows_of = dg(pick_head.astype(F32).astype(BF), table_ref[...], NT).astype(BF)
        shape = (entries, entries * 8)
        pick_entry = iota2(shape, 0) == (iota2(shape, 1) >> 3)
        wide = dg(rows_of, pick_entry.astype(F32).astype(BF), NN)
        shape = (heads * 8, entries * 8)
        same = (iota2(shape, 0) & 7) == (iota2(shape, 1) & 7)
        spread_ref[...] = jnp.where(same, wide, 0.0).astype(BF)

    for kind in range(3):
        turned = ids_ref[0, kind].astype(F32).T
        held_ref[kind] = turned
        turned_ref[kind] = turned.astype(BF)

    def body(step, carry):
        parts = []
        for u in range(2):
            group = pl.ds(pl.multiple_of(step * 16 + u * 8, 8), 8)
            onehot_rows([held_ref[kind, group, :] for kind in range(3)], oh_ref.at[u], entries // 3)
            parts.append(dg(spread_ref[...], oh_ref[u], NN).reshape(heads, 8, length))
        bias = jnp.concatenate(parts, axis=1)
        key = iota2((1, 16, length), 1) + (block * rows + step * 16)
        out_ref[:, pl.ds(pl.multiple_of(step * 16, 16), 16), :] = jnp.where(
            key < valid, bias, MASKED
        ).astype(BF)
        return carry

    lax.fori_loop(0, rows // 16, body, 0, unroll=4)


def bias_scores(buckets, valid, table, first, steps, before=None, rows=128):
    length = buckets.shape[-1]
    entries, heads = table.shape
    held = () if before is None else tuple(before)
    return pl.pallas_call(
        functools.partial(bias_kernel, first=first),
        grid=(steps,),
        in_specs=[
            SMEM,
            pl.BlockSpec((1, 3, length, rows), lambda i: (0, 0, 0, first + i)),
            pl.BlockSpec((entries, heads), lambda i: (0, 0)),
        ]
        + [ANY] * len(held),
        out_specs=[
            pl.BlockSpec((heads, rows, length), lambda i: (0, first + i, 0)),
            pl.BlockSpec((3, rows, length), lambda i: (0, first + i, 0)),
        ],
        out_shape=[shaped((heads, length, length), BF), shaped((3, length, length), BF)],
        scratch_shapes=[
            pltpu.VMEM((heads * 8, entries * 8), BF),
            pltpu.VMEM((3, rows, length), F32),
            pltpu.VMEM((2, entries * 8, length), BF),
        ],
        input_output_aliases={3: 0, 4: 1} if held else {},
        compiler_params=params(56),
        cost_estimate=cost(8),
        name="bias_scores",
    )(valid, buckets, table, *held)


def table_kernel(ids_ref, grad_ref, out_ref, acc_ref, oh_ref):
    heads, rows, length = grad_ref.shape
    entries = out_ref.shape[1]

    @pl.when(pl.program_id(0) == 0)
    def _():
        acc_ref[...] = jnp.zeros_like(acc_ref)

    def body(step, carry):
        tile = pl.ds(pl.multiple_of(step * 16, 16), 16)
        grads = grad_ref[:, tile, :].astype(F32)
        ids = [ids_ref[kind, tile, :].astype(F32) for kind in range(3)]
        total = None
        for u in range(2):
            part = slice(u * 8, (u + 1) * 8)
            onehot_rows([item[part] for item in ids], oh_ref.at[u], entries // 3)
            part = dg(oh_ref[u], grads[:, part, :].reshape(heads * 8, length).astype(BF), NT)
            total = part if total is None else total + part
        acc_ref[...] += total
        return carry

    lax.fori_loop(0, rows // 16, body, 0, unroll=4)

    @pl.when(pl.program_id(0) == pl.num_programs(0) - 1)
    def _():
        shape = acc_ref.shape
        same = (iota2(shape, 0) & 7) == (iota2(shape, 1) & 7)
        kept = jnp.where(same, acc_ref[...], 0.0)
        rows_in = kept.reshape(entries, 8, heads * 8).sum(axis=1)
        shape = (out_ref.shape[0], heads * 8)
        fold = (iota2(shape, 0) == (iota2(shape, 1) >> 3)).astype(F32)
        out_ref[...] = lax.dot_general(
            fold, rows_in, NT, precision=lax.Precision.HIGHEST, preferred_element_type=F32
        )


def table_grad(ids, grads, entries, part, parts, rows=64):
    heads, length, _ = grads.shape
    padded = -(-heads // 8) * 8
    steps = length // rows // parts
    first = part * steps
    return pl.pallas_call(
        table_kernel,
        grid=(steps,),
        in_specs=[
            pl.BlockSpec((3, rows, length), lambda i: (0, first + i, 0)),
            pl.BlockSpec((heads, rows, length), lambda i: (0, first + i, 0)),
        ],
        out_specs=pl.BlockSpec((padded, entries), lambda i: (0, 0)),
        out_shape=shaped((padded, entries), F32),
        scratch_shapes=[
            pltpu.VMEM((entries * 8, heads * 8), F32),
            pltpu.VMEM((2, entries * 8, length), BF),
        ],
        compiler_params=params(30),
        cost_estimate=cost(9.5),
        name="table_grad",
    )(ids, grads)


class Place:
    def __init__(
        self, rows, blocks, begin=0, shard=0, unit=0, core=0, mate=0, which=None, columns=None
    ):
        self.rows = rows
        self.blocks = blocks
        self.begin = begin
        self.shard = shard
        self.unit = unit
        self.core = core
        self.mate = mate
        self.which = which
        self.columns = columns

    def row(self, coords_ref):
        def at(index, step, size):
            return lax.rem(coords_ref[index] + step % size, size)

        row = at(3, self.shard, self.blocks) * self.rows + self.begin
        if not self.unit:
            return row
        spot = at(0, self.core, 2)
        if self.which is not None:
            spot = spot * 2 + at(self.which, self.mate, 2)
        return row + spot * self.unit


class Weight:
    def __init__(self, pieces, places, shape):
        self.pieces = pieces
        self.places = places
        self.shape = shape
        self.count = len(pieces)


def start_fetch(refs, places, coords_ref, whole_ref, sem_ref, first=0):
    copies = []
    for index, ref in enumerate(refs):
        begin = pl.multiple_of(places[index].row(coords_ref), 16)
        target = whole_ref.at[pl.ds(begin, ref.shape[0])]
        if places[index].columns is not None:
            ref = ref.at[:, pl.ds(places[index].columns, whole_ref.shape[1])]
        copy = pltpu.make_async_copy(ref, target, sem_ref.at[first + index])
        copy.start()
        copies.append(copy)
    return copies


def finish(copies):
    for copy in copies:
        copy.wait()


def save_halves(core_ref, whole_ref, sent_ref, kept_ref, sem_ref, first, begin=0):
    columns = whole_ref.shape[1] // 2
    mine = core_ref[0]
    copies = []
    for index, (half, ref) in enumerate(((1 - mine, sent_ref), (mine, kept_ref))):
        cols = pl.ds(pl.multiple_of(half * columns, WIDE), columns)
        copy = pltpu.make_async_copy(
            whole_ref.at[:, cols], ref.at[:, pl.ds(begin, columns)], sem_ref.at[first + index]
        )
        copy.start()
        copies.append(copy)
    return copies


def attend_pair(q, k, v, bias_ref, p_ref, o_ref, ot_ref, size):
    width = q.shape[1]
    lane = iota2((1, width), 1)
    vt = v.T
    mixed = []
    for g in range(width // size):
        mine = (lane >= g * size) & (lane < (g + 1) * size)
        scores = dg(jnp.where(mine, k, jnp.zeros_like(k)), q, NT) + bias_ref[g].astype(F32)
        top = jnp.max(scores, axis=0, keepdims=True)
        shifted = jnp.exp(scores - top)
        norm = jnp.sum(shifted, axis=0, keepdims=True)
        probs = (shifted * (1.0 / norm)).astype(BF)
        p_ref[g] = probs
        mixed.append(dg(vt[g * size : (g + 1) * size], probs, NN))
    turned = jnp.concatenate(mixed, axis=0)
    ot_ref[...] = turned.astype(BF)
    o_ref[...] = turned.T.astype(BF)


def attend_first_kernel(*refs, size, places, factor):
    count = len(places)
    coords_ref, x_ref, shift_ref, bias_ref = refs[:4]
    pieces = refs[4 : 4 + count]
    qkv_ref, p_ref, o_ref, ot_ref, xt_ref, w_ref, sem_ref = refs[4 + count :]
    pair = pl.program_id(0)
    model = x_ref.shape[1]
    width = o_ref.shape[1]

    @pl.when(pair == 0)
    def _():
        copies = start_fetch(pieces, places, coords_ref, w_ref, sem_ref)
        xt_ref[...] = x_ref[...].T
        finish(copies)
        for part in range(3):
            cols = slice(part * model, (part + 1) * model)
            value = dg(x_ref[...], w_ref[:, cols], NN) + shift_ref[:, cols]
            if part == 0:
                value = value * factor
            qkv_ref[:, cols] = value.astype(BF)

    def block(part):
        return qkv_ref[:, pl.ds(pl.multiple_of(part * model + pair * width, width), width)]

    attend_pair(block(0), block(1), block(2), bias_ref, p_ref, o_ref, ot_ref, size)


def attend_rest_kernel(q_ref, k_ref, v_ref, bias_ref, _p, _o, _ot, p_ref, o_ref, ot_ref, *, size):
    attend_pair(q_ref[...], k_ref[...], v_ref[...], bias_ref, p_ref, o_ref, ot_ref, size)


def attend_first(coords, tokens, shift_row, weight, bias, size, steps):
    length, model = tokens.shape
    group = WIDE // size
    count = weight.count
    return pl.pallas_call(
        functools.partial(
            attend_first_kernel, size=size, places=weight.places, factor=size**-0.5
        ),
        grid=(steps,),
        in_specs=[
            SMEM,
            pl.BlockSpec((length, model), lambda i: (0, 0)),
            pl.BlockSpec((1, 3 * model), lambda i: (0, 0)),
            pl.BlockSpec((group, length, length), lambda i: (i, 0, 0)),
        ]
        + [ANY] * count,
        out_specs=[
            pl.BlockSpec((length, 3 * model), lambda i: (0, 0)),
            pl.BlockSpec((group, length, length), lambda i: (i, 0, 0)),
            pl.BlockSpec((length, WIDE), lambda i: (0, i)),
            pl.BlockSpec((WIDE, length), lambda i: (i, 0)),
            pl.BlockSpec((model, length), lambda i: (0, 0)),
        ],
        out_shape=[
            shaped((length, 3 * model), BF),
            shaped((model // size, length, length), BF),
            shaped((length, model), BF),
            shaped((model, length), BF),
            shaped((model, length), BF),
        ],
        scratch_shapes=[pltpu.VMEM(weight.shape, BF), pltpu.SemaphoreType.DMA((count,))],
        compiler_params=params(56),
        cost_estimate=cost(11.5),
        name="attend_first",
    )(coords, tokens, shift_row, bias, *weight.pieces)


def attend_rest(qkv, bias, probs, mixed, turned, size, first):
    length, model = mixed.shape
    group = WIDE // size
    blocks = model // WIDE
    return pl.pallas_call(
        functools.partial(attend_rest_kernel, size=size),
        grid=(blocks - first,),
        in_specs=[
            pl.BlockSpec((length, WIDE), lambda i: (0, first + i)),
            pl.BlockSpec((length, WIDE), lambda i: (0, blocks + first + i)),
            pl.BlockSpec((length, WIDE), lambda i: (0, 2 * blocks + first + i)),
            pl.BlockSpec((group, length, length), lambda i: (first + i, 0, 0)),
            ANY,
            ANY,
            ANY,
        ],
        out_specs=[
            pl.BlockSpec((group, length, length), lambda i: (first + i, 0, 0)),
            pl.BlockSpec((length, WIDE), lambda i: (0, first + i)),
            pl.BlockSpec((WIDE, length), lambda i: (first + i, 0)),
        ],
        out_shape=[
            shaped(probs.shape, BF),
            shaped(mixed.shape, BF),
            shaped(turned.shape, BF),
        ],
        input_output_aliases={4: 0, 5: 1, 6: 2},
        compiler_params=params(56),
        cost_estimate=cost(7),
        name="attend_rest",
    )(qkv, qkv, qkv, bias, probs, mixed, turned)


def attend_back_kernel(
    core_ref,
    q_ref,
    k_ref,
    v_ref,
    p_ref,
    o_ref,
    g_ref,
    xt_ref,
    prior_ref,
    out_ref,
    ds_ref,
    sent_ref,
    kept_ref,
    product_ref,
    sem_ref,
    *,
    size,
    factor,
):
    pair = pl.program_id(0)
    width = q_ref.shape[1]
    model = out_ref.shape[1] // 3
    count = width // size
    lane = iota2((1, width), 1)
    q = q_ref[...]
    v = v_ref[...]
    ob = g_ref[...]
    kt = k_ref[...].T
    product = o_ref[...].astype(F32) * ob.astype(F32)
    qs, ks, vs = [], [], []
    for g in range(count):
        mine = (lane >= g * size) & (lane < (g + 1) * size)
        spare = ((g + 1) % count) * size
        inner = jnp.sum(jnp.where(mine, product, 0.0), axis=1, keepdims=True)
        high = inner.astype(BF).astype(F32)
        extra = jnp.where(lane == spare, high, jnp.where(lane == spare + 1, inner - high, 0.0))
        minus = jnp.where((lane == spare) | (lane == spare + 1), -1.0, 0.0)
        left = jnp.where(mine, v, minus.astype(BF))
        right = jnp.where(mine, ob, extra.astype(BF))
        probs = p_ref[g]
        ds = (probs.astype(F32) * dg(left, right, NT)).astype(BF)
        ds_ref[g] = ds
        vs.append(dg(probs, ob, NN))
        ks.append(dg(ds, q, NN))
        qs.append(dg(kt[g * size : (g + 1) * size], ds, NN))

    def pick(items):
        chosen = items[0]
        for g in range(1, count):
            chosen = jnp.where(lane >= g * size, items[g], chosen)
        return chosen

    def place(start):
        return pl.ds(pl.multiple_of(start + pair * width, width), width)

    q_grad = jnp.concatenate(qs, axis=0).T.astype(BF).astype(F32) * factor
    out_ref[:, place(0)] = q_grad.astype(BF)
    out_ref[:, place(model)] = pick(ks).astype(BF)
    out_ref[:, place(2 * model)] = pick(vs).astype(BF)

    @pl.when(pair == pl.num_programs(0) - 1)
    def _():
        begin = prior_ref.shape[1] // 2
        copies = save_halves(core_ref, prior_ref, sent_ref, kept_ref, sem_ref, 0)
        for part in range(3):
            cols = slice(part * model, (part + 1) * model)
            product_ref[:, cols] = dg(xt_ref[...], out_ref[:, cols], NN).astype(BF)
        copies += save_halves(core_ref, product_ref, sent_ref, kept_ref, sem_ref, 2, begin)
        finish(copies)


def attend_back(core, qkv, probs, mixed, grad_mixed, turned, prior, size):
    length = qkv.shape[0]
    model = qkv.shape[1] // 3
    blocks = model // WIDE
    group = WIDE // size
    halves = shaped((model, (prior.shape[1] + 3 * model) // 2), BF)
    return pl.pallas_call(
        functools.partial(attend_back_kernel, size=size, factor=size**-0.5),
        grid=(blocks,),
        in_specs=[
            SMEM,
            pl.BlockSpec((length, WIDE), lambda i: (0, i)),
            pl.BlockSpec((length, WIDE), lambda i: (0, blocks + i)),
            pl.BlockSpec((length, WIDE), lambda i: (0, 2 * blocks + i)),
            pl.BlockSpec((group, length, length), lambda i: (i, 0, 0)),
            pl.BlockSpec((length, WIDE), lambda i: (0, i)),
            pl.BlockSpec((length, WIDE), lambda i: (0, i)),
            pl.BlockSpec((model, length), lambda i: (0, 0)),
            pl.BlockSpec(prior.shape, lambda i: (0, 0)),
        ],
        out_specs=[
            pl.BlockSpec((length, 3 * model), lambda i: (0, 0)),
            pl.BlockSpec((group, length, length), lambda i: (i, 0, 0)),
            ANY,
            ANY,
        ],
        out_shape=[
            shaped((length, 3 * model), BF),
            shaped((model // size, length, length), BF),
            halves,
            halves,
        ],
        scratch_shapes=[
            pltpu.VMEM((model, 3 * model), BF),
            pltpu.SemaphoreType.DMA((4,)),
        ],
        compiler_params=params(30),
        cost_estimate=cost(17),
        name="attend_back",
    )(core, qkv, qkv, qkv, probs, mixed, grad_mixed, turned, prior)


def norm_forward(inputs, gain_vec, shift_vec):
    center = inputs - jnp.mean(inputs, axis=-1, keepdims=True)
    inverse = lax.rsqrt(jnp.mean(center * center, axis=-1, keepdims=True) + EPSILON)
    scaled = center * inverse
    return (scaled * gain_vec + shift_vec, scaled, inverse)


def norm_backward(grad_in, scaled, inverse, gain_vec):
    inner_term = grad_in * gain_vec
    centered = inner_term - jnp.mean(inner_term, axis=-1, keepdims=True)
    return inverse * (centered - scaled * jnp.mean(inner_term * scaled, axis=-1, keepdims=True))


def gelu_pair(u):
    square = jnp.exp(u * u * -0.5)
    t = 1.0 / (1.0 + jnp.abs(u) * (0.3275911 * 0.7071067811865476))
    poly = t * (
        0.254829592
        + t * (-0.284496736 + t * (1.421413741 + t * (-1.453152027 + t * 1.061405429)))
    )
    tail = 0.5 * poly * square
    below = jnp.where(u >= 0.0, 1.0 - tail, tail)
    return u * below, below + u * (square * 0.3989422804014327)


def column_sum(values):
    return jnp.sum(values, axis=0, keepdims=True)


OUT_B, GAIN1, SHIFT1, DOWN_B, GAIN2, SHIFT2 = range(2, 8)


def up_kernel(*refs, out_places, up_places, chunk):
    outs, ups = len(out_places), len(up_places)
    coords_ref, mixed_ref, x_ref, vec_ref, upb_ref = refs[:5]
    out_pieces = refs[5 : 5 + outs]
    up_pieces = refs[5 + outs : 5 + outs + ups]
    (
        n1t_out,
        z1_out,
        r1_ref,
        hidden_out,
        turned_out,
        slope_out,
        w_out,
        w_up,
        n1t,
        z1_low,
        hidden,
        turned,
        slope,
        sem_ref,
        save_sem,
    ) = refs[5 + outs + ups :]
    first = start_fetch(out_pieces, out_places, coords_ref, w_out, sem_ref)
    second = start_fetch(up_pieces, up_places, coords_ref, w_up, sem_ref, outs)

    def vec(row):
        return vec_ref[row : row + 1, :]

    finish(first)
    summed = x_ref[...].astype(F32) + (dg(mixed_ref[...], w_out[...], NN) + vec(OUT_B))
    n1, z1, r1 = norm_forward(summed, vec(GAIN1), vec(SHIFT1))
    low = n1.astype(BF)
    n1t[...] = low.T
    z1_low[...] = z1.astype(BF)
    r1_ref[...] = r1
    saves = [
        pltpu.make_async_copy(n1t, n1t_out, save_sem.at[0]),
        pltpu.make_async_copy(z1_low, z1_out, save_sem.at[1]),
    ]
    for save in saves:
        save.start()
    finish(second)
    for index, begin in enumerate(range(0, hidden.shape[1], chunk)):
        cols = slice(begin, begin + chunk)
        h, s = gelu_pair(dg(low, w_up[:, cols], NN) + upb_ref[:, cols])
        h = h.astype(BF)
        hidden[:, cols] = h
        turned[cols, :] = h.T
        slope[:, cols] = s.astype(BF)
        part = pl.ds(begin, chunk)
        for kind, (left, right) in enumerate(
            (
                (hidden.at[:, part], hidden_out.at[:, part]),
                (turned.at[part, :], turned_out.at[part, :]),
                (slope.at[:, part], slope_out.at[:, part]),
            )
        ):
            save = pltpu.make_async_copy(left, right, save_sem.at[2 + index * 3 + kind])
            save.start()
            saves.append(save)
    finish(saves)


def go_up(coords, mixed, tokens, vecs, up_bias, w_out, w_up, chunk=512):
    length, model = tokens.shape
    wide = up_bias.shape[1]
    return pl.pallas_call(
        functools.partial(
            up_kernel, out_places=w_out.places, up_places=w_up.places, chunk=chunk
        ),
        in_specs=[SMEM] + [VMEM] * 4 + [ANY] * (w_out.count + w_up.count),
        out_specs=[ANY] * 2 + [VMEM] + [ANY] * 3,
        out_shape=[
            shaped((model, length), BF),
            shaped((length, model), BF),
            shaped((length, 1), F32),
            shaped((length, wide), BF),
            shaped((wide, length), BF),
            shaped((length, wide), BF),
        ],
        scratch_shapes=[
            pltpu.VMEM(w_out.shape, BF),
            pltpu.VMEM(w_up.shape, BF),
            pltpu.VMEM((model, length), BF),
            pltpu.VMEM((length, model), BF),
            pltpu.VMEM((length, wide), BF),
            pltpu.VMEM((wide, length), BF),
            pltpu.VMEM((length, wide), BF),
            pltpu.SemaphoreType.DMA((w_out.count + w_up.count,)),
            pltpu.SemaphoreType.DMA((2 + 3 * (wide // chunk),)),
        ],
        compiler_params=params(56),
        cost_estimate=cost(14.5),
        name="go_up",
    )(coords, mixed, tokens, vecs, up_bias, *w_out.pieces, *w_up.pieces)


def down_kernel(*refs, places, chunk):
    count = len(places)
    coords_ref, len_ref, z1_ref, vec_ref, cot_in, hidden_in, turned_in = refs[:7]
    pieces = refs[7 : 7 + count]
    (
        y_out,
        fb_out,
        sums_ref,
        sent_ref,
        kept_ref,
        w_ref,
        cot,
        y_low,
        fb_low,
        hidden,
        turned,
        product_ref,
        sem_ref,
        own_sem,
    ) = refs[7 + count :]
    load = pltpu.make_async_copy(hidden_in, hidden, own_sem.at[0])
    load.start()
    copies = start_fetch(pieces, places, coords_ref, w_ref, sem_ref)
    load_cot = pltpu.make_async_copy(cot_in, cot, own_sem.at[2])
    load_cot.start()
    load_turned = pltpu.make_async_copy(turned_in, turned, own_sem.at[1])
    load_turned.start()

    def vec(row):
        return vec_ref[row : row + 1, :]

    n1 = z1_ref[...].astype(F32) * vec(GAIN1) + vec(SHIFT1)
    load.wait()
    finish(copies)
    n2, z2, r2 = norm_forward(
        n1 + (dg(hidden[...], w_ref[...], NN) + vec(DOWN_B)), vec(GAIN2), vec(SHIFT2)
    )
    rows = z1_ref.shape[0]
    valid = (iota2((rows, 1), 0) < len_ref[0]).astype(F32)
    y_low[...] = (n2 * valid).astype(BF)
    load_cot.wait()
    g2 = cot[...].astype(F32) * valid
    back = norm_backward(g2, z2, r2, vec(GAIN2))
    fb = back.astype(BF)
    fb_low[...] = fb
    saves = [
        pltpu.make_async_copy(y_low, y_out, own_sem.at[3]),
        pltpu.make_async_copy(fb_low, fb_out, own_sem.at[4]),
    ]
    for save in saves:
        save.start()
    sums_ref[...] = jnp.concatenate(
        [column_sum(fb.astype(F32)), column_sum(g2 * z2), column_sum(g2)]
        + [jnp.zeros((5, z1_ref.shape[1]), F32)],
        axis=0,
    )
    load_turned.wait()
    for index, begin in enumerate(range(0, turned.shape[0], chunk)):
        part = pl.ds(begin, chunk)
        product_ref[part, :] = dg(turned[part, :], fb, NN).astype(BF)
        saves += save_halves(
            coords_ref, product_ref.at[part], sent_ref.at[part], kept_ref.at[part], own_sem, 5 + 2 * index
        )
    finish(saves)


def go_down(coords, lengths, z1, cotangent, vecs, hidden, turned, weight, chunk=1024):
    length, model = z1.shape
    wide = hidden.shape[1]
    return pl.pallas_call(
        functools.partial(down_kernel, places=weight.places, chunk=chunk),
        in_specs=[SMEM] * 2 + [VMEM] * 2 + [ANY] * (3 + weight.count),
        out_specs=[ANY] * 2 + [VMEM] + [ANY] * 2,
        out_shape=[
            shaped((length, model), BF),
            shaped((length, model), BF),
            shaped((8, model), F32),
            shaped((wide, model // 2), BF),
            shaped((wide, model // 2), BF),
        ],
        scratch_shapes=[
            pltpu.VMEM(weight.shape, BF),
            pltpu.VMEM((length, model), BF),
            pltpu.VMEM((length, model), BF),
            pltpu.VMEM((length, model), BF),
            pltpu.VMEM((length, wide), BF),
            pltpu.VMEM((wide, length), BF),
            pltpu.VMEM((wide, model), BF),
            pltpu.SemaphoreType.DMA((weight.count,)),
            pltpu.SemaphoreType.DMA((5 + 2 * (wide // chunk),)),
        ],
        compiler_params=params(56),
        cost_estimate=cost(16),
        name="go_down",
    )(coords, lengths, z1, vecs, cotangent, hidden, turned, *weight.pieces)


def back_down_kernel(*refs, places, chunk):
    count = len(places)
    coords_ref, fb_ref, n1t_ref, slope_in = refs[:4]
    pieces = refs[4 : 4 + count]
    ub_out, upsum_ref, sent_ref, kept_ref, w_ref, slope, product_ref, sem_ref, own_sem = refs[
        4 + count :
    ]
    load = pltpu.make_async_copy(slope_in, slope, own_sem.at[0])
    copies = start_fetch(pieces, places, coords_ref, w_ref, sem_ref)
    load.start()
    fb = fb_ref[...]
    n1t = n1t_ref[...]
    upsum_ref[...] = jnp.zeros_like(upsum_ref)
    finish(copies)
    load.wait()
    saves = []
    for index, begin in enumerate(range(0, slope.shape[1], chunk)):
        cols = slice(begin, begin + chunk)
        ub = (slope[:, cols].astype(F32) * dg(fb, w_ref[cols, :], NT)).astype(BF)
        slope[:, cols] = ub
        upsum_ref[index : index + 1, :] = column_sum(ub.astype(F32))
        save = pltpu.make_async_copy(
            slope.at[:, pl.ds(begin, chunk)], ub_out.at[:, pl.ds(begin, chunk)], own_sem.at[3 + index]
        )
        save.start()
        saves.append(save)
        product_ref[:, cols] = dg(n1t, ub, NN).astype(BF)
    saves += save_halves(coords_ref, product_ref, sent_ref, kept_ref, own_sem, 1)
    finish(saves)


def back_down(coords, fb, n1t, slope, weight):
    length, model = fb.shape
    wide = slope.shape[1]
    chunk = model
    return pl.pallas_call(
        functools.partial(back_down_kernel, places=weight.places, chunk=chunk),
        in_specs=[SMEM] + [VMEM] * 2 + [ANY] * (1 + weight.count),
        out_specs=[ANY, VMEM, ANY, ANY],
        out_shape=[
            shaped((length, wide), BF),
            shaped((8, model), F32),
            shaped((model, wide // 2), BF),
            shaped((model, wide // 2), BF),
        ],
        scratch_shapes=[
            pltpu.VMEM(weight.shape, BF),
            pltpu.VMEM((length, wide), BF),
            pltpu.VMEM((model, wide), BF),
            pltpu.SemaphoreType.DMA((weight.count,)),
            pltpu.SemaphoreType.DMA((3 + wide // chunk,)),
        ],
        compiler_params=params(56),
        cost_estimate=cost(13.5),
        name="back_down",
    )(coords, fb, n1t, slope, *weight.pieces)


def back_up_kernel(*refs, up_places, out_places):
    ups, outs = len(up_places), len(out_places)
    coords_ref, fb_ref, r1_ref, vec_ref, z1_in, ot_in, ub_in = refs[:7]
    up_pieces = refs[7 : 7 + ups]
    out_pieces = refs[7 + ups : 7 + ups + outs]
    (
        ab_out,
        ob_out,
        sums_ref,
        product_ref,
        w_up,
        w_out,
        ub,
        z1_low,
        ot,
        ab_low,
        ob_low,
        sem_ref,
        own_sem,
    ) = refs[7 + ups + outs :]
    load = pltpu.make_async_copy(ub_in, ub, own_sem.at[0])
    load.start()
    second = start_fetch(up_pieces, up_places, coords_ref, w_up, sem_ref)
    load_z1 = pltpu.make_async_copy(z1_in, z1_low, own_sem.at[1])
    load_z1.start()
    first = start_fetch(out_pieces, out_places, coords_ref, w_out, sem_ref, ups)
    load_ot = pltpu.make_async_copy(ot_in, ot, own_sem.at[2])
    load_ot.start()
    load.wait()
    finish(second)
    n1b = fb_ref[...].astype(F32) + dg(ub[...], w_up[...], NT)
    load_z1.wait()
    z1 = z1_low[...].astype(F32)
    back = norm_backward(n1b, z1, r1_ref[...], vec_ref[GAIN1 : GAIN1 + 1, :])
    ab = back.astype(BF)
    ab_low[...] = ab
    save_ab = pltpu.make_async_copy(ab_low, ab_out, own_sem.at[3])
    save_ab.start()
    sums_ref[...] = jnp.concatenate(
        [column_sum(ab.astype(F32)), column_sum(n1b * z1), column_sum(n1b)]
        + [jnp.zeros((5, z1.shape[1]), F32)],
        axis=0,
    )
    finish(first)
    ob_low[...] = dg(ab, w_out[...], NT).astype(BF)
    save_ob = pltpu.make_async_copy(ob_low, ob_out, own_sem.at[4])
    save_ob.start()
    load_ot.wait()
    product_ref[...] = dg(ot[...], ab, NN).astype(BF)
    save_ab.wait()
    save_ob.wait()


def back_up(coords, ub, fb, z1, r1, vecs, turned, w_up, w_out):
    length, model = fb.shape
    wide = ub.shape[1]
    return pl.pallas_call(
        functools.partial(back_up_kernel, up_places=w_up.places, out_places=w_out.places),
        in_specs=[SMEM] + [VMEM] * 3 + [ANY] * (3 + w_up.count + w_out.count),
        out_specs=[ANY] * 2 + [VMEM] * 2,
        out_shape=[
            shaped((length, model), BF),
            shaped((length, model), BF),
            shaped((8, model), F32),
            shaped((model, model), BF),
        ],
        scratch_shapes=[
            pltpu.VMEM(w_up.shape, BF),
            pltpu.VMEM(w_out.shape, BF),
            pltpu.VMEM((length, wide), BF),
            pltpu.VMEM((length, model), BF),
            pltpu.VMEM((model, length), BF),
            pltpu.VMEM((length, model), BF),
            pltpu.VMEM((length, model), BF),
            pltpu.SemaphoreType.DMA((w_up.count + w_out.count,)),
            pltpu.SemaphoreType.DMA((5,)),
        ],
        compiler_params=params(56),
        cost_estimate=cost(13.5),
        name="back_up",
    )(coords, fb, r1, vecs, z1, turned, ub, *w_up.pieces, *w_out.pieces)


def inputs_kernel(*refs, places, counts):
    count = len(places)
    coords_ref, pb_ref, back_ref = refs[:3]
    vectors = refs[3 : 3 + len(counts)]
    tables = refs[3 + len(counts) : 5 + len(counts)]
    pieces = refs[5 + len(counts) : 5 + len(counts) + count]
    out_ref, sums_ref, w_ref, sem_ref = refs[5 + len(counts) + count :]
    copies = start_fetch(pieces, places, coords_ref, w_ref, sem_ref)
    pb = pb_ref[...]
    flat = column_sum(pb.astype(F32))
    model = out_ref.shape[1]
    sums_ref[...] = jnp.zeros_like(sums_ref)
    begin = 0
    for rows, ref in zip(counts, vectors):
        sums_ref[begin : begin + rows, :] = ref[:rows, :]
        begin += rows
    for part in range(3):
        sums_ref[begin : begin + 1, :] = flat[:, part * model : (part + 1) * model]
        begin += 1
    table = tables[0][...] + tables[1][...]
    for head in range(table.shape[0]):
        row = begin + head // (model // WIDE)
        lane = head % (model // WIDE) * WIDE
        if row < sums_ref.shape[0]:
            sums_ref[row : row + 1, lane : lane + table.shape[1]] = table[head : head + 1, :]
    finish(copies)
    out_ref[...] = (back_ref[...].astype(F32) + dg(pb, w_ref[...], NT)).astype(BF)


def inputs_grad(coords, grad_packed, back, vectors, counts, tables, heads, weight):
    length, model = back.shape
    count = weight.count
    rows = sum(counts) + 3 + -(-heads // (model // WIDE))
    rows = -(-rows // 8) * 8
    return pl.pallas_call(
        functools.partial(inputs_kernel, places=weight.places, counts=counts),
        in_specs=[SMEM] + [VMEM] * (4 + len(counts)) + [ANY] * count,
        out_specs=[VMEM] * 2,
        out_shape=[shaped((length, model), BF), shaped((rows, model), F32)],
        scratch_shapes=[
            pltpu.VMEM(weight.shape, BF),
            pltpu.SemaphoreType.DMA((count,)),
        ],
        compiler_params=params(56),
        cost_estimate=cost(7),
        name="inputs_grad",
    )(coords, grad_packed, back, *vectors, *tables, *weight.pieces)


def finish_kernel(at_ref, mine_ref, theirs_ref, *out_refs):
    first = at_ref[0] == 0
    begin = 0
    for out_ref in out_refs:
        columns = out_ref.shape[1] // 2
        mine = mine_ref[:, begin : begin + columns]
        theirs = theirs_ref[:, begin : begin + columns]
        out_ref[:, :columns] = jnp.where(first, mine, theirs).astype(F32)
        out_ref[:, columns:] = jnp.where(first, theirs, mine).astype(F32)
        begin += columns


def finish_pair(core, mine, theirs, widths):
    rows, columns = mine.shape
    step = rows // 4 if (rows // 4) % 16 == 0 else rows
    spec = pl.BlockSpec((step, columns), lambda i: (i, 0))
    return pl.pallas_call(
        finish_kernel,
        grid=(rows // step,),
        in_specs=[SMEM, spec, spec],
        out_specs=[pl.BlockSpec((step, width), lambda i: (i, 0)) for width in widths],
        out_shape=[shaped((rows, width), F32) for width in widths],
        compiler_params=params(16),
        cost_estimate=cost(4.4),
        name="finish_pair",
    )(core, mine, theirs)


class Axis:
    def __init__(self, name, total, stride, size):
        self.name = name
        self.total = total
        self.stride = stride
        self.size = size
        self.at = (lax.axis_index(name) // stride) % size

    def send(self, value, step):
        pairs = []
        for index in range(self.total):
            place = (index // self.stride) % self.size
            pairs.append((index, index + ((place + step) % self.size - place) * self.stride))
        return lax.ppermute(value, self.name, pairs)

    def peer(self, step):
        return (self.at + step) % self.size


def tie(value, *others):
    if not others:
        return value
    return lax.optimization_barrier((value,) + others)[0]


def take(stack, index, dim=0):
    return lax.dynamic_index_in_dim(stack, index, axis=dim, keepdims=False)


def arrange(axis, block, got, dim=0):
    if axis.size == 1:
        return jnp.expand_dims(block, dim)
    shape = [1] * (block.ndim + 1)
    shape[dim] = axis.size
    place = jnp.arange(axis.size, dtype=jnp.int32).reshape(shape)
    stack = jnp.expand_dims(block, dim)
    for step, value in enumerate(got):
        stack = jnp.where(place == axis.peer(-1 - step), jnp.expand_dims(value, dim), stack)
    return stack


def send_all(axis, block):
    return [axis.send(block, step) for step in range(1, axis.size)]


class Links:
    def __init__(self, dp, fsdp):
        core = 2
        rest = dp // core
        near = 2 if rest % 2 == 0 else 1
        self.core = Axis("dp", dp, 1, core)
        self.near = Axis("dp", dp, core, near)
        self.far = Axis("dp", dp, core * near, rest // near)
        self.pair = Axis("dp", dp, core * near, 2 if (rest // near) % 2 == 0 else 1)
        self.shard = Axis("fsdp", fsdp, 1, fsdp)


class Portion:
    def __init__(self, links, blocks, begin, count, mate):
        self.links = links
        self.mate = mate
        self.begin = begin
        self.rows = blocks[0].shape[0]
        parts = links.core.size * (mate.size if mate else 1)
        self.unit = count // parts
        self.blocks = blocks
        self.inbox = []
        self.held = []

    def spot(self, s, t):
        core = self.links.core.peer(-s)
        return core * self.mate.size + self.mate.peer(-t) if self.mate else core

    def start(self, *after):
        begin = self.begin + self.spot(0, 0) * self.unit
        mine = [lax.dynamic_slice_in_dim(item, begin, self.unit, 0) for item in self.blocks]
        mine = tie(jnp.concatenate(mine, axis=1) if len(mine) > 1 else mine[0], *after)
        self.inbox = send_all(self.links.shard, mine)
        return [mine]

    def hop(self):
        self.got = self.inbox
        if self.mate:
            self.inbox = [self.mate.send(item, 1) for item in self.got]
        return list(self.got)

    def cross(self, *after):
        self.crossed = [self.links.core.send(tie(item, *after), 1) for item in self.got]

    def last(self):
        self.hops = self.inbox if self.mate else []
        self.inbox = [self.links.core.send(item, 1) for item in self.hops]
        return list(self.hops) + list(self.crossed)

    def pieces(self):
        shard = self.links.shard
        which = None if self.mate is None else 1 if self.mate is self.links.near else 2
        found = []
        for index in range(len(self.got)):
            group = [(self.got[index], 0, 0), (self.crossed[index], 1, 0)]
            if self.mate:
                group += [(self.hops[index], 0, 1), (self.inbox[index], 1, 1)]
            for value, s, t in group:
                found.append(
                    (value, (self.rows, shard.size, self.begin, -1 - index, self.unit, -s, -t, which))
                )
        return found


class Fetch:
    def __init__(self, links, *blocks):
        self.links = links
        self.blocks = blocks
        rows = blocks[0].shape[0]
        mates = (links.near, links.pair)
        if rows % 128 == 0 and all(mate.size == 2 for mate in mates):
            half = rows // 2
            self.parts = [
                Portion(links, blocks, index * half, half, mate) for index, mate in enumerate(mates)
            ]
        else:
            self.parts = [Portion(links, blocks, 0, rows, None)]

    def do(self, name, *after):
        found = []
        for part in self.parts:
            found += getattr(part, name)(*after) or []
        return found

    def weights(self):
        rows = self.blocks[0].shape[0]
        count = self.links.shard.size
        found = []
        for part in self.parts:
            found += part.pieces()
        done = []
        begin = 0
        for block in self.blocks:
            columns = None if len(self.blocks) == 1 else begin
            done.append(
                Weight(
                    [block] + [item for item, _ in found],
                    [Place(rows, count)] + [Place(*place, columns=columns) for _, place in found],
                    (rows * count, block.shape[1]),
                )
            )
            begin += block.shape[1]
        return done


def meet(owners, *values):
    flat = [item for owner in owners for item in owner.inbox + owner.held]
    flat = lax.optimization_barrier(tuple(flat) + tuple(values))
    begin = 0
    for owner in owners:
        count = len(owner.inbox)
        owner.inbox = list(flat[begin : begin + count])
        begin += count
        count = len(owner.held)
        owner.held = list(flat[begin : begin + count])
        begin += count
    return list(flat[begin:])


def add_up(terms):
    total = terms[0].astype(F32)
    for term in terms[1:]:
        total = total + term.astype(F32)
    return total


class Chain:
    def __init__(self, links, sent, kept, line):
        self.links = links
        self.sent = sent
        self.line = line and links.far.size == 4
        rows, columns = kept.shape
        sizes = (links.shard.size, links.near.size, links.far.size, 2)
        whole = sizes[0] * sizes[1] * sizes[2] * sizes[3]
        self.shape = sizes + (rows // whole, columns)
        self.kept = kept

    def cross(self):
        self.inbox = [self.links.core.send(self.sent, 1)]
        self.held = [self.kept]
        return [self.sent]

    def hop(self, terms, axis):
        sent = []
        for step in range(1, axis.size):
            pieces = [term(axis.peer(step)) for term in terms]
            sent.append(lax.optimization_barrier(add_up(pieces).astype(BF)))
        return [axis.send(value, step + 1) for step, value in enumerate(sent)], sent

    def piece(self, term, way, x=None, y=None):
        shard, near, far, _, rows, columns = self.shape
        begin = [0 if x is None else x, 0 if y is None else y, 0, way, 0, 0]
        sizes = [shard if x is None else 1, near if y is None else 1, far, 1, rows, columns]
        keep = [size for at, size in zip((x, y), sizes[:2]) if at is None]
        part = lax.dynamic_slice(term.reshape(self.shape), begin, sizes)
        return part.reshape(*keep, far, rows, columns)

    def first(self):
        self.held = self.held + self.inbox
        held = self.held
        a, sent_a = self.hop(
            [lambda to, f=f: self.piece(f, 0, x=to) for f in held], self.links.shard
        )
        b, sent_b = self.hop([lambda to, f=f: self.piece(f, 1, y=to) for f in held], self.links.near)
        self.inbox = a + b
        self.cut = len(a)
        return sent_a + sent_b

    def second(self):
        x, y = self.links.shard.at, self.links.near.at
        got_a, got_b = self.inbox[: self.cut], self.inbox[self.cut :]
        held = self.held[:2]
        terms = [lambda to, f=f: self.piece(f, 0, x, to) for f in held]
        terms += [lambda to, v=v: take(v, to) for v in got_a]
        a, sent_a = self.hop(terms, self.links.near)
        terms = [lambda to, f=f: self.piece(f, 1, to, y) for f in held]
        terms += [lambda to, v=v: take(v, to) for v in got_b]
        b, sent_b = self.hop(terms, self.links.shard)
        self.held = held + got_a + got_b
        self.inbox = a + b
        self.last_cut = len(a)
        return sent_a + sent_b

    def third(self):
        x, y = self.links.shard.at, self.links.near.at
        got = self.held[2:]
        halves = []
        for way, (early, at) in enumerate(((got[: self.cut], y), (got[self.cut :], x))):
            late = self.inbox[: self.last_cut] if way == 0 else self.inbox[self.last_cut :]
            own = [self.piece(f, way, x, y) for f in self.held[:2]]
            halves.append(add_up(own + [take(v, at) for v in early] + late))
        self.held = []
        self.block = lax.optimization_barrier(jnp.stack(halves, axis=1).astype(BF))
        if self.line:
            self.inbox = [self.line_send(self.block, ((0, 1), (3, 2)))]
            return [self.block]
        far = self.links.far
        self.inbox, sent = self.hop([lambda to: take(self.block, to)], far)
        self.kept_block = self.block
        return sent

    def line_send(self, value, moves):
        far = self.links.far
        pairs = []
        for index in range(far.total):
            place = (index // far.stride) % far.size
            pairs += [(index, index + (to - place) * far.stride) for at, to in moves if at == place]
        return lax.ppermute(value, far.name, pairs)

    def middle(self):
        if not self.line:
            return []
        self.block = lax.optimization_barrier(add_up([self.block] + self.inbox).astype(BF))
        self.inbox = [self.line_send(self.block, ((1, 2), (2, 1)))]
        return [self.block]

    def fourth(self):
        if self.line:
            self.block = lax.optimization_barrier(add_up([self.block] + self.inbox).astype(BF))
            self.inbox = [self.line_send(self.block, ((1, 0), (2, 3)))]
            return [self.block]
        mine = take(self.kept_block, self.links.far.at)
        self.block = lax.optimization_barrier(add_up([mine] + self.inbox).astype(BF))
        self.inbox = send_all(self.links.far, self.block)
        return [self.block]

    def fifth(self):
        far = self.links.far
        if self.line:
            outer = (far.at == 0) | (far.at == 3)
            block = jnp.where(outer, self.inbox[0], self.block)
        else:
            block = arrange(far, self.block, self.inbox)
        self.block = lax.optimization_barrier(block)
        self.inbox = send_all(self.links.near, self.block)
        return [self.block]

    def sixth(self):
        block = arrange(self.links.near, self.block, self.inbox)
        self.block = lax.optimization_barrier(block.reshape(-1, block.shape[-1]))
        self.inbox = [self.links.core.send(self.block, 1)]
        return [self.block]

    def done(self, widths):
        return finish_pair(self.links.coords, self.block, self.inbox[0], widths)


class Sums:
    def __init__(self, links, value):
        self.links = links
        self.total = value
        self.inbox = []
        self.held = []

    def step(self, name):
        self.settle()
        self.inbox = send_all(getattr(self.links, name), self.total)
        return [self.total]

    def settle(self):
        self.total = functools.reduce(jnp.add, self.inbox, self.total)
        self.inbox = []


def per_device(
    dp,
    fsdp,
    tokens,
    lengths,
    buckets,
    qkv_weight,
    q_bias,
    v_bias,
    out_weight,
    out_bias,
    bias_table,
    norm1_gain,
    norm1_bias,
    up_weight,
    up_bias,
    down_weight,
    down_bias,
    norm2_gain,
    norm2_bias,
    cotangent,
):
    links = Links(dp, fsdp)
    model = tokens.shape[1]
    wide = up_weight.shape[1]
    heads = bias_table.shape[1]
    size = model // heads
    entries = bias_table.shape[0] * fsdp
    links.coords = coords = jnp.stack(
        [links.core.at, links.near.at, links.pair.at, links.shard.at]
    ).astype(jnp.int32)

    table_got = send_all(links.shard, bias_table)
    qkv = Fetch(links, qkv_weight)
    outup = Fetch(links, out_weight, up_weight)
    down = Fetch(links, down_weight)
    token = qkv.do("start", bias_table)
    narrow = (q_bias, v_bias, out_bias, norm1_gain, norm1_bias, down_bias, norm2_gain, norm2_bias)
    narrow = lax.optimization_barrier(narrow + (up_bias,) + tuple(token))
    row = jnp.arange(8, dtype=jnp.int32)[:, None]
    rows = jnp.broadcast_to(narrow[0][None], (8, narrow[0].size))
    for index in range(1, 8):
        rows = jnp.where(row == index, narrow[index][None], rows)
    part = out_bias.size
    rows = jnp.concatenate([rows, narrow[8].reshape(-1, part)], axis=0)
    rows = lax.optimization_barrier(rows)
    rows_got = send_all(links.shard, rows)
    table = arrange(links.shard, bias_table, table_got).reshape(entries, heads)
    bias = bias_scores(tie(buckets, rows, *token), lengths, table, 0, 1)
    tied = meet(qkv.parts, bias[0], bias[1], *rows_got)
    bias, rows_got = tied[:2], tied[2:]
    token = qkv.do("hop")
    qkv.do("cross")
    token = outup.do("start", *token)
    bias = bias_scores(tie(buckets, *token), lengths, table, 1, tokens.shape[0] // 128 - 1, bias)
    bias = meet(qkv.parts + outup.parts, *bias)
    token = qkv.do("last")
    token += outup.do("hop")
    token += down.do("start", *token)
    bias, ids = bias
    every = arrange(links.shard, rows, rows_got)
    vecs = jnp.swapaxes(every[:, :8], 0, 1).reshape(8, model).astype(F32)
    up_vec = every[:, 8:].reshape(1, -1).astype(F32)
    shift_row = jnp.concatenate([vecs[0:1], jnp.zeros((1, model), F32), vecs[1:2]], axis=1)
    shift_row, up_vec = lax.optimization_barrier((shift_row, up_vec) + tuple(token))[:2]
    (w_qkv,) = qkv.weights()
    half = model // WIDE * 2 // 3
    packed, probs, mixed, mixed_t, tokens_t = attend_first(
        coords, tokens, shift_row, w_qkv, bias, size, half
    )
    (mixed_t,) = meet(outup.parts + down.parts, mixed_t)
    outup.do("cross", mixed_t)
    token = outup.do("last")
    token += down.do("hop")
    probs, mixed, mixed_t = attend_rest(
        packed, bias, tie(probs, *token), mixed, mixed_t, size, half
    )
    (mixed,) = meet(outup.parts, mixed)
    w_out, w_up = outup.weights()
    n1t, z1, r1, hidden, hidden_t, slope = go_up(
        coords, mixed, tokens, vecs, up_vec, w_out, w_up
    )
    (z1,) = meet(down.parts, z1)
    down.do("cross", z1)
    token = down.do("last")
    (w_down,) = down.weights()
    output, fb, sums_two, sent, kept = go_down(
        coords, lengths, tie(z1, *token), cotangent, vecs, hidden, hidden_t, w_down
    )

    chain_down = Chain(links, sent, kept, True)
    token = chain_down.cross()
    ub, up_sum, sent, kept = back_down(coords, tie(fb, *token), n1t, slope, w_down)
    ub, sent = meet([chain_down], ub, sent)
    chain_up = Chain(links, sent, kept, True)
    token = chain_down.first() + chain_up.cross()
    back, ob, sums_one, out_product = back_up(
        coords, tie(ub, *token), fb, z1, r1, vecs, mixed_t, w_up, w_out
    )
    (ob,) = meet([chain_down, chain_up], ob)
    token = chain_down.second() + chain_up.first()
    grad_packed, grad_scores, sent, kept = attend_back(
        coords, packed, probs, mixed, tie(ob, *token), tokens_t, out_product, size
    )
    sent, grad_scores, grad_packed = meet([chain_down, chain_up], sent, grad_scores, grad_packed)
    chain_qkv = Chain(links, sent, kept, False)
    token = chain_down.third() + chain_up.second() + chain_qkv.cross()
    table_one = table_grad(ids, tie(grad_scores, *token), entries, 0, 2)
    (table_one,) = meet([chain_down, chain_up, chain_qkv], table_one)
    token = chain_down.middle() + chain_up.third() + chain_qkv.first()
    table_two = table_grad(ids, tie(grad_scores, table_one, *token), entries, 1, 2)
    (table_two,) = meet([chain_down, chain_up, chain_qkv], table_two)
    token = chain_down.fourth() + chain_up.middle() + chain_qkv.second()
    counts = (3, 3, wide // model)
    tokens_grad, packed_sums = inputs_grad(
        coords,
        tie(grad_packed, table_two, *token),
        back,
        (sums_one, sums_two, up_sum),
        counts,
        (table_one, table_two),
        heads,
        w_qkv,
    )
    (packed_sums,) = meet([chain_down, chain_up, chain_qkv], packed_sums)
    sums = Sums(links, packed_sums)
    chain_down.fifth()
    chain_up.fourth()
    chain_qkv.third()
    sums.step("shard")
    meet([sums])
    sums.step("core")
    meet([chain_down, chain_up, chain_qkv, sums])
    chain_down.sixth()
    chain_up.fifth()
    chain_qkv.fourth()
    sums.step("near")
    meet([chain_down, sums])
    (g_down,) = chain_down.done((model,))
    (g_down,) = meet([chain_up, chain_qkv], g_down)
    chain_qkv.fifth()
    chain_up.sixth()
    sums.step("far")
    meet([chain_up])
    (g_up,) = chain_up.done((wide,))
    (g_up,) = meet([chain_qkv, sums], g_up)
    sums.settle()
    chain_qkv.sixth()
    g_out, g_qkv = chain_qkv.done((model, 3 * model))

    total = sums.total
    place = links.shard.at

    def piece(row):
        return lax.dynamic_slice(total, (row, place * part), (1, part)).reshape(part)

    g_out_bias, g_gain_one, g_shift_one = [piece(row) for row in range(3)]
    g_down_bias, g_gain_two, g_shift_two = [piece(row) for row in range(3, 6)]
    row = 6 + wide // model
    up_flat = total[6:row].reshape(wide)
    g_up_bias = lax.dynamic_slice_in_dim(up_flat, place * up_bias.size, up_bias.size)
    g_query_bias = piece(row)
    g_value_bias = piece(row + 2)
    count = -(-heads // (model // WIDE))
    g_table = lax.dynamic_slice_in_dim(
        total[row + 3 : row + 3 + count].reshape(-1, WIDE)[:heads],
        place * bias_table.shape[0],
        bias_table.shape[0],
        1,
    ).T
    return (
        output,
        tokens_grad,
        g_qkv,
        g_query_bias,
        g_value_bias,
        g_out,
        g_out_bias,
        g_table,
        g_gain_one,
        g_shift_one,
        g_up,
        g_up_bias,
        g_down,
        g_down_bias,
        g_gain_two,
        g_shift_two,
    )


def solution(mesh):
    rows = P(("dp", "fsdp"), None)
    mat = P("fsdp", None)
    vec = P("fsdp")
    return jax.shard_map(
        functools.partial(per_device, mesh.shape["dp"], mesh.shape["fsdp"]),
        mesh=mesh,
        in_specs=(
            rows,
            P(("dp", "fsdp")),
            P(("dp", "fsdp"), None, None, None),
            mat,
            vec,
            vec,
            mat,
            vec,
            mat,
            vec,
            vec,
            mat,
            vec,
            mat,
            vec,
            vec,
            vec,
            rows,
        ),
        out_specs=(
            rows,
            rows,
            mat,
            vec,
            vec,
            mat,
            vec,
            mat,
            vec,
            vec,
            mat,
            vec,
            mat,
            vec,
            vec,
            vec,
        ),
        check_vma=False,
    )
```

```python
import functools

import jax
import jax.numpy as jnp
from jax import lax
from jax.experimental import pallas as pl
from jax.experimental.pallas import tpu as pltpu
from jax.sharding import PartitionSpec as P

EPSILON = 1e-05
MASKED = -1000000000.0
BF = jnp.bfloat16
F32 = jnp.float32
NN = (((1,), (0,)), ((), ()))
NT = (((1,), (1,)), ((), ()))
TN = (((0,), (0,)), ((), ()))
WIDE = 128
ANY = pl.BlockSpec(memory_space=pl.ANY)
SMEM = pl.BlockSpec(memory_space=pltpu.SMEM)
VMEM = pl.BlockSpec(memory_space=pltpu.VMEM)


def dg(left, right, dims):
    return lax.dot_general(left, right, dims, preferred_element_type=F32)


def params(mebibytes):
    return pltpu.CompilerParams(vmem_limit_bytes=mebibytes * 2**20)


def cost(micros):
    return pl.CostEstimate(flops=0, bytes_accessed=int(micros * 3e6), transcendentals=0)


def shaped(shape, dtype):
    return jax.ShapeDtypeStruct(shape, dtype)


def onehot_rows(ids, oh_ref, bucket_count):
    length = ids[0].shape[1]
    sub = lax.broadcasted_iota(jnp.int32, (16, length), 0)
    one = jnp.ones((16, length), BF)
    zero = jnp.zeros((16, length), BF)
    half = bucket_count // 2
    for kind in range(3):
        both = jnp.concatenate([ids[kind], ids[kind]], axis=0).astype(BF)
        for pair in range(half):
            level = jnp.where(sub < 8, 2 * pair, 2 * pair + 1).astype(F32).astype(BF)
            oh_ref[pl.ds((kind * half + pair) * 16, 16), :] = jnp.where(both == level, one, zero)


def iota2(shape, dim):
    return lax.broadcasted_iota(jnp.int32, shape, dim)


def bias_kernel(len_ref, ids_ref, table_ref, *rest, first):
    out_ref, turned_ref, spread_ref, held_ref, oh_ref = rest[-5:]
    step0 = pl.program_id(0)
    block = step0 + first
    heads, rows, length = out_ref.shape
    entries = table_ref.shape[0]
    valid = len_ref[0]

    @pl.when(step0 == 0)
    def _():
        pick_head = (iota2((heads * 8, heads), 0) >> 3) == iota2((heads * 8, heads), 1)
        rows_of = dg(pick_head.astype(F32).astype(BF), table_ref[...], NT).astype(BF)
        shape = (entries, entries * 8)
        pick_entry = iota2(shape, 0) == (iota2(shape, 1) >> 3)
        wide = dg(rows_of, pick_entry.astype(F32).astype(BF), NN)
        shape = (heads * 8, entries * 8)
        same = (iota2(shape, 0) & 7) == (iota2(shape, 1) & 7)
        spread_ref[...] = jnp.where(same, wide, 0.0).astype(BF)

    for kind in range(3):
        turned = ids_ref[0, kind].astype(F32).T
        held_ref[kind] = turned
        turned_ref[kind] = turned.astype(BF)

    def body(step, carry):
        parts = []
        for u in range(2):
            group = pl.ds(pl.multiple_of(step * 16 + u * 8, 8), 8)
            onehot_rows([held_ref[kind, group, :] for kind in range(3)], oh_ref.at[u], entries // 3)
            parts.append(dg(spread_ref[...], oh_ref[u], NN).reshape(heads, 8, length))
        bias = jnp.concatenate(parts, axis=1)
        key = iota2((1, 16, length), 1) + (block * rows + step * 16)
        out_ref[:, pl.ds(pl.multiple_of(step * 16, 16), 16), :] = jnp.where(
            key < valid, bias, MASKED
        ).astype(BF)
        return carry

    lax.fori_loop(0, rows // 16, body, 0, unroll=4)


def bias_scores(buckets, valid, table, first, steps, before=None, rows=128):
    length = buckets.shape[-1]
    entries, heads = table.shape
    held = () if before is None else tuple(before)
    return pl.pallas_call(
        functools.partial(bias_kernel, first=first),
        grid=(steps,),
        in_specs=[
            SMEM,
            pl.BlockSpec((1, 3, length, rows), lambda i: (0, 0, 0, first + i)),
            pl.BlockSpec((entries, heads), lambda i: (0, 0)),
        ]
        + [ANY] * len(held),
        out_specs=[
            pl.BlockSpec((heads, rows, length), lambda i: (0, first + i, 0)),
            pl.BlockSpec((3, rows, length), lambda i: (0, first + i, 0)),
        ],
        out_shape=[shaped((heads, length, length), BF), shaped((3, length, length), BF)],
        scratch_shapes=[
            pltpu.VMEM((heads * 8, entries * 8), BF),
            pltpu.VMEM((3, rows, length), F32),
            pltpu.VMEM((2, entries * 8, length), BF),
        ],
        input_output_aliases={3: 0, 4: 1} if held else {},
        compiler_params=params(56),
        cost_estimate=cost(8),
        name="bias_scores",
    )(valid, buckets, table, *held)


def table_kernel(ids_ref, grad_ref, out_ref, acc_ref, oh_ref):
    heads, rows, length = grad_ref.shape
    entries = out_ref.shape[1]

    @pl.when(pl.program_id(0) == 0)
    def _():
        acc_ref[...] = jnp.zeros_like(acc_ref)

    def body(step, carry):
        tile = pl.ds(pl.multiple_of(step * 16, 16), 16)
        grads = grad_ref[:, tile, :].astype(F32)
        ids = [ids_ref[kind, tile, :].astype(F32) for kind in range(3)]
        total = None
        for u in range(2):
            part = slice(u * 8, (u + 1) * 8)
            onehot_rows([item[part] for item in ids], oh_ref.at[u], entries // 3)
            part = dg(oh_ref[u], grads[:, part, :].reshape(heads * 8, length).astype(BF), NT)
            total = part if total is None else total + part
        acc_ref[...] += total
        return carry

    lax.fori_loop(0, rows // 16, body, 0, unroll=4)

    @pl.when(pl.program_id(0) == pl.num_programs(0) - 1)
    def _():
        shape = acc_ref.shape
        same = (iota2(shape, 0) & 7) == (iota2(shape, 1) & 7)
        kept = jnp.where(same, acc_ref[...], 0.0)
        rows_in = kept.reshape(entries, 8, heads * 8).sum(axis=1)
        shape = (out_ref.shape[0], heads * 8)
        fold = (iota2(shape, 0) == (iota2(shape, 1) >> 3)).astype(F32)
        out_ref[...] = lax.dot_general(
            fold, rows_in, NT, precision=lax.Precision.HIGHEST, preferred_element_type=F32
        )


def table_grad(ids, grads, entries, part, parts, rows=64):
    heads, length, _ = grads.shape
    padded = -(-heads // 8) * 8
    steps = length // rows // parts
    first = part * steps
    return pl.pallas_call(
        table_kernel,
        grid=(steps,),
        in_specs=[
            pl.BlockSpec((3, rows, length), lambda i: (0, first + i, 0)),
            pl.BlockSpec((heads, rows, length), lambda i: (0, first + i, 0)),
        ],
        out_specs=pl.BlockSpec((padded, entries), lambda i: (0, 0)),
        out_shape=shaped((padded, entries), F32),
        scratch_shapes=[
            pltpu.VMEM((entries * 8, heads * 8), F32),
            pltpu.VMEM((2, entries * 8, length), BF),
        ],
        compiler_params=params(30),
        cost_estimate=cost(9.5),
        name="table_grad",
    )(ids, grads)


class Place:
    def __init__(
        self, rows, blocks, begin=0, shard=0, unit=0, core=0, mate=0, which=None, columns=None
    ):
        self.rows = rows
        self.blocks = blocks
        self.begin = begin
        self.shard = shard
        self.unit = unit
        self.core = core
        self.mate = mate
        self.which = which
        self.columns = columns

    def row(self, coords_ref):
        def at(index, step, size):
            return lax.rem(coords_ref[index] + step % size, size)

        row = at(3, self.shard, self.blocks) * self.rows + self.begin
        if not self.unit:
            return row
        spot = at(0, self.core, 2)
        if self.which is not None:
            spot = spot * 2 + at(self.which, self.mate, 2)
        return row + spot * self.unit


class Weight:
    def __init__(self, pieces, places, shape):
        self.pieces = pieces
        self.places = places
        self.shape = shape
        self.count = len(pieces)


def start_fetch(refs, places, coords_ref, whole_ref, sem_ref, first=0):
    copies = []
    for index, ref in enumerate(refs):
        begin = pl.multiple_of(places[index].row(coords_ref), 16)
        target = whole_ref.at[pl.ds(begin, ref.shape[0])]
        if places[index].columns is not None:
            ref = ref.at[:, pl.ds(places[index].columns, whole_ref.shape[1])]
        copy = pltpu.make_async_copy(ref, target, sem_ref.at[first + index])
        copy.start()
        copies.append(copy)
    return copies


def finish(copies):
    for copy in copies:
        copy.wait()


def save_halves(core_ref, whole_ref, sent_ref, kept_ref, sem_ref, first, begin=0):
    columns = whole_ref.shape[1] // 2
    mine = core_ref[0]
    copies = []
    for index, (half, ref) in enumerate(((1 - mine, sent_ref), (mine, kept_ref))):
        cols = pl.ds(pl.multiple_of(half * columns, WIDE), columns)
        copy = pltpu.make_async_copy(
            whole_ref.at[:, cols], ref.at[:, pl.ds(begin, columns)], sem_ref.at[first + index]
        )
        copy.start()
        copies.append(copy)
    return copies


def attend_pair(q, k, v, bias_ref, p_ref, o_ref, ot_ref, size):
    width = q.shape[1]
    lane = iota2((1, width), 1)
    vt = v.T
    mixed = []
    for g in range(width // size):
        mine = (lane >= g * size) & (lane < (g + 1) * size)
        scores = dg(jnp.where(mine, k, jnp.zeros_like(k)), q, NT) + bias_ref[g].astype(F32)
        top = jnp.max(scores, axis=0, keepdims=True)
        shifted = jnp.exp(scores - top)
        norm = jnp.sum(shifted, axis=0, keepdims=True)
        probs = (shifted * (1.0 / norm)).astype(BF)
        p_ref[g] = probs
        mixed.append(dg(vt[g * size : (g + 1) * size], probs, NN))
    turned = jnp.concatenate(mixed, axis=0)
    ot_ref[...] = turned.astype(BF)
    o_ref[...] = turned.T.astype(BF)


def attend_first_kernel(*refs, size, places, factor):
    count = len(places)
    coords_ref, x_ref, shift_ref, bias_ref = refs[:4]
    pieces = refs[4 : 4 + count]
    qkv_ref, p_ref, o_ref, ot_ref, xt_ref, w_ref, sem_ref = refs[4 + count :]
    pair = pl.program_id(0)
    model = x_ref.shape[1]
    width = o_ref.shape[1]

    @pl.when(pair == 0)
    def _():
        copies = start_fetch(pieces, places, coords_ref, w_ref, sem_ref)
        xt_ref[...] = x_ref[...].T
        finish(copies)
        for part in range(3):
            cols = slice(part * model, (part + 1) * model)
            value = dg(x_ref[...], w_ref[:, cols], NN) + shift_ref[:, cols]
            if part == 0:
                value = value * factor
            qkv_ref[:, cols] = value.astype(BF)

    def block(part):
        return qkv_ref[:, pl.ds(pl.multiple_of(part * model + pair * width, width), width)]

    attend_pair(block(0), block(1), block(2), bias_ref, p_ref, o_ref, ot_ref, size)


def attend_rest_kernel(q_ref, k_ref, v_ref, bias_ref, _p, _o, _ot, p_ref, o_ref, ot_ref, *, size):
    attend_pair(q_ref[...], k_ref[...], v_ref[...], bias_ref, p_ref, o_ref, ot_ref, size)


def attend_first(coords, tokens, shift_row, weight, bias, size, steps):
    length, model = tokens.shape
    group = WIDE // size
    count = weight.count
    return pl.pallas_call(
        functools.partial(
            attend_first_kernel, size=size, places=weight.places, factor=size**-0.5
        ),
        grid=(steps,),
        in_specs=[
            SMEM,
            pl.BlockSpec((length, model), lambda i: (0, 0)),
            pl.BlockSpec((1, 3 * model), lambda i: (0, 0)),
            pl.BlockSpec((group, length, length), lambda i: (i, 0, 0)),
        ]
        + [ANY] * count,
        out_specs=[
            pl.BlockSpec((length, 3 * model), lambda i: (0, 0)),
            pl.BlockSpec((group, length, length), lambda i: (i, 0, 0)),
            pl.BlockSpec((length, WIDE), lambda i: (0, i)),
            pl.BlockSpec((WIDE, length), lambda i: (i, 0)),
            pl.BlockSpec((model, length), lambda i: (0, 0)),
        ],
        out_shape=[
            shaped((length, 3 * model), BF),
            shaped((model // size, length, length), BF),
            shaped((length, model), BF),
            shaped((model, length), BF),
            shaped((model, length), BF),
        ],
        scratch_shapes=[pltpu.VMEM(weight.shape, BF), pltpu.SemaphoreType.DMA((count,))],
        compiler_params=params(56),
        cost_estimate=cost(11.5),
        name="attend_first",
    )(coords, tokens, shift_row, bias, *weight.pieces)


def attend_rest(qkv, bias, probs, mixed, turned, size, first):
    length, model = mixed.shape
    group = WIDE // size
    blocks = model // WIDE
    return pl.pallas_call(
        functools.partial(attend_rest_kernel, size=size),
        grid=(blocks - first,),
        in_specs=[
            pl.BlockSpec((length, WIDE), lambda i: (0, first + i)),
            pl.BlockSpec((length, WIDE), lambda i: (0, blocks + first + i)),
            pl.BlockSpec((length, WIDE), lambda i: (0, 2 * blocks + first + i)),
            pl.BlockSpec((group, length, length), lambda i: (first + i, 0, 0)),
            ANY,
            ANY,
            ANY,
        ],
        out_specs=[
            pl.BlockSpec((group, length, length), lambda i: (first + i, 0, 0)),
            pl.BlockSpec((length, WIDE), lambda i: (0, first + i)),
            pl.BlockSpec((WIDE, length), lambda i: (first + i, 0)),
        ],
        out_shape=[
            shaped(probs.shape, BF),
            shaped(mixed.shape, BF),
            shaped(turned.shape, BF),
        ],
        input_output_aliases={4: 0, 5: 1, 6: 2},
        compiler_params=params(56),
        cost_estimate=cost(7),
        name="attend_rest",
    )(qkv, qkv, qkv, bias, probs, mixed, turned)


def attend_back_kernel(
    core_ref,
    q_ref,
    k_ref,
    v_ref,
    p_ref,
    o_ref,
    g_ref,
    xt_ref,
    prior_ref,
    out_ref,
    ds_ref,
    sent_ref,
    kept_ref,
    product_ref,
    sem_ref,
    *,
    size,
    factor,
):
    pair = pl.program_id(0)
    width = q_ref.shape[1]
    model = out_ref.shape[1] // 3
    count = width // size
    lane = iota2((1, width), 1)
    q = q_ref[...]
    v = v_ref[...]
    ob = g_ref[...]
    kt = k_ref[...].T
    product = o_ref[...].astype(F32) * ob.astype(F32)
    qs, ks, vs = [], [], []
    for g in range(count):
        mine = (lane >= g * size) & (lane < (g + 1) * size)
        spare = ((g + 1) % count) * size
        inner = jnp.sum(jnp.where(mine, product, 0.0), axis=1, keepdims=True)
        high = inner.astype(BF).astype(F32)
        extra = jnp.where(lane == spare, high, jnp.where(lane == spare + 1, inner - high, 0.0))
        minus = jnp.where((lane == spare) | (lane == spare + 1), -1.0, 0.0)
        left = jnp.where(mine, v, minus.astype(BF))
        right = jnp.where(mine, ob, extra.astype(BF))
        probs = p_ref[g]
        ds = (probs.astype(F32) * dg(left, right, NT)).astype(BF)
        ds_ref[g] = ds
        vs.append(dg(probs, ob, NN))
        ks.append(dg(ds, q, NN))
        qs.append(dg(kt[g * size : (g + 1) * size], ds, NN))

    def pick(items):
        chosen = items[0]
        for g in range(1, count):
            chosen = jnp.where(lane >= g * size, items[g], chosen)
        return chosen

    def place(start):
        return pl.ds(pl.multiple_of(start + pair * width, width), width)

    q_grad = jnp.concatenate(qs, axis=0).T.astype(BF).astype(F32) * factor
    out_ref[:, place(0)] = q_grad.astype(BF)
    out_ref[:, place(model)] = pick(ks).astype(BF)
    out_ref[:, place(2 * model)] = pick(vs).astype(BF)

    @pl.when(pair == pl.num_programs(0) - 1)
    def _():
        begin = prior_ref.shape[1] // 2
        copies = save_halves(core_ref, prior_ref, sent_ref, kept_ref, sem_ref, 0)
        for part in range(3):
            cols = slice(part * model, (part + 1) * model)
            product_ref[:, cols] = dg(xt_ref[...], out_ref[:, cols], NN).astype(BF)
        copies += save_halves(core_ref, product_ref, sent_ref, kept_ref, sem_ref, 2, begin)
        finish(copies)


def attend_back(core, qkv, probs, mixed, grad_mixed, turned, prior, size):
    length = qkv.shape[0]
    model = qkv.shape[1] // 3
    blocks = model // WIDE
    group = WIDE // size
    halves = shaped((model, (prior.shape[1] + 3 * model) // 2), BF)
    return pl.pallas_call(
        functools.partial(attend_back_kernel, size=size, factor=size**-0.5),
        grid=(blocks,),
        in_specs=[
            SMEM,
            pl.BlockSpec((length, WIDE), lambda i: (0, i)),
            pl.BlockSpec((length, WIDE), lambda i: (0, blocks + i)),
            pl.BlockSpec((length, WIDE), lambda i: (0, 2 * blocks + i)),
            pl.BlockSpec((group, length, length), lambda i: (i, 0, 0)),
            pl.BlockSpec((length, WIDE), lambda i: (0, i)),
            pl.BlockSpec((length, WIDE), lambda i: (0, i)),
            pl.BlockSpec((model, length), lambda i: (0, 0)),
            pl.BlockSpec(prior.shape, lambda i: (0, 0)),
        ],
        out_specs=[
            pl.BlockSpec((length, 3 * model), lambda i: (0, 0)),
            pl.BlockSpec((group, length, length), lambda i: (i, 0, 0)),
            ANY,
            ANY,
        ],
        out_shape=[
            shaped((length, 3 * model), BF),
            shaped((model // size, length, length), BF),
            halves,
            halves,
        ],
        scratch_shapes=[
            pltpu.VMEM((model, 3 * model), BF),
            pltpu.SemaphoreType.DMA((4,)),
        ],
        compiler_params=params(30),
        cost_estimate=cost(17),
        name="attend_back",
    )(core, qkv, qkv, qkv, probs, mixed, grad_mixed, turned, prior)


def norm_forward(inputs, gain_vec, shift_vec):
    center = inputs - jnp.mean(inputs, axis=-1, keepdims=True)
    inverse = lax.rsqrt(jnp.mean(center * center, axis=-1, keepdims=True) + EPSILON)
    scaled = center * inverse
    return (scaled * gain_vec + shift_vec, scaled, inverse)


def norm_backward(grad_in, scaled, inverse, gain_vec):
    inner_term = grad_in * gain_vec
    centered = inner_term - jnp.mean(inner_term, axis=-1, keepdims=True)
    return inverse * (centered - scaled * jnp.mean(inner_term * scaled, axis=-1, keepdims=True))


def gelu_pair(u):
    square = jnp.exp(u * u * -0.5)
    t = 1.0 / (1.0 + jnp.abs(u) * (0.3275911 * 0.7071067811865476))
    poly = t * (
        0.254829592
        + t * (-0.284496736 + t * (1.421413741 + t * (-1.453152027 + t * 1.061405429)))
    )
    tail = 0.5 * poly * square
    below = jnp.where(u >= 0.0, 1.0 - tail, tail)
    return u * below, below + u * (square * 0.3989422804014327)


def column_sum(values):
    return jnp.sum(values, axis=0, keepdims=True)


OUT_B, GAIN1, SHIFT1, DOWN_B, GAIN2, SHIFT2 = range(2, 8)


def up_kernel(*refs, out_places, up_places, chunk):
    outs, ups = len(out_places), len(up_places)
    coords_ref, mixed_ref, x_ref, vec_ref, upb_ref = refs[:5]
    out_pieces = refs[5 : 5 + outs]
    up_pieces = refs[5 + outs : 5 + outs + ups]
    (
        n1t_out,
        z1_out,
        r1_ref,
        hidden_out,
        turned_out,
        slope_out,
        w_out,
        w_up,
        n1t,
        z1_low,
        hidden,
        turned,
        slope,
        sem_ref,
        save_sem,
    ) = refs[5 + outs + ups :]
    first = start_fetch(out_pieces, out_places, coords_ref, w_out, sem_ref)
    second = start_fetch(up_pieces, up_places, coords_ref, w_up, sem_ref, outs)

    def vec(row):
        return vec_ref[row : row + 1, :]

    finish(first)
    summed = x_ref[...].astype(F32) + (dg(mixed_ref[...], w_out[...], NN) + vec(OUT_B))
    n1, z1, r1 = norm_forward(summed, vec(GAIN1), vec(SHIFT1))
    low = n1.astype(BF)
    n1t[...] = low.T
    z1_low[...] = z1.astype(BF)
    r1_ref[...] = r1
    saves = [
        pltpu.make_async_copy(n1t, n1t_out, save_sem.at[0]),
        pltpu.make_async_copy(z1_low, z1_out, save_sem.at[1]),
    ]
    for save in saves:
        save.start()
    finish(second)
    for index, begin in enumerate(range(0, hidden.shape[1], chunk)):
        cols = slice(begin, begin + chunk)
        h, s = gelu_pair(dg(low, w_up[:, cols], NN) + upb_ref[:, cols])
        h = h.astype(BF)
        hidden[:, cols] = h
        turned[cols, :] = h.T
        slope[:, cols] = s.astype(BF)
        part = pl.ds(begin, chunk)
        for kind, (left, right) in enumerate(
            (
                (hidden.at[:, part], hidden_out.at[:, part]),
                (turned.at[part, :], turned_out.at[part, :]),
                (slope.at[:, part], slope_out.at[:, part]),
            )
        ):
            save = pltpu.make_async_copy(left, right, save_sem.at[2 + index * 3 + kind])
            save.start()
            saves.append(save)
    finish(saves)


def go_up(coords, mixed, tokens, vecs, up_bias, w_out, w_up, chunk=512):
    length, model = tokens.shape
    wide = up_bias.shape[1]
    return pl.pallas_call(
        functools.partial(
            up_kernel, out_places=w_out.places, up_places=w_up.places, chunk=chunk
        ),
        in_specs=[SMEM] + [VMEM] * 4 + [ANY] * (w_out.count + w_up.count),
        out_specs=[ANY] * 2 + [VMEM] + [ANY] * 3,
        out_shape=[
            shaped((model, length), BF),
            shaped((length, model), BF),
            shaped((length, 1), F32),
            shaped((length, wide), BF),
            shaped((wide, length), BF),
            shaped((length, wide), BF),
        ],
        scratch_shapes=[
            pltpu.VMEM(w_out.shape, BF),
            pltpu.VMEM(w_up.shape, BF),
            pltpu.VMEM((model, length), BF),
            pltpu.VMEM((length, model), BF),
            pltpu.VMEM((length, wide), BF),
            pltpu.VMEM((wide, length), BF),
            pltpu.VMEM((length, wide), BF),
            pltpu.SemaphoreType.DMA((w_out.count + w_up.count,)),
            pltpu.SemaphoreType.DMA((2 + 3 * (wide // chunk),)),
        ],
        compiler_params=params(56),
        cost_estimate=cost(14.5),
        name="go_up",
    )(coords, mixed, tokens, vecs, up_bias, *w_out.pieces, *w_up.pieces)


def down_kernel(*refs, places, chunk):
    count = len(places)
    coords_ref, len_ref, z1_ref, vec_ref, cot_in, hidden_in, turned_in = refs[:7]
    pieces = refs[7 : 7 + count]
    (
        y_out,
        fb_out,
        sums_ref,
        sent_ref,
        kept_ref,
        w_ref,
        cot,
        y_low,
        fb_low,
        hidden,
        turned,
        product_ref,
        sem_ref,
        own_sem,
    ) = refs[7 + count :]
    load = pltpu.make_async_copy(hidden_in, hidden, own_sem.at[0])
    load.start()
    copies = start_fetch(pieces, places, coords_ref, w_ref, sem_ref)
    load_cot = pltpu.make_async_copy(cot_in, cot, own_sem.at[2])
    load_cot.start()
    load_turned = pltpu.make_async_copy(turned_in, turned, own_sem.at[1])
    load_turned.start()

    def vec(row):
        return vec_ref[row : row + 1, :]

    n1 = z1_ref[...].astype(F32) * vec(GAIN1) + vec(SHIFT1)
    load.wait()
    finish(copies)
    n2, z2, r2 = norm_forward(
        n1 + (dg(hidden[...], w_ref[...], NN) + vec(DOWN_B)), vec(GAIN2), vec(SHIFT2)
    )
    rows = z1_ref.shape[0]
    valid = (iota2((rows, 1), 0) < len_ref[0]).astype(F32)
    y_low[...] = (n2 * valid).astype(BF)
    load_cot.wait()
    g2 = cot[...].astype(F32) * valid
    back = norm_backward(g2, z2, r2, vec(GAIN2))
    fb = back.astype(BF)
    fb_low[...] = fb
    saves = [
        pltpu.make_async_copy(y_low, y_out, own_sem.at[3]),
        pltpu.make_async_copy(fb_low, fb_out, own_sem.at[4]),
    ]
    for save in saves:
        save.start()
    sums_ref[...] = jnp.concatenate(
        [column_sum(fb.astype(F32)), column_sum(g2 * z2), column_sum(g2)]
        + [jnp.zeros((5, z1_ref.shape[1]), F32)],
        axis=0,
    )
    load_turned.wait()
    for index, begin in enumerate(range(0, turned.shape[0], chunk)):
        part = pl.ds(begin, chunk)
        product_ref[part, :] = dg(turned[part, :], fb, NN).astype(BF)
        saves += save_halves(
            coords_ref, product_ref.at[part], sent_ref.at[part], kept_ref.at[part], own_sem, 5 + 2 * index
        )
    finish(saves)


def go_down(coords, lengths, z1, cotangent, vecs, hidden, turned, weight, chunk=512):
    length, model = z1.shape
    wide = hidden.shape[1]
    return pl.pallas_call(
        functools.partial(down_kernel, places=weight.places, chunk=chunk),
        in_specs=[SMEM] * 2 + [VMEM] * 2 + [ANY] * (3 + weight.count),
        out_specs=[ANY] * 2 + [VMEM] + [ANY] * 2,
        out_shape=[
            shaped((length, model), BF),
            shaped((length, model), BF),
            shaped((8, model), F32),
            shaped((wide, model // 2), BF),
            shaped((wide, model // 2), BF),
        ],
        scratch_shapes=[
            pltpu.VMEM(weight.shape, BF),
            pltpu.VMEM((length, model), BF),
            pltpu.VMEM((length, model), BF),
            pltpu.VMEM((length, model), BF),
            pltpu.VMEM((length, wide), BF),
            pltpu.VMEM((wide, length), BF),
            pltpu.VMEM((wide, model), BF),
            pltpu.SemaphoreType.DMA((weight.count,)),
            pltpu.SemaphoreType.DMA((5 + 2 * (wide // chunk),)),
        ],
        compiler_params=params(56),
        cost_estimate=cost(16),
        name="go_down",
    )(coords, lengths, z1, vecs, cotangent, hidden, turned, *weight.pieces)


def back_down_kernel(*refs, places, chunk):
    count = len(places)
    coords_ref, fb_ref, n1t_ref, slope_in = refs[:4]
    pieces = refs[4 : 4 + count]
    ub_out, upsum_ref, sent_ref, kept_ref, w_ref, slope, product_ref, sem_ref, own_sem = refs[
        4 + count :
    ]
    load = pltpu.make_async_copy(slope_in, slope, own_sem.at[0])
    copies = start_fetch(pieces, places, coords_ref, w_ref, sem_ref)
    load.start()
    fb = fb_ref[...]
    n1t = n1t_ref[...]
    upsum_ref[...] = jnp.zeros_like(upsum_ref)
    finish(copies)
    load.wait()
    saves = []
    for index, begin in enumerate(range(0, slope.shape[1], chunk)):
        cols = slice(begin, begin + chunk)
        ub = (slope[:, cols].astype(F32) * dg(fb, w_ref[cols, :], NT)).astype(BF)
        slope[:, cols] = ub
        upsum_ref[index : index + 1, :] = column_sum(ub.astype(F32))
        save = pltpu.make_async_copy(
            slope.at[:, pl.ds(begin, chunk)], ub_out.at[:, pl.ds(begin, chunk)], own_sem.at[3 + index]
        )
        save.start()
        saves.append(save)
        product_ref[:, cols] = dg(n1t, ub, NN).astype(BF)
    saves += save_halves(coords_ref, product_ref, sent_ref, kept_ref, own_sem, 1)
    finish(saves)


def back_down(coords, fb, n1t, slope, weight):
    length, model = fb.shape
    wide = slope.shape[1]
    chunk = model
    return pl.pallas_call(
        functools.partial(back_down_kernel, places=weight.places, chunk=chunk),
        in_specs=[SMEM] + [VMEM] * 2 + [ANY] * (1 + weight.count),
        out_specs=[ANY, VMEM, ANY, ANY],
        out_shape=[
            shaped((length, wide), BF),
            shaped((8, model), F32),
            shaped((model, wide // 2), BF),
            shaped((model, wide // 2), BF),
        ],
        scratch_shapes=[
            pltpu.VMEM(weight.shape, BF),
            pltpu.VMEM((length, wide), BF),
            pltpu.VMEM((model, wide), BF),
            pltpu.SemaphoreType.DMA((weight.count,)),
            pltpu.SemaphoreType.DMA((3 + wide // chunk,)),
        ],
        compiler_params=params(56),
        cost_estimate=cost(13.5),
        name="back_down",
    )(coords, fb, n1t, slope, *weight.pieces)


def back_up_kernel(*refs, up_places, out_places):
    ups, outs = len(up_places), len(out_places)
    coords_ref, fb_ref, r1_ref, vec_ref, z1_in, ot_in, ub_in = refs[:7]
    up_pieces = refs[7 : 7 + ups]
    out_pieces = refs[7 + ups : 7 + ups + outs]
    (
        ab_out,
        ob_out,
        sums_ref,
        product_ref,
        w_up,
        w_out,
        ub,
        z1_low,
        ot,
        ab_low,
        ob_low,
        sem_ref,
        own_sem,
    ) = refs[7 + ups + outs :]
    load = pltpu.make_async_copy(ub_in, ub, own_sem.at[0])
    load.start()
    second = start_fetch(up_pieces, up_places, coords_ref, w_up, sem_ref)
    load_z1 = pltpu.make_async_copy(z1_in, z1_low, own_sem.at[1])
    load_z1.start()
    first = start_fetch(out_pieces, out_places, coords_ref, w_out, sem_ref, ups)
    load_ot = pltpu.make_async_copy(ot_in, ot, own_sem.at[2])
    load_ot.start()
    load.wait()
    finish(second)
    n1b = fb_ref[...].astype(F32) + dg(ub[...], w_up[...], NT)
    load_z1.wait()
    z1 = z1_low[...].astype(F32)
    back = norm_backward(n1b, z1, r1_ref[...], vec_ref[GAIN1 : GAIN1 + 1, :])
    ab = back.astype(BF)
    ab_low[...] = ab
    save_ab = pltpu.make_async_copy(ab_low, ab_out, own_sem.at[3])
    save_ab.start()
    sums_ref[...] = jnp.concatenate(
        [column_sum(ab.astype(F32)), column_sum(n1b * z1), column_sum(n1b)]
        + [jnp.zeros((5, z1.shape[1]), F32)],
        axis=0,
    )
    finish(first)
    ob_low[...] = dg(ab, w_out[...], NT).astype(BF)
    save_ob = pltpu.make_async_copy(ob_low, ob_out, own_sem.at[4])
    save_ob.start()
    load_ot.wait()
    product_ref[...] = dg(ot[...], ab, NN).astype(BF)
    save_ab.wait()
    save_ob.wait()


def back_up(coords, ub, fb, z1, r1, vecs, turned, w_up, w_out):
    length, model = fb.shape
    wide = ub.shape[1]
    return pl.pallas_call(
        functools.partial(back_up_kernel, up_places=w_up.places, out_places=w_out.places),
        in_specs=[SMEM] + [VMEM] * 3 + [ANY] * (3 + w_up.count + w_out.count),
        out_specs=[ANY] * 2 + [VMEM] * 2,
        out_shape=[
            shaped((length, model), BF),
            shaped((length, model), BF),
            shaped((8, model), F32),
            shaped((model, model), BF),
        ],
        scratch_shapes=[
            pltpu.VMEM(w_up.shape, BF),
            pltpu.VMEM(w_out.shape, BF),
            pltpu.VMEM((length, wide), BF),
            pltpu.VMEM((length, model), BF),
            pltpu.VMEM((model, length), BF),
            pltpu.VMEM((length, model), BF),
            pltpu.VMEM((length, model), BF),
            pltpu.SemaphoreType.DMA((w_up.count + w_out.count,)),
            pltpu.SemaphoreType.DMA((5,)),
        ],
        compiler_params=params(56),
        cost_estimate=cost(13.5),
        name="back_up",
    )(coords, fb, r1, vecs, z1, turned, ub, *w_up.pieces, *w_out.pieces)


def inputs_kernel(*refs, places, counts):
    count = len(places)
    coords_ref, pb_ref, back_ref = refs[:3]
    vectors = refs[3 : 3 + len(counts)]
    tables = refs[3 + len(counts) : 5 + len(counts)]
    pieces = refs[5 + len(counts) : 5 + len(counts) + count]
    out_ref, sums_ref, w_ref, sem_ref = refs[5 + len(counts) + count :]
    copies = start_fetch(pieces, places, coords_ref, w_ref, sem_ref)
    pb = pb_ref[...]
    flat = column_sum(pb.astype(F32))
    model = out_ref.shape[1]
    sums_ref[...] = jnp.zeros_like(sums_ref)
    begin = 0
    for rows, ref in zip(counts, vectors):
        sums_ref[begin : begin + rows, :] = ref[:rows, :]
        begin += rows
    for part in range(3):
        sums_ref[begin : begin + 1, :] = flat[:, part * model : (part + 1) * model]
        begin += 1
    table = tables[0][...] + tables[1][...]
    for head in range(table.shape[0]):
        row = begin + head // (model // WIDE)
        lane = head % (model // WIDE) * WIDE
        if row < sums_ref.shape[0]:
            sums_ref[row : row + 1, lane : lane + table.shape[1]] = table[head : head + 1, :]
    finish(copies)
    out_ref[...] = (back_ref[...].astype(F32) + dg(pb, w_ref[...], NT)).astype(BF)


def inputs_grad(coords, grad_packed, back, vectors, counts, tables, heads, weight):
    length, model = back.shape
    count = weight.count
    rows = sum(counts) + 3 + -(-heads // (model // WIDE))
    rows = -(-rows // 8) * 8
    return pl.pallas_call(
        functools.partial(inputs_kernel, places=weight.places, counts=counts),
        in_specs=[SMEM] + [VMEM] * (4 + len(counts)) + [ANY] * count,
        out_specs=[VMEM] * 2,
        out_shape=[shaped((length, model), BF), shaped((rows, model), F32)],
        scratch_shapes=[
            pltpu.VMEM(weight.shape, BF),
            pltpu.SemaphoreType.DMA((count,)),
        ],
        compiler_params=params(56),
        cost_estimate=cost(7),
        name="inputs_grad",
    )(coords, grad_packed, back, *vectors, *tables, *weight.pieces)


def finish_kernel(at_ref, mine_ref, theirs_ref, *out_refs):
    first = at_ref[0] == 0
    begin = 0
    for out_ref in out_refs:
        columns = out_ref.shape[1] // 2
        mine = mine_ref[:, begin : begin + columns]
        theirs = theirs_ref[:, begin : begin + columns]
        out_ref[:, :columns] = jnp.where(first, mine, theirs).astype(F32)
        out_ref[:, columns:] = jnp.where(first, theirs, mine).astype(F32)
        begin += columns


def finish_pair(core, mine, theirs, widths):
    rows, columns = mine.shape
    step = rows // 4 if (rows // 4) % 16 == 0 else rows
    spec = pl.BlockSpec((step, columns), lambda i: (i, 0))
    return pl.pallas_call(
        finish_kernel,
        grid=(rows // step,),
        in_specs=[SMEM, spec, spec],
        out_specs=[pl.BlockSpec((step, width), lambda i: (i, 0)) for width in widths],
        out_shape=[shaped((rows, width), F32) for width in widths],
        compiler_params=params(16),
        cost_estimate=cost(4.4),
        name="finish_pair",
    )(core, mine, theirs)


class Axis:
    def __init__(self, name, total, stride, size):
        self.name = name
        self.total = total
        self.stride = stride
        self.size = size
        self.at = (lax.axis_index(name) // stride) % size

    def send(self, value, step):
        pairs = []
        for index in range(self.total):
            place = (index // self.stride) % self.size
            pairs.append((index, index + ((place + step) % self.size - place) * self.stride))
        return lax.ppermute(value, self.name, pairs)

    def peer(self, step):
        return (self.at + step) % self.size


def tie(value, *others):
    if not others:
        return value
    return lax.optimization_barrier((value,) + others)[0]


def take(stack, index, dim=0):
    return lax.dynamic_index_in_dim(stack, index, axis=dim, keepdims=False)


def arrange(axis, block, got, dim=0):
    if axis.size == 1:
        return jnp.expand_dims(block, dim)
    shape = [1] * (block.ndim + 1)
    shape[dim] = axis.size
    place = jnp.arange(axis.size, dtype=jnp.int32).reshape(shape)
    stack = jnp.expand_dims(block, dim)
    for step, value in enumerate(got):
        stack = jnp.where(place == axis.peer(-1 - step), jnp.expand_dims(value, dim), stack)
    return stack


def send_all(axis, block):
    return [axis.send(block, step) for step in range(1, axis.size)]


class Links:
    def __init__(self, dp, fsdp):
        core = 2
        rest = dp // core
        near = 2 if rest % 2 == 0 else 1
        self.core = Axis("dp", dp, 1, core)
        self.near = Axis("dp", dp, core, near)
        self.far = Axis("dp", dp, core * near, rest // near)
        self.pair = Axis("dp", dp, core * near, 2 if (rest // near) % 2 == 0 else 1)
        self.shard = Axis("fsdp", fsdp, 1, fsdp)


class Portion:
    def __init__(self, links, blocks, begin, count, mate):
        self.links = links
        self.mate = mate
        self.begin = begin
        self.rows = blocks[0].shape[0]
        parts = links.core.size * (mate.size if mate else 1)
        self.unit = count // parts
        self.blocks = blocks
        self.inbox = []
        self.held = []

    def spot(self, s, t):
        core = self.links.core.peer(-s)
        return core * self.mate.size + self.mate.peer(-t) if self.mate else core

    def start(self, *after):
        begin = self.begin + self.spot(0, 0) * self.unit
        mine = [lax.dynamic_slice_in_dim(item, begin, self.unit, 0) for item in self.blocks]
        mine = tie(jnp.concatenate(mine, axis=1) if len(mine) > 1 else mine[0], *after)
        self.inbox = send_all(self.links.shard, mine)
        return [mine]

    def hop(self):
        self.got = self.inbox
        if self.mate:
            self.inbox = [self.mate.send(item, 1) for item in self.got]
        return list(self.got)

    def cross(self, *after):
        self.crossed = [self.links.core.send(tie(item, *after), 1) for item in self.got]

    def last(self):
        self.hops = self.inbox if self.mate else []
        self.inbox = [self.links.core.send(item, 1) for item in self.hops]
        return list(self.hops) + list(self.crossed)

    def pieces(self):
        shard = self.links.shard
        which = None if self.mate is None else 1 if self.mate is self.links.near else 2
        found = []
        for index in range(len(self.got)):
            group = [(self.got[index], 0, 0), (self.crossed[index], 1, 0)]
            if self.mate:
                group += [(self.hops[index], 0, 1), (self.inbox[index], 1, 1)]
            for value, s, t in group:
                found.append(
                    (value, (self.rows, shard.size, self.begin, -1 - index, self.unit, -s, -t, which))
                )
        return found


class Fetch:
    def __init__(self, links, *blocks):
        self.links = links
        self.blocks = blocks
        rows = blocks[0].shape[0]
        mates = (links.near, links.pair)
        if rows % 128 == 0 and all(mate.size == 2 for mate in mates):
            half = rows // 2
            self.parts = [
                Portion(links, blocks, index * half, half, mate) for index, mate in enumerate(mates)
            ]
        else:
            self.parts = [Portion(links, blocks, 0, rows, None)]

    def do(self, name, *after):
        found = []
        for part in self.parts:
            found += getattr(part, name)(*after) or []
        return found

    def weights(self):
        rows = self.blocks[0].shape[0]
        count = self.links.shard.size
        found = []
        for part in self.parts:
            found += part.pieces()
        done = []
        begin = 0
        for block in self.blocks:
            columns = None if len(self.blocks) == 1 else begin
            done.append(
                Weight(
                    [block] + [item for item, _ in found],
                    [Place(rows, count)] + [Place(*place, columns=columns) for _, place in found],
                    (rows * count, block.shape[1]),
                )
            )
            begin += block.shape[1]
        return done


def meet(owners, *values):
    flat = [item for owner in owners for item in owner.inbox + owner.held]
    flat = lax.optimization_barrier(tuple(flat) + tuple(values))
    begin = 0
    for owner in owners:
        count = len(owner.inbox)
        owner.inbox = list(flat[begin : begin + count])
        begin += count
        count = len(owner.held)
        owner.held = list(flat[begin : begin + count])
        begin += count
    return list(flat[begin:])


def add_up(terms):
    total = terms[0].astype(F32)
    for term in terms[1:]:
        total = total + term.astype(F32)
    return total


class Chain:
    def __init__(self, links, sent, kept, line):
        self.links = links
        self.sent = sent
        self.line = line and links.far.size == 4
        rows, columns = kept.shape
        sizes = (links.shard.size, links.near.size, links.far.size, 2)
        whole = sizes[0] * sizes[1] * sizes[2] * sizes[3]
        self.shape = sizes + (rows // whole, columns)
        self.kept = kept

    def cross(self):
        self.inbox = [self.links.core.send(self.sent, 1)]
        self.held = [self.kept]
        return [self.sent]

    def hop(self, terms, axis):
        sent = []
        for step in range(1, axis.size):
            pieces = [term(axis.peer(step)) for term in terms]
            sent.append(lax.optimization_barrier(add_up(pieces).astype(BF)))
        return [axis.send(value, step + 1) for step, value in enumerate(sent)], sent

    def piece(self, term, way, x=None, y=None):
        shard, near, far, _, rows, columns = self.shape
        begin = [0 if x is None else x, 0 if y is None else y, 0, way, 0, 0]
        sizes = [shard if x is None else 1, near if y is None else 1, far, 1, rows, columns]
        keep = [size for at, size in zip((x, y), sizes[:2]) if at is None]
        part = lax.dynamic_slice(term.reshape(self.shape), begin, sizes)
        return part.reshape(*keep, far, rows, columns)

    def first(self):
        self.held = self.held + self.inbox
        held = self.held
        a, sent_a = self.hop(
            [lambda to, f=f: self.piece(f, 0, x=to) for f in held], self.links.shard
        )
        b, sent_b = self.hop([lambda to, f=f: self.piece(f, 1, y=to) for f in held], self.links.near)
        self.inbox = a + b
        self.cut = len(a)
        return sent_a + sent_b

    def second(self):
        x, y = self.links.shard.at, self.links.near.at
        got_a, got_b = self.inbox[: self.cut], self.inbox[self.cut :]
        held = self.held[:2]
        terms = [lambda to, f=f: self.piece(f, 0, x, to) for f in held]
        terms += [lambda to, v=v: take(v, to) for v in got_a]
        a, sent_a = self.hop(terms, self.links.near)
        terms = [lambda to, f=f: self.piece(f, 1, to, y) for f in held]
        terms += [lambda to, v=v: take(v, to) for v in got_b]
        b, sent_b = self.hop(terms, self.links.shard)
        self.held = held + got_a + got_b
        self.inbox = a + b
        self.last_cut = len(a)
        return sent_a + sent_b

    def third(self):
        x, y = self.links.shard.at, self.links.near.at
        got = self.held[2:]
        halves = []
        for way, (early, at) in enumerate(((got[: self.cut], y), (got[self.cut :], x))):
            late = self.inbox[: self.last_cut] if way == 0 else self.inbox[self.last_cut :]
            own = [self.piece(f, way, x, y) for f in self.held[:2]]
            halves.append(add_up(own + [take(v, at) for v in early] + late))
        self.held = []
        self.block = lax.optimization_barrier(jnp.stack(halves, axis=1).astype(BF))
        if self.line:
            self.inbox = [self.line_send(self.block, ((0, 1), (3, 2)))]
            return [self.block]
        far = self.links.far
        self.inbox, sent = self.hop([lambda to: take(self.block, to)], far)
        self.kept_block = self.block
        return sent

    def line_send(self, value, moves):
        far = self.links.far
        pairs = []
        for index in range(far.total):
            place = (index // far.stride) % far.size
            pairs += [(index, index + (to - place) * far.stride) for at, to in moves if at == place]
        return lax.ppermute(value, far.name, pairs)

    def middle(self):
        if not self.line:
            return []
        self.block = lax.optimization_barrier(add_up([self.block] + self.inbox).astype(BF))
        self.inbox = [self.line_send(self.block, ((1, 2), (2, 1)))]
        return [self.block]

    def fourth(self):
        if self.line:
            self.block = lax.optimization_barrier(add_up([self.block] + self.inbox).astype(BF))
            self.inbox = [self.line_send(self.block, ((1, 0), (2, 3)))]
            return [self.block]
        mine = take(self.kept_block, self.links.far.at)
        self.block = lax.optimization_barrier(add_up([mine] + self.inbox).astype(BF))
        self.inbox = send_all(self.links.far, self.block)
        return [self.block]

    def fifth(self):
        far = self.links.far
        if self.line:
            outer = (far.at == 0) | (far.at == 3)
            block = jnp.where(outer, self.inbox[0], self.block)
        else:
            block = arrange(far, self.block, self.inbox)
        self.block = lax.optimization_barrier(block)
        self.inbox = send_all(self.links.near, self.block)
        return [self.block]

    def sixth(self):
        block = arrange(self.links.near, self.block, self.inbox)
        self.block = lax.optimization_barrier(block.reshape(-1, block.shape[-1]))
        self.inbox = [self.links.core.send(self.block, 1)]
        return [self.block]

    def done(self, widths):
        return finish_pair(self.links.coords, self.block, self.inbox[0], widths)


class Sums:
    def __init__(self, links, value):
        self.links = links
        self.total = value
        self.inbox = []
        self.held = []

    def step(self, name):
        self.settle()
        self.inbox = send_all(getattr(self.links, name), self.total)
        return [self.total]

    def settle(self):
        self.total = functools.reduce(jnp.add, self.inbox, self.total)
        self.inbox = []


def per_device(
    dp,
    fsdp,
    tokens,
    lengths,
    buckets,
    qkv_weight,
    q_bias,
    v_bias,
    out_weight,
    out_bias,
    bias_table,
    norm1_gain,
    norm1_bias,
    up_weight,
    up_bias,
    down_weight,
    down_bias,
    norm2_gain,
    norm2_bias,
    cotangent,
):
    links = Links(dp, fsdp)
    model = tokens.shape[1]
    wide = up_weight.shape[1]
    heads = bias_table.shape[1]
    size = model // heads
    entries = bias_table.shape[0] * fsdp
    links.coords = coords = jnp.stack(
        [links.core.at, links.near.at, links.pair.at, links.shard.at]
    ).astype(jnp.int32)

    table_got = send_all(links.shard, bias_table)
    qkv = Fetch(links, qkv_weight)
    outup = Fetch(links, out_weight, up_weight)
    down = Fetch(links, down_weight)
    token = qkv.do("start", bias_table)
    narrow = (q_bias, v_bias, out_bias, norm1_gain, norm1_bias, down_bias, norm2_gain, norm2_bias)
    narrow = lax.optimization_barrier(narrow + (up_bias,) + tuple(token))
    row = jnp.arange(8, dtype=jnp.int32)[:, None]
    rows = jnp.broadcast_to(narrow[0][None], (8, narrow[0].size))
    for index in range(1, 8):
        rows = jnp.where(row == index, narrow[index][None], rows)
    part = out_bias.size
    rows = jnp.concatenate([rows, narrow[8].reshape(-1, part)], axis=0)
    rows = lax.optimization_barrier(rows)
    rows_got = send_all(links.shard, rows)
    table = arrange(links.shard, bias_table, table_got).reshape(entries, heads)
    bias = bias_scores(tie(buckets, rows, *token), lengths, table, 0, 1)
    tied = meet(qkv.parts, bias[0], bias[1], *rows_got)
    bias, rows_got = tied[:2], tied[2:]
    token = qkv.do("hop")
    qkv.do("cross")
    token = outup.do("start", *token)
    bias = bias_scores(tie(buckets, *token), lengths, table, 1, tokens.shape[0] // 128 - 1, bias)
    bias = meet(qkv.parts + outup.parts, *bias)
    token = qkv.do("last")
    token += outup.do("hop")
    token += down.do("start", *token)
    bias, ids = bias
    every = arrange(links.shard, rows, rows_got)
    vecs = jnp.swapaxes(every[:, :8], 0, 1).reshape(8, model).astype(F32)
    up_vec = every[:, 8:].reshape(1, -1).astype(F32)
    shift_row = jnp.concatenate([vecs[0:1], jnp.zeros((1, model), F32), vecs[1:2]], axis=1)
    shift_row, up_vec = lax.optimization_barrier((shift_row, up_vec) + tuple(token))[:2]
    (w_qkv,) = qkv.weights()
    half = model // WIDE * 5 // 6
    packed, probs, mixed, mixed_t, tokens_t = attend_first(
        coords, tokens, shift_row, w_qkv, bias, size, half
    )
    (mixed_t,) = meet(outup.parts + down.parts, mixed_t)
    outup.do("cross", mixed_t)
    token = outup.do("last")
    token += down.do("hop")
    probs, mixed, mixed_t = attend_rest(
        packed, bias, tie(probs, *token), mixed, mixed_t, size, half
    )
    (mixed,) = meet(outup.parts, mixed)
    w_out, w_up = outup.weights()
    n1t, z1, r1, hidden, hidden_t, slope = go_up(
        coords, mixed, tokens, vecs, up_vec, w_out, w_up
    )
    (z1,) = meet(down.parts, z1)
    down.do("cross", z1)
    token = down.do("last")
    (w_down,) = down.weights()
    output, fb, sums_two, sent, kept = go_down(
        coords, lengths, tie(z1, *token), cotangent, vecs, hidden, hidden_t, w_down
    )

    chain_down = Chain(links, sent, kept, True)
    token = chain_down.cross()
    ub, up_sum, sent, kept = back_down(coords, tie(fb, *token), n1t, slope, w_down)
    ub, sent = meet([chain_down], ub, sent)
    chain_up = Chain(links, sent, kept, True)
    token = chain_down.first() + chain_up.cross()
    back, ob, sums_one, out_product = back_up(
        coords, tie(ub, *token), fb, z1, r1, vecs, mixed_t, w_up, w_out
    )
    (ob,) = meet([chain_down, chain_up], ob)
    token = chain_down.second() + chain_up.first()
    grad_packed, grad_scores, sent, kept = attend_back(
        coords, packed, probs, mixed, tie(ob, *token), tokens_t, out_product, size
    )
    sent, grad_scores, grad_packed = meet([chain_down, chain_up], sent, grad_scores, grad_packed)
    chain_qkv = Chain(links, sent, kept, False)
    token = chain_down.third() + chain_up.second() + chain_qkv.cross()
    table_one = table_grad(ids, tie(grad_scores, *token), entries, 0, 2)
    (table_one,) = meet([chain_down, chain_up, chain_qkv], table_one)
    token = chain_down.middle() + chain_up.third() + chain_qkv.first()
    table_two = table_grad(ids, tie(grad_scores, table_one, *token), entries, 1, 2)
    (table_two,) = meet([chain_down, chain_up, chain_qkv], table_two)
    token = chain_down.fourth() + chain_up.middle() + chain_qkv.second()
    counts = (3, 3, wide // model)
    tokens_grad, packed_sums = inputs_grad(
        coords,
        tie(grad_packed, table_two, *token),
        back,
        (sums_one, sums_two, up_sum),
        counts,
        (table_one, table_two),
        heads,
        w_qkv,
    )
    (packed_sums,) = meet([chain_down, chain_up, chain_qkv], packed_sums)
    sums = Sums(links, packed_sums)
    chain_down.fifth()
    chain_up.fourth()
    chain_qkv.third()
    sums.step("shard")
    meet([sums])
    sums.step("core")
    meet([chain_down, chain_up, chain_qkv, sums])
    chain_down.sixth()
    chain_up.fifth()
    chain_qkv.fourth()
    sums.step("near")
    meet([chain_down, sums])
    (g_down,) = chain_down.done((model,))
    (g_down,) = meet([chain_up, chain_qkv], g_down)
    chain_qkv.fifth()
    chain_up.sixth()
    sums.step("far")
    meet([chain_up])
    (g_up,) = chain_up.done((wide,))
    (g_up,) = meet([chain_qkv, sums], g_up)
    sums.settle()
    chain_qkv.sixth()
    g_out, g_qkv = chain_qkv.done((model, 3 * model))

    total = sums.total
    place = links.shard.at

    def piece(row):
        return lax.dynamic_slice(total, (row, place * part), (1, part)).reshape(part)

    g_out_bias, g_gain_one, g_shift_one = [piece(row) for row in range(3)]
    g_down_bias, g_gain_two, g_shift_two = [piece(row) for row in range(3, 6)]
    row = 6 + wide // model
    up_flat = total[6:row].reshape(wide)
    g_up_bias = lax.dynamic_slice_in_dim(up_flat, place * up_bias.size, up_bias.size)
    g_query_bias = piece(row)
    g_value_bias = piece(row + 2)
    count = -(-heads // (model // WIDE))
    g_table = lax.dynamic_slice_in_dim(
        total[row + 3 : row + 3 + count].reshape(-1, WIDE)[:heads],
        place * bias_table.shape[0],
        bias_table.shape[0],
        1,
    ).T
    return (
        output,
        tokens_grad,
        g_qkv,
        g_query_bias,
        g_value_bias,
        g_out,
        g_out_bias,
        g_table,
        g_gain_one,
        g_shift_one,
        g_up,
        g_up_bias,
        g_down,
        g_down_bias,
        g_gain_two,
        g_shift_two,
    )


def solution(mesh):
    rows = P(("dp", "fsdp"), None)
    mat = P("fsdp", None)
    vec = P("fsdp")
    return jax.shard_map(
        functools.partial(per_device, mesh.shape["dp"], mesh.shape["fsdp"]),
        mesh=mesh,
        in_specs=(
            rows,
            P(("dp", "fsdp")),
            P(("dp", "fsdp"), None, None, None),
            mat,
            vec,
            vec,
            mat,
            vec,
            mat,
            vec,
            vec,
            mat,
            vec,
            mat,
            vec,
            vec,
            vec,
            rows,
        ),
        out_specs=(
            rows,
            rows,
            mat,
            vec,
            vec,
            mat,
            vec,
            mat,
            vec,
            vec,
            mat,
            vec,
            mat,
            vec,
            vec,
            vec,
        ),
        check_vma=False,
    )
```
